32 devices in a mesh: tm: 16 (over z, x, core), freq: 2 (over y).
Axes of the slice: x: 2, y: 2, z: 4, core: 2. Of those that a mesh axis runs over, the one named last changes fastest.
Arguments:
- features: bfloat16 [128, 256, 256], P('tm', 'freq'), may hold values from -6 to 6
- upstream: bfloat16 [128, 256, 256], P('tm', 'freq'), may hold values from -6 to 6
- weights: bfloat16 [8, 256, 256], replicated, may hold values from -8 to 8
- gains: float32 [2, 256], replicated, may hold values from 0.5 to 1.5
Outputs:
- grad_input: bfloat16 [128, 256, 256], P('tm', 'freq')
- weight_grads: float32 [8, 256, 256], replicated
- gain_grads: float32 [2, 256], replicated
The draws below stay inside these ranges and needn't reach their ends.
All inputs are finite; a program needn't handle non-finite values.
Results may differ from the reference program's by a relative error of at most 0.02.
Values may be sent and summed in bfloat16 or wider, within the bound.
No kernel may reach another device: no remote copies, remote signals or barrier semaphores. Data moves between devices by JAX's collectives and lax.ppermute only.
A program may use at most 128 MiB of HBM per device.

```python
import jax
import jax.numpy as jnp
from jax import lax

D = 256
BINS = 256
HEADS = 4
WINDOW = 128
FRAMES_DEV = 8
FRAMES = 128


def draw_weights(key, part):
    first_key = jax.random.fold_in(jax.random.fold_in(key, 7177), 0)
    matrices = jax.random.normal(first_key, (8, D, D), jnp.float32) * D ** (-0.5)
    return jnp.clip(matrices, -8.0, 8.0).astype(jnp.bfloat16)


def block_scale(stream_key, shape, pieces, low, high):
    factor_of, own = 1.0, jax.random.fold_in(stream_key, 6)
    for position, shards_of in pieces:
        draws = jnp.exp(jax.random.uniform(jax.random.fold_in(own, position), (shards_of,), jnp.float32, low / len(pieces), high / len(pieces)))
        factor_of = factor_of * jnp.repeat(draws, shape[position] // shards_of).reshape([-1 if axis == position else 1 for axis in range(len(shape))])
    return factor_of


def noise(own_key, shape, deviation, reach, pieces=(), kind=jnp.bfloat16):
    values = jax.random.normal(own_key, shape, jnp.float32) * deviation
    if len(pieces) > 0:
        values = block_scale(own_key, shape, pieces, -0.22, 0.18) * values
    return jnp.clip(values, min=-reach, max=reach).astype(kind)


def setup_inputs(seed: int = 0) -> dict:
    arg_keys = jax.random.split(jax.random.key(seed), 5)
    features = noise(arg_keys[0], (FRAMES, BINS, D), 1.0, 6.0, ((0, 16), (1, 2)))
    upstream = noise(arg_keys[1], (FRAMES, BINS, D), 1.0, 6.0, ((0, 16), (1, 2)))
    weights = draw_weights(jax.random.fold_in(arg_keys[4], 71), 0)
    gains = jnp.clip(1.0 + 0.1 * jax.random.normal(arg_keys[3], (2, D), jnp.float32), 0.5, 1.5)
    return dict(features=features, upstream=upstream, weights=weights, gains=gains)


epsilon = 1e-06
masked_score = -1e+30
exact_mode = lax.Precision.HIGHEST

def norm_forward(inputs, gain):
    widened = inputs.astype(jnp.float32)
    inverse = lax.rsqrt(lax.optimization_barrier(jnp.mean(widened * widened, axis=-1, keepdims=True)) + epsilon)
    unit_rows = widened * inverse
    return ((unit_rows * gain).astype(jnp.bfloat16), inverse, unit_rows)

def norm_backward(incoming, inverse, unit_rows, gain):
    scaled = incoming * gain
    result = inverse * (scaled - unit_rows * lax.optimization_barrier(jnp.mean(scaled * unit_rows, axis=-1, keepdims=True)))
    gain_grad = lax.optimization_barrier(jnp.sum((incoming * unit_rows).reshape(-1, unit_rows.shape[-1]), axis=0))
    return (result, gain_grad)

def project(inputs, matrix):
    flat_rows = inputs.reshape(-1, inputs.shape[-1])
    product = jnp.dot(flat_rows, matrix, preferred_element_type=jnp.float32)
    return product.reshape(inputs.shape[:-1] + (matrix.shape[1],))

def project_back(grads, matrices):
    running = jnp.zeros((grads[0].size // grads[0].shape[-1], matrices[0].shape[0]), jnp.float32)
    for grad_part, matrix in zip(grads, matrices):
        flat_rows = grad_part.reshape(-1, grad_part.shape[-1])
        running = running + jnp.dot(flat_rows, matrix.T, preferred_element_type=jnp.float32)
    return running.reshape(grads[0].shape[:-1] + (matrices[0].shape[0],))

def weight_grad(inputs, grads):
    return jnp.dot(inputs.reshape(-1, inputs.shape[-1]).T, grads.reshape(-1, grads.shape[-1]), preferred_element_type=jnp.float32)

def heads_of(array):
    return array.reshape(array.shape[:-1] + (HEADS, array.shape[-1] // HEADS))

def heads_merged(array):
    return array.reshape(array.shape[:-2] + (array.shape[-2] * array.shape[-1],))

def mixing(form, left, right):
    return jnp.einsum(form, left.astype(jnp.float32), right.astype(jnp.float32), precision=exact_mode)

def attend(queries, key_rows, value_rows, allowed, query_form, key_form):
    scaling = queries.shape[-1] ** (-0.5)
    scores = mixing(query_form + ',' + key_form + '->bhqk', queries, key_rows) * scaling
    scores = jnp.where(allowed, scores, masked_score)
    largest = lax.optimization_barrier(jnp.max(scores, axis=-1, keepdims=True))
    log_total = largest + jnp.log(lax.optimization_barrier(jnp.sum(jnp.exp(scores - largest), axis=-1, keepdims=True)))
    attention = jnp.exp(scores - log_total)
    mixed_rows = mixing('bhqk,' + key_form + '->' + query_form, attention.astype(jnp.bfloat16), value_rows).astype(jnp.bfloat16)
    return (mixed_rows, log_total[..., 0], attention)

def query_backward(attention, grad_out, key_rows, value_rows, query_form, key_form):
    scaling = key_rows.shape[-1] ** (-0.5)
    grad_attention = mixing(query_form + ',' + key_form + '->bhqk', grad_out, value_rows)
    row_dot = lax.optimization_barrier(jnp.sum(grad_attention * attention, axis=-1, keepdims=True))
    grad_scores = (attention * (grad_attention - row_dot) * scaling).astype(jnp.bfloat16)
    grad_queries = mixing('bhqk,' + key_form + '->' + query_form, grad_scores, key_rows).astype(jnp.bfloat16)
    return (grad_queries, row_dot[..., 0], grad_scores)

def key_terms(attention, grad_scores, queries, grad_out, query_form, key_form):
    grad_keys = mixing('bhqk,' + query_form + '->' + key_form, grad_scores, queries)
    grad_values = mixing('bhqk,' + query_form + '->' + key_form, attention.astype(jnp.bfloat16), grad_out)
    return (grad_keys, grad_values)

def key_backward(queries, grad_out, log_total, row_dot, key_rows, value_rows, allowed, query_form, key_form):
    scaling = queries.shape[-1] ** (-0.5)
    scores = mixing(query_form + ',' + key_form + '->bhqk', queries, key_rows) * scaling
    scores = jnp.where(allowed, scores, masked_score)
    attention = jnp.exp(scores - log_total[..., None])
    grad_attention = mixing(query_form + ',' + key_form + '->bhqk', grad_out, value_rows)
    grad_scores = (attention * (grad_attention - row_dot[..., None]) * scaling).astype(jnp.bfloat16)
    return key_terms(attention, grad_scores, queries, grad_out, query_form, key_form)

def window_masks(first_frame, frames_dev, window, total_frames):
    half_window = window // 2
    row_ids = jnp.arange(frames_dev, dtype=jnp.int32)[:, None]
    col_ids = jnp.arange(frames_dev + window, dtype=jnp.int32)[None, :]
    frame_ids = first_frame - half_window + col_ids
    inside = (frame_ids >= 0) & (frame_ids < total_frames)
    distance = col_ids - row_ids
    ahead_mask = (distance >= 0) & (distance < window) & inside
    behind_mask = (distance.T >= 1) & (distance.T <= window) & inside.T
    return (ahead_mask, behind_mask)

def reference(features, upstream, weights, gains):
    total_frames = features.shape[0]
    half_window = WINDOW // 2
    block_ids = jnp.arange(total_frames // FRAMES_DEV, dtype=jnp.int32)

    def cut(array, first_frame, count):
        return lax.dynamic_slice_in_dim(array, first_frame, count, 0)

    def padded(array):
        return jnp.pad(array, ((half_window, half_window),) + ((0, 0),) * (array.ndim - 1))
    norm_one, inverse_one, unit_one = norm_forward(features, gains[0])
    query_one = project(norm_one, weights[0]).astype(jnp.bfloat16)
    key_one = project(norm_one, weights[1]).astype(jnp.bfloat16)
    value_one = project(norm_one, weights[2]).astype(jnp.bfloat16)

    def freq_forward(block_index):
        first_frame = (block_index * FRAMES_DEV).astype(jnp.int32)
        mixed_rows, _, _ = attend(heads_of(cut(query_one, first_frame, FRAMES_DEV)), heads_of(cut(key_one, first_frame, FRAMES_DEV)), heads_of(cut(value_one, first_frame, FRAMES_DEV)), True, 'bqhd', 'bkhd')
        return heads_merged(mixed_rows)
    mixed_one = lax.map(freq_forward, block_ids).reshape(features.shape)
    hidden = (features.astype(jnp.float32) + project(mixed_one, weights[3])).astype(jnp.bfloat16)
    norm_two, inverse_two, unit_two = norm_forward(hidden, gains[1])
    query_two = project(norm_two, weights[4]).astype(jnp.bfloat16)
    key_two = project(norm_two, weights[5]).astype(jnp.bfloat16)
    value_two = project(norm_two, weights[6]).astype(jnp.bfloat16)
    pad_key = padded(key_two)
    pad_value = padded(value_two)

    def time_attend(block_index):
        first_frame = (block_index * FRAMES_DEV).astype(jnp.int32)
        ahead_mask, _ = window_masks(first_frame, FRAMES_DEV, WINDOW, total_frames)
        window_keys = heads_of(cut(pad_key, first_frame, FRAMES_DEV + WINDOW))
        window_values = heads_of(cut(pad_value, first_frame, FRAMES_DEV + WINDOW))
        result = attend(heads_of(cut(query_two, first_frame, FRAMES_DEV)), window_keys, window_values, ahead_mask[None, None], 'qbhd', 'kbhd')
        return (result, window_keys, window_values)

    def time_forward(block_index):
        result, _, _ = time_attend(block_index)
        return (heads_merged(result[0]), jnp.transpose(result[1], (2, 0, 1)))
    mixed_two, log_two = lax.map(time_forward, block_ids)
    mixed_two = mixed_two.reshape(features.shape)
    log_two = log_two.reshape(total_frames, features.shape[1], HEADS)
    grad_mixed_two = project_back([upstream], [weights[7]]).astype(jnp.bfloat16)

    def time_query(block_index):
        result, window_keys, window_values = time_attend(block_index)
        first_frame = (block_index * FRAMES_DEV).astype(jnp.int32)
        grad_queries, row_dot, _ = query_backward(result[2], heads_of(cut(grad_mixed_two, first_frame, FRAMES_DEV)), window_keys, window_values, 'qbhd', 'kbhd')
        return (heads_merged(grad_queries), jnp.transpose(row_dot, (2, 0, 1)))
    grad_query_two, row_two = lax.map(time_query, block_ids)
    grad_query_two = grad_query_two.reshape(features.shape)
    row_two = row_two.reshape(total_frames, features.shape[1], HEADS)
    pad_query = padded(query_two)
    pad_grad = padded(grad_mixed_two)
    pad_log = padded(log_two)
    pad_row = padded(row_two)

    def time_key(block_index):
        first_frame = (block_index * FRAMES_DEV).astype(jnp.int32)
        _, behind_mask = window_masks(first_frame, FRAMES_DEV, WINDOW, total_frames)
        grad_keys, grad_values = key_backward(heads_of(cut(pad_query, first_frame, FRAMES_DEV + WINDOW)), heads_of(cut(pad_grad, first_frame, FRAMES_DEV + WINDOW)), jnp.transpose(cut(pad_log, first_frame, FRAMES_DEV + WINDOW), (1, 2, 0)), jnp.transpose(cut(pad_row, first_frame, FRAMES_DEV + WINDOW), (1, 2, 0)), heads_of(cut(key_two, first_frame, FRAMES_DEV)), heads_of(cut(value_two, first_frame, FRAMES_DEV)), behind_mask[None, None], 'qbhd', 'kbhd')
        return (heads_merged(grad_keys.astype(jnp.bfloat16)), heads_merged(grad_values.astype(jnp.bfloat16)))
    grad_key_two, grad_value_two = lax.map(time_key, block_ids)
    grad_key_two = grad_key_two.reshape(features.shape)
    grad_value_two = grad_value_two.reshape(features.shape)
    grad_norm_two = project_back([grad_query_two, grad_key_two, grad_value_two], [weights[4], weights[5], weights[6]])
    hidden_part, gain_two = norm_backward(grad_norm_two, inverse_two, unit_two, gains[1])
    grad_hidden = (upstream.astype(jnp.float32) + hidden_part).astype(jnp.bfloat16)
    grad_mixed_one = project_back([grad_hidden], [weights[3]]).astype(jnp.bfloat16)

    def freq_backward(block_index):
        first_frame = (block_index * FRAMES_DEV).astype(jnp.int32)
        queries = heads_of(cut(query_one, first_frame, FRAMES_DEV))
        key_rows = heads_of(cut(key_one, first_frame, FRAMES_DEV))
        value_rows = heads_of(cut(value_one, first_frame, FRAMES_DEV))
        grad_out = heads_of(cut(grad_mixed_one, first_frame, FRAMES_DEV))
        _, _, attention = attend(queries, key_rows, value_rows, True, 'bqhd', 'bkhd')
        grad_queries, _, grad_scores = query_backward(attention, grad_out, key_rows, value_rows, 'bqhd', 'bkhd')
        grad_keys, grad_values = key_terms(attention, grad_scores, queries, grad_out, 'bqhd', 'bkhd')
        return (heads_merged(grad_queries), heads_merged(grad_keys.astype(jnp.bfloat16)), heads_merged(grad_values.astype(jnp.bfloat16)))
    grad_query_one, grad_key_one, grad_value_one = lax.map(freq_backward, block_ids)
    grad_query_one = grad_query_one.reshape(features.shape)
    grad_key_one = grad_key_one.reshape(features.shape)
    grad_value_one = grad_value_one.reshape(features.shape)
    grad_norm_one = project_back([grad_query_one, grad_key_one, grad_value_one], [weights[0], weights[1], weights[2]])
    input_part, gain_one = norm_backward(grad_norm_one, inverse_one, unit_one, gains[0])
    grad_input = (grad_hidden.astype(jnp.float32) + input_part).astype(jnp.bfloat16)
    inv_root = (features.shape[0] * features.shape[1]) ** (-0.5)
    weight_grads = jnp.stack([weight_grad(norm_one, grad_query_one), weight_grad(norm_one, grad_key_one), weight_grad(norm_one, grad_value_one), weight_grad(mixed_one, grad_hidden), weight_grad(norm_two, grad_query_two), weight_grad(norm_two, grad_key_two), weight_grad(norm_two, grad_value_two), weight_grad(mixed_two, upstream)]) * inv_root
    gain_grads = jnp.stack([gain_one, gain_two]) * inv_root
    return (grad_input, weight_grads, gain_grads)
```

```python
import functools

import jax
import jax.numpy as jnp
from jax import lax
from jax.experimental import pallas as pl
from jax.experimental.pallas import tpu as pltpu
from jax.sharding import PartitionSpec as P

HEADS = 4
WINDOW = 128

epsilon = 1e-06
masked_score = -1e30

f32 = jnp.float32
bf16 = jnp.bfloat16
LANES = 128
VMEM_LIMIT = 48 * 1024 * 1024

CONTRACT_LAST = (((1,), (1,)), ((), ()))
CONTRACT_FIRST = (((0,), (0,)), ((), ()))


def dot(left, right):
    return jnp.dot(left, right, preferred_element_type=f32)


def dot_nt(left, right):
    return lax.dot_general(left, right, CONTRACT_LAST, preferred_element_type=f32)


def dot_tn(left, right):
    return lax.dot_general(left, right, CONTRACT_FIRST, preferred_element_type=f32)


def put(ref, rows, value):
    for c in range(ref.shape[0]):
        ref[c, rows, :] = value[:, c * LANES : (c + 1) * LANES]


def get(ref, rows):
    return jnp.concatenate([ref[c, rows, :] for c in range(ref.shape[0])], axis=1)


def norm_parts(widened):
    inverse = lax.rsqrt(jnp.mean(widened * widened, axis=-1, keepdims=True) + epsilon)
    return inverse, widened * inverse


def norm_backward(incoming, inverse, unit_rows, gain):
    scaled = incoming * gain
    return inverse * (scaled - unit_rows * jnp.mean(scaled * unit_rows, axis=-1, keepdims=True))


def spread(rows, factor):
    width = rows.shape[-1]
    owner = lax.broadcasted_iota(jnp.int32, (1, width), 1) // (width // HEADS)
    return jnp.concatenate(
        [rows * jnp.where(owner == h, factor, 0.0).astype(rows.dtype) for h in range(HEADS)], axis=0
    )


def softmax_heads(scores, keys, allowed):
    parts = []
    for h in range(HEADS):
        s = scores[:, h * keys : (h + 1) * keys]
        if allowed is not None:
            s = jnp.where(allowed, s, masked_score)
        e = jnp.exp(s - jnp.max(s, axis=-1, keepdims=True))
        parts.append(e * (1.0 / jnp.sum(e, axis=-1, keepdims=True)))
    return parts


def attention_backward(probs, grad_out, q, v, k_spread, scale):
    keys = v.shape[0]
    grad_probs = dot_nt(grad_out, spread(v, 1.0))
    grad_scores = []
    for h in range(HEADS):
        gp = grad_probs[:, h * keys : (h + 1) * keys]
        row_dot = jnp.sum(gp * probs[h], axis=-1, keepdims=True)
        grad_scores.append((probs[h] * (gp - row_dot)).astype(bf16))
    g_q = dot(jnp.concatenate(grad_scores, axis=1), k_spread)
    g_k = dot_tn(jnp.concatenate(grad_scores, axis=0), spread(q, scale))
    g_v = dot_tn(
        jnp.concatenate([p.astype(bf16) for p in probs], axis=0), spread(grad_out, 1.0)
    )
    return g_q, g_k, g_v


def freq_forward_kernel(x_ref, w_ref, gain_ref, q_ref, k_ref, v_ref, o_ref, p_ref, h_ref, hold):
    step = pl.program_id(0)
    freq, _, bins_dev, width = x_ref.shape
    bins = freq * bins_dev
    bins_time = hold.shape[2] // pl.num_programs(0)
    scale = (width // HEADS) ** (-0.5)
    x = x_ref[...].reshape(bins, width).astype(f32)
    _, unit = norm_parts(x)
    n = (unit * gain_ref[0:1, :]).astype(bf16)
    q = dot(n, w_ref[0]).astype(bf16)
    k = dot(n, w_ref[1]).astype(bf16)
    v = dot(n, w_ref[2]).astype(bf16)
    probs = softmax_heads(dot_nt(q, spread(k, scale)), bins, None)
    for h in range(HEADS):
        p_ref[0, h] = probs[h]
    o = dot(jnp.concatenate([p.astype(bf16) for p in probs], axis=1), spread(v, 1.0)).astype(bf16)
    hidden = x + dot(o, w_ref[3])
    q_ref[0] = q
    k_ref[0] = k
    v_ref[0] = v
    o_ref[0] = o
    rows = pl.ds(pl.multiple_of(step * bins_time, bins_time), bins_time)
    for f in range(freq):
        part = hidden[f * bins_dev : (f + 1) * bins_dev].reshape(-1, bins_time, width)
        hold[:, f, rows, :] = part

    @pl.when(step == pl.num_programs(0) - 1)
    def _():
        h_ref[...] = hold[...].astype(bf16)


def freq_forward(x, weights, gains, group):
    freq, frames, bins_dev, width = x.shape
    bins = freq * bins_dev
    rows = frames * (bins_dev // group)
    rowspec = pl.BlockSpec((1, bins, width), lambda i: (i, 0, 0))
    rowshape = jax.ShapeDtypeStruct((frames, bins, width), bf16)
    whole = (group, freq, rows, width)
    flops = frames * 2 * bins * (4 * width * width + 2 * HEADS * bins * width)
    return pl.pallas_call(
        freq_forward_kernel,
        grid=(frames,),
        in_specs=[
            pl.BlockSpec((freq, 1, bins_dev, width), lambda i: (0, i, 0, 0)),
            pl.BlockSpec(weights.shape, lambda i: (0, 0, 0)),
            pl.BlockSpec(gains.shape, lambda i: (0, 0)),
        ],
        out_specs=[rowspec] * 4
        + [
            pl.BlockSpec((1, HEADS, bins, bins), lambda i: (i, 0, 0, 0)),
            pl.BlockSpec(whole, lambda i: (0, 0, 0, 0)),
        ],
        out_shape=[rowshape] * 4
        + [
            jax.ShapeDtypeStruct((frames, HEADS, bins, bins), f32),
            jax.ShapeDtypeStruct(whole, bf16),
        ],
        scratch_shapes=[pltpu.VMEM(whole, f32)],
        compiler_params=pltpu.CompilerParams(vmem_limit_bytes=VMEM_LIMIT),
        cost_estimate=pl.CostEstimate(
            flops=flops, bytes_accessed=8 * 1024 * 1024, transcendentals=frames * HEADS * bins * bins
        ),
        name="freq_forward",
    )(x, weights, gains)


def freq_backward_kernel(
    x_ref, q_ref, k_ref, v_ref, o_ref, p_ref, gh_ref, w_ref, gain_ref, gx_ref, dw_ref, dg_ref, hold
):
    step = pl.program_id(0)
    freq, _, bins_dev, width = x_ref.shape
    bins = freq * bins_dev
    group = hold.shape[0]
    bins_time = bins_dev // group
    scale = (width // HEADS) ** (-0.5)

    @pl.when(step == 0)
    def _():
        hold[...] = gh_ref[...].astype(f32)
        dw_ref[...] = jnp.zeros_like(dw_ref)
        dg_ref[...] = jnp.zeros_like(dg_ref)

    rows = pl.ds(pl.multiple_of(step * bins_time, bins_time), bins_time)
    grad_hidden = jnp.concatenate(
        [hold[:, f, rows, :].reshape(bins_dev, width) for f in range(freq)], axis=0
    )
    grad_hidden_low = grad_hidden.astype(bf16)
    grad_out = dot_nt(grad_hidden_low, w_ref[3]).astype(bf16)
    q, k, v = q_ref[0], k_ref[0], v_ref[0]
    probs = [p_ref[0, h] for h in range(HEADS)]
    g_q, g_k, g_v = attention_backward(probs, grad_out, q, v, spread(k, scale), scale)
    g_q, g_k, g_v = g_q.astype(bf16), g_k.astype(bf16), g_v.astype(bf16)
    g_n = dot_nt(g_q, w_ref[0]) + dot_nt(g_k, w_ref[1]) + dot_nt(g_v, w_ref[2])
    x = x_ref[...].reshape(bins, width).astype(f32)
    inverse, unit = norm_parts(x)
    gain = gain_ref[0:1, :]
    n = (unit * gain).astype(bf16)
    grad_x = grad_hidden + norm_backward(g_n, inverse, unit, gain)
    gx_ref[...] = grad_x.astype(bf16).reshape(gx_ref.shape)
    dw_ref[0] += dot_tn(n, g_q)
    dw_ref[1] += dot_tn(n, g_k)
    dw_ref[2] += dot_tn(n, g_v)
    dw_ref[3] += dot_tn(o_ref[0], grad_hidden_low)
    dg_ref[...] += jnp.sum(g_n * unit, axis=0, keepdims=True)


def freq_backward(x, q, k, v, o, probs, grad_hidden, weights, gains):
    freq, frames, bins_dev, width = x.shape
    bins = freq * bins_dev
    rowspec = pl.BlockSpec((1, bins, width), lambda i: (i, 0, 0))
    xspec = pl.BlockSpec((freq, 1, bins_dev, width), lambda i: (0, i, 0, 0))
    flops = frames * 2 * bins * (8 * width * width + 4 * HEADS * bins * width)
    return pl.pallas_call(
        freq_backward_kernel,
        grid=(frames,),
        in_specs=[
            xspec,
            rowspec,
            rowspec,
            rowspec,
            rowspec,
            pl.BlockSpec((1, HEADS, bins, bins), lambda i: (i, 0, 0, 0)),
            pl.BlockSpec(grad_hidden.shape, lambda i: (0, 0, 0, 0)),
            pl.BlockSpec(weights.shape, lambda i: (0, 0, 0)),
            pl.BlockSpec(gains.shape, lambda i: (0, 0)),
        ],
        out_specs=[
            xspec,
            pl.BlockSpec((4, width, width), lambda i: (0, 0, 0)),
            pl.BlockSpec((1, width), lambda i: (0, 0)),
        ],
        out_shape=[
            jax.ShapeDtypeStruct(x.shape, bf16),
            jax.ShapeDtypeStruct((4, width, width), f32),
            jax.ShapeDtypeStruct((1, width), f32),
        ],
        scratch_shapes=[pltpu.VMEM(grad_hidden.shape, f32)],
        compiler_params=pltpu.CompilerParams(vmem_limit_bytes=VMEM_LIMIT),
        cost_estimate=pl.CostEstimate(
            flops=flops, bytes_accessed=8 * 1024 * 1024, transcendentals=0
        ),
        name="freq_backward",
    )(x, q, k, v, o, probs, grad_hidden, weights, gains)


def time_kernel(
    bins, own_start, total_frames, first_ref, h_ref, up_ref, w_ref, gain_ref, gh_ref, dw_ref,
    dg_ref, q_s, k_s, v_s, go_s, o_s, gq_s, gk_s, gv_s
):
    span_rows, width = h_ref.shape
    span = span_rows // bins
    own_rows = gh_ref.shape[0]
    own = own_rows // bins
    scale = (width // HEADS) ** (-0.5)
    gain = gain_ref[1:2, :]
    chunk = own_rows
    while chunk > 256 and chunk % 32 == 0:
        chunk //= 2

    def project(i, carry):
        rows = pl.ds(pl.multiple_of(i * chunk, chunk), chunk)
        _, unit = norm_parts(h_ref[rows, :].astype(f32))
        n = (unit * gain).astype(bf16)
        put(q_s, rows, dot(n, w_ref[4]))
        put(k_s, rows, dot(n, w_ref[5]))
        put(v_s, rows, dot(n, w_ref[6]))
        put(go_s, rows, dot_nt(up_ref[rows, :], w_ref[7]))
        return carry

    lax.fori_loop(0, span_rows // chunk, project, 0)

    query = lax.broadcasted_iota(jnp.int32, (span, span), 0)
    key = lax.broadcasted_iota(jnp.int32, (span, span), 1)
    distance = key - query
    allowed = (distance >= -(WINDOW // 2)) & (distance < WINDOW // 2)
    if own != span:
        frame = first_ref[0] + key
        allowed = allowed & (frame >= 0) & (frame < total_frames)

    def attend(b, carry):
        rows = pl.ds(b, span, stride=bins)
        q = get(q_s, rows).astype(bf16)
        k = get(k_s, rows).astype(bf16)
        v = get(v_s, rows).astype(bf16)
        grad_out = get(go_s, rows).astype(bf16)
        k_spread = spread(k, scale)
        probs = softmax_heads(dot_nt(q, k_spread), span, allowed)
        o = dot(jnp.concatenate([p.astype(bf16) for p in probs], axis=1), spread(v, 1.0))
        g_q, g_k, g_v = attention_backward(probs, grad_out, q, v, k_spread, scale)
        put(o_s, rows, o)
        put(gq_s, rows, g_q)
        put(gk_s, rows, g_k)
        put(gv_s, rows, g_v)
        return carry

    lax.fori_loop(0, bins, attend, 0)

    dw_ref[...] = jnp.zeros_like(dw_ref)
    dg_ref[...] = jnp.zeros_like(dg_ref)

    def finish(i, carry):
        mine = pl.ds(pl.multiple_of(i * chunk, chunk), chunk)
        rows = pl.ds(pl.multiple_of(own_start + i * chunk, chunk), chunk)
        g_q = get(gq_s, rows).astype(bf16)
        g_k = get(gk_s, rows).astype(bf16)
        g_v = get(gv_s, rows).astype(bf16)
        g_n = dot_nt(g_q, w_ref[4]) + dot_nt(g_k, w_ref[5]) + dot_nt(g_v, w_ref[6])
        inverse, unit = norm_parts(h_ref[rows, :].astype(f32))
        n = (unit * gain).astype(bf16)
        up = up_ref[rows, :]
        grad_hidden = up.astype(f32) + norm_backward(g_n, inverse, unit, gain)
        gh_ref[mine, :] = grad_hidden.astype(bf16)
        dw_ref[0] += dot_tn(n, g_q)
        dw_ref[1] += dot_tn(n, g_k)
        dw_ref[2] += dot_tn(n, g_v)
        dw_ref[3] += dot_tn(get(o_s, rows).astype(bf16), up)
        dg_ref[...] += jnp.sum(g_n * unit, axis=0, keepdims=True)
        return carry

    lax.fori_loop(0, own_rows // chunk, finish, 0)


def time_attention(first, hidden, upstream, weights, gains, bins, own_start, own_rows, total):
    span_rows, width = hidden.shape
    vmem = pl.BlockSpec(memory_space=pltpu.VMEM)
    span = span_rows // bins
    flops = 2 * span_rows * (11 * width * width + 6 * HEADS * span * width)
    return pl.pallas_call(
        functools.partial(time_kernel, bins, own_start, total),
        in_specs=[pl.BlockSpec(memory_space=pltpu.SMEM)] + [vmem] * 4,
        out_specs=[vmem] * 3,
        out_shape=[
            jax.ShapeDtypeStruct((own_rows, width), bf16),
            jax.ShapeDtypeStruct((4, width, width), f32),
            jax.ShapeDtypeStruct((1, width), f32),
        ],
        scratch_shapes=[pltpu.VMEM((width // LANES, span_rows, LANES), f32)] * 8,
        compiler_params=pltpu.CompilerParams(vmem_limit_bytes=VMEM_LIMIT),
        cost_estimate=pl.CostEstimate(
            flops=flops,
            bytes_accessed=4 * 1024 * 1024,
            transcendentals=bins * HEADS * span * span,
        ),
        name="time_attention",
    )(first, hidden, upstream, weights, gains)


def group_size(devices, bins_dev):
    best = 1
    for size in range(1, devices + 1):
        if devices % size == 0 and bins_dev % (8 * size) == 0:
            best = size
    return best


def per_device(features, upstream, weights, gains):
    frames_dev, bins_dev, width = features.shape
    tm, freq = lax.axis_size("tm"), lax.axis_size("freq")
    total_frames = frames_dev * tm
    frames = frames_dev // freq
    group = group_size(tm, bins_dev)
    bins_time = bins_dev // group
    group_frames = group * frames_dev
    whole = group == tm
    sides = 0 if whole else -(-WINDOW // group_frames)
    groups = (
        None
        if whole
        else [list(range(g * group, (g + 1) * group)) for g in range(tm // group)]
    )

    def over_tm(blocks):
        return lax.all_to_all(blocks, "tm", 0, 0, tiled=True, axis_index_groups=groups)

    def over_all(blocks):
        if whole:
            flat = blocks.reshape((tm * freq,) + blocks.shape[2:])
            return lax.all_to_all(flat, ("tm", "freq"), 0, 0, tiled=True).reshape(blocks.shape)
        return over_tm(lax.all_to_all(blocks, "freq", 1, 1, tiled=True))

    def with_sides(rows):
        parts = [rows]
        for away in range(1, sides + 1):
            shift = away * group
            before = lax.ppermute(rows, "tm", [(i, i + shift) for i in range(tm - shift)])
            after = lax.ppermute(rows, "tm", [(i + shift, i) for i in range(tm - shift)])
            parts = [before] + parts + [after]
        return jnp.concatenate(parts, axis=0) if sides else rows

    x = lax.all_to_all(
        features.reshape(freq, frames, bins_dev, width), "freq", 0, 0, tiled=True
    )
    up_blocks = jnp.swapaxes(upstream.reshape(frames_dev, group, bins_time, width), 0, 1)
    up_rows = over_tm(up_blocks).reshape(-1, width)
    q, k, v, o, probs, hidden_blocks = freq_forward(x, weights, gains, group)
    hidden_rows = over_all(hidden_blocks).reshape(-1, width)
    own_rows = hidden_rows.shape[0]
    position = lax.axis_index("tm") // group
    first = ((position - sides) * group_frames).astype(jnp.int32).reshape(1)
    grad_rows, time_dw, time_dg = time_attention(
        first,
        with_sides(hidden_rows),
        with_sides(up_rows),
        weights,
        gains,
        bins_time,
        sides * own_rows,
        own_rows,
        total_frames,
    )
    grad_hidden = over_all(grad_rows.reshape(hidden_blocks.shape))
    grad_x, freq_dw, freq_dg = freq_backward(
        x, q, k, v, o, probs, grad_hidden, weights, gains
    )
    grad_input = lax.all_to_all(grad_x, "freq", 0, 0, tiled=True).reshape(features.shape)

    inv_root = (total_frames * bins_dev * freq) ** (-0.5)
    devices = tm * freq
    partial = jnp.concatenate([freq_dw, time_dw], axis=0)
    pieces = (partial * inv_root).astype(bf16).reshape(devices, -1, width)
    gain_rows = jnp.concatenate([freq_dg, time_dg], axis=0) * inv_root
    high = gain_rows.astype(bf16)
    low = (gain_rows - high.astype(f32)).astype(bf16)
    extra = jnp.broadcast_to(jnp.concatenate([high, low], axis=0)[None], (devices, 4, width))
    sent = jnp.concatenate([pieces, extra], axis=1)
    arrived = lax.all_to_all(sent, ("tm", "freq"), 0, 0, tiled=True)
    summed = jnp.sum(arrived.astype(f32), axis=0)
    count = pieces.shape[1]
    gain_grads = summed[count : count + 2] + summed[count + 2 :]
    own = summed[:count].astype(bf16)
    gathered = lax.all_to_all(
        jnp.broadcast_to(own[None], (devices,) + own.shape), ("tm", "freq"), 0, 0, tiled=True
    )
    weight_grads = gathered.astype(f32).reshape(partial.shape)
    return (grad_input, weight_grads, gain_grads)


def solution(mesh):
    return jax.shard_map(
        per_device,
        mesh=mesh,
        in_specs=(P("tm", "freq", None), P("tm", "freq", None), P(), P()),
        out_specs=(P("tm", "freq", None), P(), P()),
        check_vma=False,
    )
```

```python
import functools

import jax
import jax.numpy as jnp
from jax import lax
from jax.experimental import pallas as pl
from jax.experimental.pallas import tpu as pltpu
from jax.sharding import PartitionSpec as P

HEADS = 4
WINDOW = 128

epsilon = 1e-06
masked_score = -1e30

f32 = jnp.float32
bf16 = jnp.bfloat16
LANES = 128
VMEM_LIMIT = 48 * 1024 * 1024

CONTRACT_LAST = (((1,), (1,)), ((), ()))
CONTRACT_FIRST = (((0,), (0,)), ((), ()))


def dot(left, right):
    return jnp.dot(left, right, preferred_element_type=f32)


def dot_nt(left, right):
    return lax.dot_general(left, right, CONTRACT_LAST, preferred_element_type=f32)


def dot_tn(left, right):
    return lax.dot_general(left, right, CONTRACT_FIRST, preferred_element_type=f32)


def put(ref, rows, value):
    for c in range(ref.shape[0]):
        ref[c, rows, :] = value[:, c * LANES : (c + 1) * LANES]


def get(ref, rows):
    return jnp.concatenate([ref[c, rows, :] for c in range(ref.shape[0])], axis=1)


def norm_parts(widened):
    inverse = lax.rsqrt(jnp.mean(widened * widened, axis=-1, keepdims=True) + epsilon)
    return inverse, widened * inverse


def norm_backward(incoming, inverse, unit_rows, gain):
    scaled = incoming * gain
    return inverse * (scaled - unit_rows * jnp.mean(scaled * unit_rows, axis=-1, keepdims=True))


def spread(rows, factor):
    width = rows.shape[-1]
    owner = lax.broadcasted_iota(jnp.int32, (1, width), 1) // (width // HEADS)
    return jnp.concatenate(
        [rows * jnp.where(owner == h, factor, 0.0).astype(rows.dtype) for h in range(HEADS)], axis=0
    )


def softmax_heads(scores, keys, allowed):
    parts = []
    for h in range(HEADS):
        s = scores[:, h * keys : (h + 1) * keys]
        if allowed is not None:
            s = jnp.where(allowed, s, masked_score)
        e = jnp.exp(s - jnp.max(s, axis=-1, keepdims=True))
        parts.append(e * (1.0 / jnp.sum(e, axis=-1, keepdims=True)))
    return parts


def attention_backward(probs, grad_out, q, v, k_spread, scale):
    keys = v.shape[0]
    grad_probs = dot_nt(grad_out, spread(v, 1.0))
    grad_scores = []
    for h in range(HEADS):
        gp = grad_probs[:, h * keys : (h + 1) * keys]
        row_dot = jnp.sum(gp * probs[h], axis=-1, keepdims=True)
        grad_scores.append((probs[h] * (gp - row_dot)).astype(bf16))
    g_q = dot(jnp.concatenate(grad_scores, axis=1), k_spread)
    g_k = dot_tn(jnp.concatenate(grad_scores, axis=0), spread(q, scale))
    g_v = dot_tn(
        jnp.concatenate([p.astype(bf16) for p in probs], axis=0), spread(grad_out, 1.0)
    )
    return g_q, g_k, g_v


def slot_of(position, back, freq):
    return lax.rem(position - back + freq, freq)


def freq_forward_kernel(
    place_ref, own_ref, others_ref, w_ref, gain_ref, q_ref, k_ref, v_ref, o_ref, p_ref, h_ref, hold
):
    step = pl.program_id(0)
    freq, bins_dev, width = others_ref.shape[0] + 1, own_ref.shape[2], own_ref.shape[3]
    bins = freq * bins_dev
    bins_time = hold.shape[2] // pl.num_programs(0)
    scale = (width // HEADS) ** (-0.5)
    x = joined(own_ref, others_ref)
    _, unit = norm_parts(x)
    n = (unit * gain_ref[0:1, :]).astype(bf16)
    q = dot(n, w_ref[0]).astype(bf16)
    k = dot(n, w_ref[1]).astype(bf16)
    v = dot(n, w_ref[2]).astype(bf16)
    probs = softmax_heads(dot_nt(q, spread(k, scale)), bins, None)
    for h in range(HEADS):
        p_ref[0, h] = probs[h]
    o = dot(jnp.concatenate([p.astype(bf16) for p in probs], axis=1), spread(v, 1.0)).astype(bf16)
    hidden = x + dot(o, w_ref[3])
    q_ref[0] = q
    k_ref[0] = k
    v_ref[0] = v
    o_ref[0] = o
    rows = pl.ds(pl.multiple_of(step * bins_time, bins_time), bins_time)
    for f in range(freq):
        part = hidden[f * bins_dev : (f + 1) * bins_dev].reshape(-1, bins_time, width)
        hold[:, slot_of(place_ref[0], f, freq), rows, :] = part

    @pl.when(step == pl.num_programs(0) - 1)
    def _():
        h_ref[...] = hold[...].astype(bf16)


def joined(own_ref, others_ref):
    width = own_ref.shape[-1]
    return jnp.concatenate(
        [own_ref[...].reshape(-1, width), others_ref[...].reshape(-1, width)], axis=0
    ).astype(f32)


def frame_specs(freq, bins_dev, width):
    own = pl.BlockSpec((1, 1, bins_dev, width), lambda i, place: (place[0], i, 0, 0))
    others = pl.BlockSpec((freq - 1, 1, bins_dev, width), lambda i, place: (0, i, 0, 0))
    rows = pl.BlockSpec((1, freq * bins_dev, width), lambda i, place: (i, 0, 0))
    return own, others, rows


def fixed(shape):
    return pl.BlockSpec(shape, lambda i, place: (0,) * len(shape))


def freq_forward(place, features, others, weights, gains, group):
    freq, frames, bins_dev, width = features.shape
    bins = freq * bins_dev
    rows = frames * (bins_dev // group)
    own_spec, others_spec, row_spec = frame_specs(freq, bins_dev, width)
    rowshape = jax.ShapeDtypeStruct((frames, bins, width), bf16)
    whole = (group, freq, rows, width)
    flops = frames * 2 * bins * (4 * width * width + 2 * HEADS * bins * width)
    return pl.pallas_call(
        freq_forward_kernel,
        grid_spec=pltpu.PrefetchScalarGridSpec(
            num_scalar_prefetch=1,
            grid=(frames,),
            in_specs=[own_spec, others_spec, fixed(weights.shape), fixed(gains.shape)],
            out_specs=[row_spec] * 4
            + [pl.BlockSpec((1, HEADS, bins, bins), lambda i, place: (i, 0, 0, 0)), fixed(whole)],
            scratch_shapes=[pltpu.VMEM(whole, f32)],
        ),
        out_shape=[rowshape] * 4
        + [
            jax.ShapeDtypeStruct((frames, HEADS, bins, bins), f32),
            jax.ShapeDtypeStruct(whole, bf16),
        ],
        compiler_params=pltpu.CompilerParams(vmem_limit_bytes=VMEM_LIMIT),
        cost_estimate=pl.CostEstimate(
            flops=flops, bytes_accessed=8 * 1024 * 1024, transcendentals=frames * HEADS * bins * bins
        ),
        name="freq_forward",
    )(place, features, others, weights, gains)


def freq_backward_kernel(
    place_ref, own_ref, others_ref, q_ref, k_ref, v_ref, o_ref, p_ref, gh_ref, w_ref, gain_ref,
    gq_ref, gk_ref, gv_ref, dw_ref, hold, total
):
    step = pl.program_id(0)
    freq, bins_dev, width = others_ref.shape[0] + 1, own_ref.shape[2], own_ref.shape[3]
    group = hold.shape[0]
    bins_time = bins_dev // group
    scale = (width // HEADS) ** (-0.5)

    @pl.when(step == 0)
    def _():
        hold[...] = gh_ref[...].astype(f32)
        total[...] = jnp.zeros_like(total)

    grad_hidden = grad_hidden_rows(place_ref, hold, step, freq, bins_time).astype(bf16)
    grad_out = dot_nt(grad_hidden, w_ref[3]).astype(bf16)
    q, k, v = q_ref[0], k_ref[0], v_ref[0]
    probs = [p_ref[0, h] for h in range(HEADS)]
    g_q, g_k, g_v = attention_backward(probs, grad_out, q, v, spread(k, scale), scale)
    g_q, g_k, g_v = g_q.astype(bf16), g_k.astype(bf16), g_v.astype(bf16)
    gq_ref[0] = g_q
    gk_ref[0] = g_k
    gv_ref[0] = g_v
    _, unit = norm_parts(joined(own_ref, others_ref))
    n = (unit * gain_ref[0:1, :]).astype(bf16)
    total[0] += dot_tn(n, g_q)
    total[1] += dot_tn(n, g_k)
    total[2] += dot_tn(n, g_v)
    total[3] += dot_tn(o_ref[0], grad_hidden)

    @pl.when(step == pl.num_programs(0) - 1)
    def _():
        dw_ref[...] = total[...].astype(bf16)


def grad_hidden_rows(place_ref, hold, step, freq, bins_time):
    width = hold.shape[-1]
    rows = pl.ds(pl.multiple_of(step * bins_time, bins_time), bins_time)
    return jnp.concatenate(
        [hold[:, slot_of(place_ref[0], f, freq), rows, :].reshape(-1, width) for f in range(freq)],
        axis=0,
    )


def freq_backward(place, features, others, q, k, v, o, probs, grad_hidden, weights, gains):
    freq, frames, bins_dev, width = features.shape
    bins = freq * bins_dev
    own_spec, others_spec, row_spec = frame_specs(freq, bins_dev, width)
    flops = frames * 2 * bins * (5 * width * width + 4 * HEADS * bins * width)
    rowshape = jax.ShapeDtypeStruct((frames, bins, width), bf16)
    return pl.pallas_call(
        freq_backward_kernel,
        grid_spec=pltpu.PrefetchScalarGridSpec(
            num_scalar_prefetch=1,
            grid=(frames,),
            in_specs=[own_spec, others_spec]
            + [row_spec] * 4
            + [
                pl.BlockSpec((1, HEADS, bins, bins), lambda i, place: (i, 0, 0, 0)),
                fixed(grad_hidden.shape),
                fixed(weights.shape),
                fixed(gains.shape),
            ],
            out_specs=[row_spec] * 3 + [fixed((4, width, width))],
            scratch_shapes=[
                pltpu.VMEM(grad_hidden.shape, f32),
                pltpu.VMEM((4, width, width), f32),
            ],
        ),
        out_shape=[rowshape] * 3 + [jax.ShapeDtypeStruct((4, width, width), bf16)],
        compiler_params=pltpu.CompilerParams(vmem_limit_bytes=VMEM_LIMIT),
        cost_estimate=pl.CostEstimate(
            flops=flops, bytes_accessed=8 * 1024 * 1024, transcendentals=0
        ),
        name="freq_backward",
    )(place, features, others, q, k, v, o, probs, grad_hidden, weights, gains)


def input_grad_kernel(
    place_ref, own_ref, others_ref, gq_ref, gk_ref, gv_ref, gh_ref, w_ref, gain_ref,
    gown_ref, gothers_ref, dg_ref, hold
):
    step = pl.program_id(0)
    freq, bins_dev, width = others_ref.shape[0] + 1, own_ref.shape[2], own_ref.shape[3]
    group = hold.shape[0]

    @pl.when(step == 0)
    def _():
        hold[...] = gh_ref[...].astype(f32)
        dg_ref[...] = jnp.zeros_like(dg_ref)

    g_n = dot_nt(gq_ref[0], w_ref[0]) + dot_nt(gk_ref[0], w_ref[1]) + dot_nt(gv_ref[0], w_ref[2])
    inverse, unit = norm_parts(joined(own_ref, others_ref))
    grad_hidden = grad_hidden_rows(place_ref, hold, step, freq, bins_dev // group)
    grad_x = grad_hidden + norm_backward(g_n, inverse, unit, gain_ref[0:1, :])
    grad_x = grad_x.astype(bf16)
    gown_ref[0] = grad_x[:bins_dev]
    gothers_ref[...] = grad_x[bins_dev:].reshape(gothers_ref.shape)
    dg_ref[...] += jnp.sum(g_n * unit, axis=0, keepdims=True)


def input_grad(place, features, others, g_q, g_k, g_v, grad_hidden, weights, gains):
    freq, frames, bins_dev, width = features.shape
    own_spec, others_spec, row_spec = frame_specs(freq, bins_dev, width)
    flops = frames * 2 * freq * bins_dev * 3 * width * width
    return pl.pallas_call(
        input_grad_kernel,
        grid_spec=pltpu.PrefetchScalarGridSpec(
            num_scalar_prefetch=1,
            grid=(frames,),
            in_specs=[own_spec, others_spec]
            + [row_spec] * 3
            + [fixed(grad_hidden.shape), fixed(weights.shape), fixed(gains.shape)],
            out_specs=[
                pl.BlockSpec((1, bins_dev, width), lambda i, place: (i, 0, 0)),
                others_spec,
                fixed((1, width)),
            ],
            scratch_shapes=[pltpu.VMEM(grad_hidden.shape, f32)],
        ),
        out_shape=[
            jax.ShapeDtypeStruct((frames, bins_dev, width), bf16),
            jax.ShapeDtypeStruct(others.shape, bf16),
            jax.ShapeDtypeStruct((1, width), f32),
        ],
        compiler_params=pltpu.CompilerParams(vmem_limit_bytes=VMEM_LIMIT),
        cost_estimate=pl.CostEstimate(
            flops=flops, bytes_accessed=4 * 1024 * 1024, transcendentals=0
        ),
        name="input_grad",
    )(place, features, others, g_q, g_k, g_v, grad_hidden, weights, gains)


def time_kernel(
    bins, own_start, total_frames, first_ref, h_ref, up_ref, w_ref, gain_ref, gh_ref, n_ref,
    o_ref, gq_ref, gk_ref, gv_ref, dg_ref, q_s, k_s, v_s, go_s, o_s, gq_s, gk_s, gv_s
):
    span_rows, width = h_ref.shape
    span = span_rows // bins
    own_rows = gh_ref.shape[0]
    own = own_rows // bins
    scale = (width // HEADS) ** (-0.5)
    gain = gain_ref[1:2, :]
    chunk = own_rows
    while chunk > 256 and chunk % 32 == 0:
        chunk //= 2

    def project(i, carry):
        rows = pl.ds(pl.multiple_of(i * chunk, chunk), chunk)
        _, unit = norm_parts(h_ref[rows, :].astype(f32))
        n = (unit * gain).astype(bf16)
        put(q_s, rows, dot(n, w_ref[4]))
        put(k_s, rows, dot(n, w_ref[5]))
        put(v_s, rows, dot(n, w_ref[6]))
        put(go_s, rows, dot_nt(up_ref[rows, :], w_ref[7]))
        return carry

    lax.fori_loop(0, span_rows // chunk, project, 0)

    query = lax.broadcasted_iota(jnp.int32, (span, span), 0)
    key = lax.broadcasted_iota(jnp.int32, (span, span), 1)
    distance = key - query
    allowed = (distance >= -(WINDOW // 2)) & (distance < WINDOW // 2)
    if own != span:
        frame = first_ref[0] + key
        allowed = allowed & (frame >= 0) & (frame < total_frames)

    def attend(b, carry):
        rows = pl.ds(b, span, stride=bins)
        q = get(q_s, rows).astype(bf16)
        k = get(k_s, rows).astype(bf16)
        v = get(v_s, rows).astype(bf16)
        grad_out = get(go_s, rows).astype(bf16)
        k_spread = spread(k, scale)
        probs = softmax_heads(dot_nt(q, k_spread), span, allowed)
        o = dot(jnp.concatenate([p.astype(bf16) for p in probs], axis=1), spread(v, 1.0))
        g_q, g_k, g_v = attention_backward(probs, grad_out, q, v, k_spread, scale)
        put(o_s, rows, o)
        put(gq_s, rows, g_q)
        put(gk_s, rows, g_k)
        put(gv_s, rows, g_v)
        return carry

    lax.fori_loop(0, bins, attend, 0)

    dg_ref[...] = jnp.zeros_like(dg_ref)

    def finish(i, carry):
        mine = pl.ds(pl.multiple_of(i * chunk, chunk), chunk)
        rows = pl.ds(pl.multiple_of(own_start + i * chunk, chunk), chunk)
        g_q = get(gq_s, rows).astype(bf16)
        g_k = get(gk_s, rows).astype(bf16)
        g_v = get(gv_s, rows).astype(bf16)
        g_n = dot_nt(g_q, w_ref[4]) + dot_nt(g_k, w_ref[5]) + dot_nt(g_v, w_ref[6])
        inverse, unit = norm_parts(h_ref[rows, :].astype(f32))
        n = (unit * gain).astype(bf16)
        up = up_ref[rows, :]
        grad_hidden = up.astype(f32) + norm_backward(g_n, inverse, unit, gain)
        gh_ref[mine, :] = grad_hidden.astype(bf16)
        n_ref[mine, :] = n
        o_ref[mine, :] = get(o_s, rows).astype(bf16)
        gq_ref[mine, :] = g_q
        gk_ref[mine, :] = g_k
        gv_ref[mine, :] = g_v
        dg_ref[...] += jnp.sum(g_n * unit, axis=0, keepdims=True)
        return carry

    lax.fori_loop(0, own_rows // chunk, finish, 0)


def time_attention(first, hidden, upstream, weights, gains, bins, own_start, own_rows, total):
    span_rows, width = hidden.shape
    vmem = pl.BlockSpec(memory_space=pltpu.VMEM)
    span = span_rows // bins
    flops = 2 * span_rows * (7 * width * width + 6 * HEADS * span * width)
    return pl.pallas_call(
        functools.partial(time_kernel, bins, own_start, total),
        in_specs=[pl.BlockSpec(memory_space=pltpu.SMEM)] + [vmem] * 4,
        out_specs=[vmem] * 7,
        out_shape=[jax.ShapeDtypeStruct((own_rows, width), bf16)] * 6
        + [jax.ShapeDtypeStruct((1, width), f32)],
        scratch_shapes=[pltpu.VMEM((width // LANES, span_rows, LANES), f32)] * 8,
        compiler_params=pltpu.CompilerParams(vmem_limit_bytes=VMEM_LIMIT),
        cost_estimate=pl.CostEstimate(
            flops=flops,
            bytes_accessed=4 * 1024 * 1024,
            transcendentals=bins * HEADS * span * span,
        ),
        name="time_attention",
    )(first, hidden, upstream, weights, gains)


def weight_kernel(n_ref, o_ref, gq_ref, gk_ref, gv_ref, up_ref, dw_ref):
    n = n_ref[...]
    dw_ref[0] = dot_tn(n, gq_ref[...]).astype(bf16)
    dw_ref[1] = dot_tn(n, gk_ref[...]).astype(bf16)
    dw_ref[2] = dot_tn(n, gv_ref[...]).astype(bf16)
    dw_ref[3] = dot_tn(o_ref[...], up_ref[...]).astype(bf16)


def time_weights(n, o, g_q, g_k, g_v, upstream):
    rows, width = n.shape
    vmem = pl.BlockSpec(memory_space=pltpu.VMEM)
    return pl.pallas_call(
        weight_kernel,
        in_specs=[vmem] * 6,
        out_specs=vmem,
        out_shape=jax.ShapeDtypeStruct((4, width, width), bf16),
        compiler_params=pltpu.CompilerParams(vmem_limit_bytes=VMEM_LIMIT),
        cost_estimate=pl.CostEstimate(
            flops=8 * rows * width * width, bytes_accessed=4 * 1024 * 1024, transcendentals=0
        ),
        name="time_weights",
    )(n, o, g_q, g_k, g_v, upstream)


def group_size(devices, bins_dev):
    best = 1
    for size in range(1, devices + 1):
        if devices % size == 0 and bins_dev % (8 * size) == 0:
            best = size
    return best


def per_device(features, upstream, weights, gains):
    frames_dev, bins_dev, width = features.shape
    tm, freq = lax.axis_size("tm"), lax.axis_size("freq")
    total_frames = frames_dev * tm
    frames = frames_dev // freq
    group = group_size(tm, bins_dev)
    bins_time = bins_dev // group
    group_frames = group * frames_dev
    whole = group == tm
    sides = 0 if whole else -(-WINDOW // group_frames)
    groups = (
        None
        if whole
        else [list(range(g * group, (g + 1) * group)) for g in range(tm // group)]
    )

    def over_tm(blocks):
        return lax.all_to_all(blocks, "tm", 0, 0, tiled=True, axis_index_groups=groups)

    def over_all(blocks):
        if whole:
            flat = blocks.reshape((tm * freq,) + blocks.shape[2:])
            return lax.all_to_all(flat, ("tm", "freq"), 0, 0, tiled=True).reshape(blocks.shape)
        return over_tm(lax.all_to_all(blocks, "freq", 1, 1, tiled=True))

    def with_sides(rows):
        parts = [rows]
        for away in range(1, sides + 1):
            shift = away * group
            before = lax.ppermute(rows, "tm", [(i, i + shift) for i in range(tm - shift)])
            after = lax.ppermute(rows, "tm", [(i + shift, i) for i in range(tm - shift)])
            parts = [before] + parts + [after]
        return jnp.concatenate(parts, axis=0) if sides else rows

    place = lax.axis_index("freq").astype(jnp.int32).reshape(1)
    by_target = features.reshape(freq, frames, bins_dev, width)

    def along_freq(block, steps):
        return lax.ppermute(block, "freq", [(i, (i + steps) % freq) for i in range(freq)])

    others = jnp.stack(
        [
            along_freq(lax.dynamic_index_in_dim(by_target, (place[0] + j) % freq, 0, False), j)
            for j in range(1, freq)
        ]
    )
    up_blocks = jnp.swapaxes(upstream.reshape(frames_dev, group, bins_time, width), 0, 1)
    up_rows = over_tm(up_blocks).reshape(-1, width)
    q, k, v, o, probs, hidden_blocks = freq_forward(
        place, by_target, others, weights, gains, group
    )
    hidden_rows = over_all(hidden_blocks).reshape(-1, width)
    own_rows = hidden_rows.shape[0]
    position = lax.axis_index("tm") // group
    first = ((position - sides) * group_frames).astype(jnp.int32).reshape(1)
    grad_rows, n2, o2, g_q2, g_k2, g_v2, time_dg = time_attention(
        first,
        with_sides(hidden_rows),
        with_sides(up_rows),
        weights,
        gains,
        bins_time,
        sides * own_rows,
        own_rows,
        total_frames,
    )
    grad_hidden = over_all(grad_rows.reshape(hidden_blocks.shape))
    time_dw = time_weights(n2, o2, g_q2, g_k2, g_v2, up_rows)

    core = lax.axis_index("tm") % 2
    pairs = [(i, i ^ 1) for i in range(tm)]
    same = [
        [t * freq + f for t in range(c, tm, 2) for f in range(freq)] for c in range(2)
    ]
    peers = len(same[0])

    def over_same(blocks):
        return lax.all_to_all(
            blocks, ("tm", "freq"), 0, 0, tiled=True, axis_index_groups=same
        )

    def pair_sum(partial):
        halves = partial.reshape(2, -1, width)
        arrived = lax.ppermute(
            lax.dynamic_index_in_dim(halves, 1 - core, 0, False), "tm", pairs
        )
        kept = lax.dynamic_index_in_dim(halves, core, 0, False)
        return (kept.astype(f32) + arrived.astype(f32)).astype(bf16).reshape(peers, -1, width)

    time_half = pair_sum(time_dw)
    g_q1, g_k1, g_v1, freq_dw = freq_backward(
        place, by_target, others, q, k, v, o, probs, grad_hidden, weights, gains
    )
    freq_half = pair_sum(freq_dw)
    arrived = over_same(jnp.concatenate([freq_half, time_half], axis=1))
    grad_own, grad_others, freq_dg = input_grad(
        place, by_target, others, g_q1, g_k1, g_v1, grad_hidden, weights, gains
    )
    returned = [grad_own] + [along_freq(grad_others[j - 1], -j) for j in range(1, freq)]
    grad_input = jnp.roll(jnp.stack(returned), place[0], axis=0).reshape(features.shape)

    inv_root = (total_frames * bins_dev * freq) ** (-0.5)

    def split(rows):
        high = rows.astype(bf16)
        return [high, (rows - high.astype(f32)).astype(bf16)]

    summed = jnp.sum(arrived.astype(f32), axis=0) * inv_root
    count = summed.shape[0]
    gain_rows = jnp.concatenate([freq_dg, time_dg], axis=0) * inv_root
    sent = jnp.concatenate([summed.astype(bf16)] + split(gain_rows), axis=0)
    gathered = over_same(jnp.broadcast_to(sent[None], (peers,) + sent.shape))
    gain_sum = jnp.sum(gathered[:, count:].astype(f32), axis=0)
    gain_sum = gain_sum[:2] + gain_sum[2:]
    mine = gathered[:, :count].reshape(-1, width)
    theirs = lax.ppermute(jnp.concatenate([mine] + split(gain_sum), axis=0), "tm", pairs)
    gain_high_low = split(gain_sum)
    other_gain = theirs[-4:].astype(f32)
    gain_grads = sum(g.astype(f32) for g in gain_high_low) + other_gain[:2] + other_gain[2:]
    theirs = theirs[:-4]
    first_core = core == 0
    halves = jnp.stack(
        [jnp.where(first_core, mine, theirs), jnp.where(first_core, theirs, mine)]
    )
    weight_grads = (
        halves.reshape(2, peers, 2, -1, width).transpose(2, 0, 1, 3, 4).astype(f32)
    ).reshape(8, width, width)
    return (grad_input, weight_grads, gain_grads)


def solution(mesh):
    return jax.shard_map(
        per_device,
        mesh=mesh,
        in_specs=(P("tm", "freq", None), P("tm", "freq", None), P(), P()),
        out_specs=(P("tm", "freq", None), P(), P()),
        check_vma=False,
    )
```

```python
import functools

import jax
import jax.numpy as jnp
from jax import lax
from jax.experimental import pallas as pl
from jax.experimental.pallas import tpu as pltpu
from jax.sharding import PartitionSpec as P

HEADS = 4
WINDOW = 128

epsilon = 1e-06
masked_score = -1e30

f32 = jnp.float32
bf16 = jnp.bfloat16
LANES = 128
VMEM_LIMIT = 62 * 1024 * 1024

CONTRACT_LAST = (((1,), (1,)), ((), ()))
CONTRACT_FIRST = (((0,), (0,)), ((), ()))


def dot(left, right):
    return jnp.dot(left, right, preferred_element_type=f32)


def dot_nt(left, right):
    return lax.dot_general(left, right, CONTRACT_LAST, preferred_element_type=f32)


def dot_tn(left, right):
    return lax.dot_general(left, right, CONTRACT_FIRST, preferred_element_type=f32)


def put(ref, rows, value):
    for c in range(ref.shape[0]):
        ref[c, rows, :] = value[:, c * LANES : (c + 1) * LANES]


def get(ref, rows):
    return jnp.concatenate([ref[c, rows, :] for c in range(ref.shape[0])], axis=1)


def norm_parts(widened):
    inverse = lax.rsqrt(jnp.mean(widened * widened, axis=-1, keepdims=True) + epsilon)
    return inverse, widened * inverse


def norm_backward(incoming, inverse, unit_rows, gain):
    scaled = incoming * gain
    return inverse * (scaled - unit_rows * jnp.mean(scaled * unit_rows, axis=-1, keepdims=True))


def spread(rows, factor):
    width = rows.shape[-1]
    owner = lax.broadcasted_iota(jnp.int32, (1, width), 1) // (width // HEADS)
    return jnp.concatenate(
        [rows * jnp.where(owner == h, factor, 0.0).astype(rows.dtype) for h in range(HEADS)], axis=0
    )


def own_channels(stacked, rows):
    width = stacked.shape[-1]
    owner = lax.broadcasted_iota(jnp.int32, (1, width), 1) // (width // HEADS)
    result = stacked[:rows]
    for h in range(1, HEADS):
        result = jnp.where(owner == h, stacked[h * rows : (h + 1) * rows], result)
    return result


def head_probs(scores, allowed):
    rows = scores.shape[0] // HEADS
    probs = []
    for h in range(HEADS):
        s = scores[h * rows : (h + 1) * rows]
        if allowed is not None:
            s = jnp.where(allowed, s, masked_score)
        e = jnp.exp(s - jnp.max(s, axis=-1, keepdims=True))
        probs.append(e * (1.0 / jnp.sum(e, axis=-1, keepdims=True)))
    return probs


def head_grads(probs, grad_probs, scale):
    rows = grad_probs.shape[0] // HEADS
    grad_scores = []
    for h in range(HEADS):
        gp = grad_probs[h * rows : (h + 1) * rows]
        row_dot = jnp.sum(gp * probs[h], axis=-1, keepdims=True)
        grad_scores.append((probs[h] * (gp - row_dot) * scale).astype(bf16))
    return jnp.concatenate(grad_scores, axis=0)


def stacked_low(probs):
    return jnp.concatenate([p.astype(bf16) for p in probs], axis=0)


def slot_of(position, back, freq):
    return lax.rem(position - back + freq, freq)


def freq_forward_kernel(
    place_ref, own_ref, others_ref, w_ref, gain_ref, q_ref, k_ref, v_ref, o_ref, p_ref, h_ref, hold
):
    step = pl.program_id(0)
    freq, bins_dev, width = others_ref.shape[0] + 1, own_ref.shape[2], own_ref.shape[3]
    bins = freq * bins_dev
    bins_time = hold.shape[2] // pl.num_programs(0)
    scale = (width // HEADS) ** (-0.5)
    x = joined(own_ref, others_ref)
    _, unit = norm_parts(x)
    n = (unit * gain_ref[0:1, :]).astype(bf16)
    q = dot(n, w_ref[0]).astype(bf16)
    k = dot(n, w_ref[1]).astype(bf16)
    v = dot(n, w_ref[2]).astype(bf16)
    probs = head_probs(dot_nt(spread(q, scale), k), None)
    o = own_channels(dot(stacked_low(probs), v), bins)
    for h in range(HEADS):
        p_ref[0, h] = probs[h]
    o = o.astype(bf16)
    hidden = x + dot(o, w_ref[3])
    q_ref[0] = q
    k_ref[0] = k
    v_ref[0] = v
    o_ref[0] = o
    rows = pl.ds(pl.multiple_of(step * bins_time, bins_time), bins_time)
    for f in range(freq):
        part = hidden[f * bins_dev : (f + 1) * bins_dev].reshape(-1, bins_time, width)
        hold[:, slot_of(place_ref[0], f, freq), rows, :] = part

    @pl.when(step == pl.num_programs(0) - 1)
    def _():
        h_ref[...] = hold[...].astype(bf16)


def joined(own_ref, others_ref):
    width = own_ref.shape[-1]
    return jnp.concatenate(
        [own_ref[...].reshape(-1, width), others_ref[...].reshape(-1, width)], axis=0
    ).astype(f32)


def frame_specs(freq, bins_dev, width):
    own = pl.BlockSpec((1, 1, bins_dev, width), lambda i, place: (place[0], i, 0, 0))
    others = pl.BlockSpec((freq - 1, 1, bins_dev, width), lambda i, place: (0, i, 0, 0))
    rows = pl.BlockSpec((1, freq * bins_dev, width), lambda i, place: (i, 0, 0))
    return own, others, rows


def fixed(shape):
    return pl.BlockSpec(shape, lambda i, place: (0,) * len(shape))


def freq_forward(place, features, others, weights, gains, group):
    freq, frames, bins_dev, width = features.shape
    bins = freq * bins_dev
    rows = frames * (bins_dev // group)
    own_spec, others_spec, row_spec = frame_specs(freq, bins_dev, width)
    rowshape = jax.ShapeDtypeStruct((frames, bins, width), bf16)
    whole = (group, freq, rows, width)
    flops = frames * 2 * bins * (4 * width * width + 2 * HEADS * bins * width)
    return pl.pallas_call(
        freq_forward_kernel,
        grid_spec=pltpu.PrefetchScalarGridSpec(
            num_scalar_prefetch=1,
            grid=(frames,),
            in_specs=[own_spec, others_spec, fixed((4, width, width)), fixed(gains.shape)],
            out_specs=[row_spec] * 4
            + [pl.BlockSpec((1, HEADS, bins, bins), lambda i, place: (i, 0, 0, 0)), fixed(whole)],
            scratch_shapes=[pltpu.VMEM(whole, f32)],
        ),
        out_shape=[rowshape] * 4
        + [
            jax.ShapeDtypeStruct((frames, HEADS, bins, bins), f32),
            jax.ShapeDtypeStruct(whole, bf16),
        ],
        compiler_params=pltpu.CompilerParams(vmem_limit_bytes=VMEM_LIMIT),
        cost_estimate=pl.CostEstimate(
            flops=flops, bytes_accessed=8 * 1024 * 1024, transcendentals=frames * HEADS * bins * bins
        ),
        name="freq_forward",
    )(place, features, others, weights, gains)


def freq_backward_kernel(
    place_ref, own_ref, others_ref, q_ref, k_ref, v_ref, o_ref, p_ref, gh_ref, w_ref, gain_ref,
    gown_ref, gothers_ref, kept_ref, sent_ref, dg_ref, hold, total
):
    step = pl.program_id(0)
    freq, bins_dev, width = others_ref.shape[0] + 1, own_ref.shape[2], own_ref.shape[3]
    group = hold.shape[0]
    bins_time = bins_dev // group
    scale = (width // HEADS) ** (-0.5)

    @pl.when(step == 0)
    def _():
        hold[...] = gh_ref[...].astype(f32)
        total[...] = jnp.zeros_like(total)
        dg_ref[...] = jnp.zeros_like(dg_ref)

    grad_hidden = grad_hidden_rows(place_ref, hold, step, freq, bins_time)
    grad_hidden_low = grad_hidden.astype(bf16)
    grad_out = dot_nt(grad_hidden_low, w_ref[3]).astype(bf16)
    out_spread = spread(grad_out, 1.0)
    grad_probs = dot_nt(out_spread, v_ref[0])
    probs = [p_ref[0, h] for h in range(HEADS)]
    g_v = dot_tn(stacked_low(probs), out_spread).astype(bf16)
    grad_scores = head_grads(probs, grad_probs, scale)
    g_q = own_channels(dot(grad_scores, k_ref[0]), freq * bins_dev).astype(bf16)
    g_k = dot_tn(grad_scores, spread(q_ref[0], 1.0)).astype(bf16)
    inverse, unit = norm_parts(joined(own_ref, others_ref))
    gain = gain_ref[0:1, :]
    n = (unit * gain).astype(bf16)
    total[0] += dot_tn(n, g_q)
    total[1] += dot_tn(n, g_k)
    total[2] += dot_tn(n, g_v)
    total[3] += dot_tn(o_ref[0], grad_hidden_low)
    g_n = dot_nt(g_q, w_ref[0]) + dot_nt(g_k, w_ref[1]) + dot_nt(g_v, w_ref[2])
    grad_x = grad_hidden + norm_backward(g_n, inverse, unit, gain)
    grad_x = grad_x.astype(bf16)
    gown_ref[0] = grad_x[:bins_dev]
    gothers_ref[...] = grad_x[bins_dev:].reshape(gothers_ref.shape)
    dg_ref[...] += jnp.sum(g_n * unit, axis=0, keepdims=True)

    @pl.when(step == pl.num_programs(0) - 1)
    def _():
        put_halves(place_ref[1], total, kept_ref, sent_ref)


def put_halves(core, total, kept_ref, sent_ref):
    half = kept_ref.shape[0]
    kept_ref[...] = total[pl.ds(core * half, half)].astype(bf16)
    sent_ref[...] = total[pl.ds((1 - core) * half, half)].astype(bf16)


def grad_hidden_rows(place_ref, hold, step, freq, bins_time):
    width = hold.shape[-1]
    rows = pl.ds(pl.multiple_of(step * bins_time, bins_time), bins_time)
    return jnp.concatenate(
        [hold[:, slot_of(place_ref[0], f, freq), rows, :].reshape(-1, width) for f in range(freq)],
        axis=0,
    )


def freq_backward(place, features, others, q, k, v, o, probs, grad_hidden, weights, gains):
    freq, frames, bins_dev, width = features.shape
    bins = freq * bins_dev
    own_spec, others_spec, row_spec = frame_specs(freq, bins_dev, width)
    flops = frames * 2 * bins * (8 * width * width + 4 * HEADS * bins * width)
    half = (2, width, width)
    return pl.pallas_call(
        freq_backward_kernel,
        grid_spec=pltpu.PrefetchScalarGridSpec(
            num_scalar_prefetch=1,
            grid=(frames,),
            in_specs=[own_spec, others_spec]
            + [row_spec] * 4
            + [
                pl.BlockSpec((1, HEADS, bins, bins), lambda i, place: (i, 0, 0, 0)),
                fixed(grad_hidden.shape),
                fixed((4, width, width)),
                fixed(gains.shape),
            ],
            out_specs=[
                pl.BlockSpec((1, bins_dev, width), lambda i, place: (i, 0, 0)),
                others_spec,
                fixed(half),
                fixed(half),
                fixed((1, width)),
            ],
            scratch_shapes=[
                pltpu.VMEM(grad_hidden.shape, f32),
                pltpu.VMEM((4, width, width), f32),
            ],
        ),
        out_shape=[
            jax.ShapeDtypeStruct((frames, bins_dev, width), bf16),
            jax.ShapeDtypeStruct(others.shape, bf16),
            jax.ShapeDtypeStruct(half, bf16),
            jax.ShapeDtypeStruct(half, bf16),
            jax.ShapeDtypeStruct((1, width), f32),
        ],
        compiler_params=pltpu.CompilerParams(vmem_limit_bytes=VMEM_LIMIT),
        cost_estimate=pl.CostEstimate(
            flops=flops, bytes_accessed=8 * 1024 * 1024, transcendentals=0
        ),
        name="freq_backward",
    )(place, features, others, q, k, v, o, probs, grad_hidden, weights, gains)


def time_kernel(
    bins, own_start, total_frames, place_ref, first_ref, h_hbm, up_hbm, w_hbm, gain_ref,
    gh_hbm, kept_ref, sent_ref, dg_ref,
    h_ref, up_ref, w_ref, gh_ref, total, q_s, k_s, v_s, go_s, o_s, gq_s, gk_s, gv_s, sems
):
    span_rows, width = h_ref.shape
    span = span_rows // bins
    own_rows = gh_ref.shape[0]
    own = own_rows // bins
    scale = (width // HEADS) ** (-0.5)
    gain = gain_ref[1:2, :]
    chunk = own_rows
    while chunk > 256 and chunk % 32 == 0:
        chunk //= 2
    chunks = span_rows // chunk

    w_copy = pltpu.make_async_copy(w_hbm.at[pl.ds(4, 4)], w_ref, sems.at[0])
    h_copy = pltpu.make_async_copy(h_hbm, h_ref, sems.at[1])
    up_copy = pltpu.make_async_copy(up_hbm, up_ref, sems.at[2])
    h_copy.start()
    w_copy.start()
    up_copy.start()
    h_copy.wait()
    w_copy.wait()

    for i in range(chunks):
        rows = pl.ds(i * chunk, chunk)
        _, unit = norm_parts(h_ref[rows, :].astype(f32))
        n = (unit * gain).astype(bf16)
        put(q_s, rows, dot(n, w_ref[0]))
        put(k_s, rows, dot(n, w_ref[1]))
        put(v_s, rows, dot(n, w_ref[2]))
    up_copy.wait()
    for i in range(chunks):
        rows = pl.ds(i * chunk, chunk)
        put(go_s, rows, dot_nt(up_ref[rows, :], w_ref[3]))

    query = lax.broadcasted_iota(jnp.int32, (span, span), 0)
    key = lax.broadcasted_iota(jnp.int32, (span, span), 1)
    distance = key - query
    allowed = (distance >= -(WINDOW // 2)) & (distance < WINDOW // 2)
    if own != span:
        frame = first_ref[0] + key
        allowed = allowed & (frame >= 0) & (frame < total_frames)

    def one_bin(b, carry):
        rows = pl.ds(b, span, stride=bins)
        q = get(q_s, rows).astype(bf16)
        k = get(k_s, rows).astype(bf16)
        v = get(v_s, rows).astype(bf16)
        grad_out = get(go_s, rows).astype(bf16)
        out_spread = spread(grad_out, 1.0)
        scores = dot_nt(spread(q, scale), k)
        grad_probs = dot_nt(out_spread, v)
        probs = head_probs(scores, allowed)
        low = stacked_low(probs)
        grad_scores = head_grads(probs, grad_probs, scale)
        o = own_channels(dot(low, v), span)
        g_q = own_channels(dot(grad_scores, k), span)
        g_k = dot_tn(grad_scores, spread(q, 1.0))
        g_v = dot_tn(low, out_spread)
        put(o_s, rows, o)
        put(gq_s, rows, g_q)
        put(gk_s, rows, g_k)
        put(gv_s, rows, g_v)
        return carry

    lax.fori_loop(0, bins, one_bin, 0, unroll=UNROLL)

    dg_ref[...] = jnp.zeros_like(dg_ref)
    stores = []
    for i in range(own_rows // chunk):
        mine = pl.ds(i * chunk, chunk)
        rows = pl.ds(own_start + i * chunk, chunk)
        g_q = get(gq_s, rows).astype(bf16)
        g_k = get(gk_s, rows).astype(bf16)
        g_v = get(gv_s, rows).astype(bf16)
        g_n = dot_nt(g_q, w_ref[0]) + dot_nt(g_k, w_ref[1]) + dot_nt(g_v, w_ref[2])
        inverse, unit = norm_parts(h_ref[rows, :].astype(f32))
        n = (unit * gain).astype(bf16)
        up = up_ref[rows, :]
        grad_hidden = up.astype(f32) + norm_backward(g_n, inverse, unit, gain)
        gh_ref[mine, :] = grad_hidden.astype(bf16)
        stores.append(pltpu.make_async_copy(gh_ref.at[mine], gh_hbm.at[mine], sems.at[3 + i]))
        stores[-1].start()
        dg_ref[...] += jnp.sum(g_n * unit, axis=0, keepdims=True)
        parts = (dot_tn(n, g_q), dot_tn(n, g_k), dot_tn(n, g_v), dot_tn(get(o_s, rows).astype(bf16), up))
        for m, part in enumerate(parts):
            total[m] = part if i == 0 else total[m] + part
    put_halves(place_ref[1], total, kept_ref, sent_ref)
    for store in stores:
        store.wait()


UNROLL = 4


def time_attention(place, first, hidden, upstream, weights, gains, bins, own_start, own_rows, total):
    span_rows, width = hidden.shape
    vmem = pl.BlockSpec(memory_space=pltpu.VMEM)
    hbm = pl.BlockSpec(memory_space=pltpu.HBM)
    smem = pl.BlockSpec(memory_space=pltpu.SMEM)
    span = span_rows // bins
    flops = 2 * span_rows * (11 * width * width + 6 * HEADS * span * width)
    return pl.pallas_call(
        functools.partial(time_kernel, bins, own_start, total),
        in_specs=[smem, smem, hbm, hbm, hbm, vmem],
        out_specs=[hbm] + [vmem] * 3,
        out_shape=[jax.ShapeDtypeStruct((own_rows, width), bf16)]
        + [jax.ShapeDtypeStruct((2, width, width), bf16)] * 2
        + [jax.ShapeDtypeStruct((1, width), f32)],
        scratch_shapes=[
            pltpu.VMEM((span_rows, width), bf16),
            pltpu.VMEM((span_rows, width), bf16),
            pltpu.VMEM((4, width, width), bf16),
            pltpu.VMEM((own_rows, width), bf16),
            pltpu.VMEM((4, width, width), f32),
        ]
        + [pltpu.VMEM((width // LANES, span_rows, LANES), f32)] * 8
        + [pltpu.SemaphoreType.DMA((16,))],
        compiler_params=pltpu.CompilerParams(vmem_limit_bytes=VMEM_LIMIT),
        cost_estimate=pl.CostEstimate(
            flops=flops,
            bytes_accessed=4 * 1024 * 1024,
            transcendentals=bins * HEADS * span * span,
        ),
        name="time_attention",
    )(place, first, hidden, upstream, weights, gains)


def pair_kernel(fk_ref, fa_ref, tk_ref, ta_ref, out_ref):
    for part, (kept_ref, arrived_ref) in enumerate(((fk_ref, fa_ref), (tk_ref, ta_ref))):
        total = kept_ref[...].astype(f32) + arrived_ref[...].astype(f32)
        rows = out_ref.shape[1] // 2
        out_ref[:, part * rows : (part + 1) * rows] = total.astype(bf16).reshape(
            out_ref.shape[0], rows, out_ref.shape[2]
        )


def pair_sums(freq_kept, freq_arrived, time_kept, time_arrived, peers):
    width = freq_kept.shape[-1]
    rows = 2 * freq_kept.size // (peers * width)
    vmem = pl.BlockSpec(memory_space=pltpu.VMEM)
    return pl.pallas_call(
        pair_kernel,
        in_specs=[vmem] * 4,
        out_specs=vmem,
        out_shape=jax.ShapeDtypeStruct((peers, rows, width), bf16),
        compiler_params=pltpu.CompilerParams(vmem_limit_bytes=VMEM_LIMIT),
        cost_estimate=pl.CostEstimate(
            flops=freq_kept.size, bytes_accessed=2 * 1024 * 1024, transcendentals=0
        ),
        name="pair_sums",
    )(freq_kept, freq_arrived, time_kept, time_arrived)


def group_size(devices, bins_dev):
    best = 1
    for size in range(1, devices + 1):
        if devices % size == 0 and bins_dev % (8 * size) == 0:
            best = size
    return best


def per_device(features, upstream, weights, gains):
    frames_dev, bins_dev, width = features.shape
    tm, freq = lax.axis_size("tm"), lax.axis_size("freq")
    total_frames = frames_dev * tm
    frames = frames_dev // freq
    group = group_size(tm, bins_dev)
    bins_time = bins_dev // group
    group_frames = group * frames_dev
    whole = group == tm
    sides = 0 if whole else -(-WINDOW // group_frames)
    groups = (
        None
        if whole
        else [list(range(g * group, (g + 1) * group)) for g in range(tm // group)]
    )

    def over_tm(blocks):
        return lax.all_to_all(blocks, "tm", 0, 0, tiled=True, axis_index_groups=groups)

    def over_all(blocks):
        if whole:
            flat = blocks.reshape((tm * freq,) + blocks.shape[2:])
            return lax.all_to_all(flat, ("tm", "freq"), 0, 0, tiled=True).reshape(blocks.shape)
        return over_tm(lax.all_to_all(blocks, "freq", 1, 1, tiled=True))

    def with_sides(rows):
        parts = [rows]
        for away in range(1, sides + 1):
            shift = away * group
            before = lax.ppermute(rows, "tm", [(i, i + shift) for i in range(tm - shift)])
            after = lax.ppermute(rows, "tm", [(i + shift, i) for i in range(tm - shift)])
            parts = [before] + parts + [after]
        return jnp.concatenate(parts, axis=0) if sides else rows

    core = lax.axis_index("tm") % 2
    place = jnp.stack([lax.axis_index("freq"), core]).astype(jnp.int32)
    by_target = features.reshape(freq, frames, bins_dev, width)

    def along_freq(block, steps):
        return lax.ppermute(block, "freq", [(i, (i + steps) % freq) for i in range(freq)])

    others = jnp.stack(
        [
            along_freq(lax.dynamic_index_in_dim(by_target, (place[0] + j) % freq, 0, False), j)
            for j in range(1, freq)
        ]
    )
    up_blocks = jnp.swapaxes(upstream.reshape(frames_dev, group, bins_time, width), 0, 1)
    up_rows = over_tm(up_blocks).reshape(-1, width)
    q, k, v, o, probs, hidden_blocks = freq_forward(
        place, by_target, others, weights, gains, group
    )
    hidden_rows = over_all(hidden_blocks).reshape(-1, width)
    own_rows = hidden_rows.shape[0]
    position = lax.axis_index("tm") // group
    first = ((position - sides) * group_frames).astype(jnp.int32).reshape(1)
    grad_rows, time_kept, time_sent, time_dg = time_attention(
        place,
        first,
        with_sides(hidden_rows),
        with_sides(up_rows),
        weights,
        gains,
        bins_time,
        sides * own_rows,
        own_rows,
        total_frames,
    )
    grad_hidden = over_all(grad_rows.reshape(hidden_blocks.shape))

    pairs = [(i, i ^ 1) for i in range(tm)]
    same = [
        [t * freq + f for t in range(c, tm, 2) for f in range(freq)] for c in range(2)
    ]
    peers = len(same[0])

    def over_same(blocks):
        return lax.all_to_all(
            blocks, ("tm", "freq"), 0, 0, tiled=True, axis_index_groups=same
        )

    time_arrived = lax.ppermute(time_sent, "tm", pairs)
    grad_own, grad_others, freq_kept, freq_sent, freq_dg = freq_backward(
        place, by_target, others, q, k, v, o, probs, grad_hidden, weights, gains
    )
    freq_arrived = lax.ppermute(freq_sent, "tm", pairs)
    arrived = over_same(pair_sums(freq_kept, freq_arrived, time_kept, time_arrived, peers))
    returned = [grad_own] + [along_freq(grad_others[j - 1], -j) for j in range(1, freq)]
    returned, arrived = lax.optimization_barrier((returned, arrived))
    grad_input = jnp.roll(jnp.stack(returned), place[0], axis=0).reshape(features.shape)

    inv_root = (total_frames * bins_dev * freq) ** (-0.5)

    def split(rows):
        high = rows.astype(bf16)
        return [high, (rows - high.astype(f32)).astype(bf16)]

    summed = jnp.sum(arrived.astype(f32), axis=0) * inv_root
    count = summed.shape[0]
    gain_rows = jnp.concatenate([freq_dg, time_dg], axis=0) * inv_root
    sent = jnp.concatenate([summed.astype(bf16)] + split(gain_rows), axis=0)
    gathered = over_same(jnp.broadcast_to(sent[None], (peers,) + sent.shape))
    gain_sum = jnp.sum(gathered[:, count:].astype(f32), axis=0)
    gain_sum = gain_sum[:2] + gain_sum[2:]
    mine = gathered[:, :count].reshape(-1, width)
    theirs = lax.ppermute(jnp.concatenate([mine] + split(gain_sum), axis=0), "tm", pairs)
    gain_high_low = split(gain_sum)
    other_gain = theirs[-4:].astype(f32)
    gain_grads = sum(g.astype(f32) for g in gain_high_low) + other_gain[:2] + other_gain[2:]
    theirs = theirs[:-4]
    first_core = core == 0
    halves = jnp.stack(
        [jnp.where(first_core, mine, theirs), jnp.where(first_core, theirs, mine)]
    )
    weight_grads = (
        halves.reshape(2, peers, 2, -1, width).transpose(2, 0, 1, 3, 4).astype(f32)
    ).reshape(8, width, width)
    return (grad_input, weight_grads, gain_grads)


def solution(mesh):
    return jax.shard_map(
        per_device,
        mesh=mesh,
        in_specs=(P("tm", "freq", None), P("tm", "freq", None), P(), P()),
        out_specs=(P("tm", "freq", None), P(), P()),
        check_vma=False,
    )
```

```python
import functools

import jax
import jax.numpy as jnp
from jax import lax
from jax.experimental import pallas as pl
from jax.experimental.pallas import tpu as pltpu
from jax.sharding import PartitionSpec as P

HEADS = 4
WINDOW = 128

epsilon = 1e-06
masked_score = -1e30

f32 = jnp.float32
bf16 = jnp.bfloat16
LANES = 128
MIB = 1024 * 1024
VMEM_LIMIT = 24 * MIB

CONTRACT_LAST = (((1,), (1,)), ((), ()))
CONTRACT_FIRST = (((0,), (0,)), ((), ()))


def dot(left, right):
    return jnp.dot(left, right, preferred_element_type=f32)


def dot_nt(left, right):
    return lax.dot_general(left, right, CONTRACT_LAST, preferred_element_type=f32)


def dot_tn(left, right):
    return lax.dot_general(left, right, CONTRACT_FIRST, preferred_element_type=f32)


def put(ref, rows, value):
    for c in range(ref.shape[0]):
        ref[c, rows, :] = value[:, c * LANES : (c + 1) * LANES]


def get(ref, rows):
    return jnp.concatenate([ref[c, rows, :] for c in range(ref.shape[0])], axis=1)


def norm_parts(widened):
    inverse = lax.rsqrt(jnp.mean(widened * widened, axis=-1, keepdims=True) + epsilon)
    return inverse, widened * inverse


def norm_backward(incoming, inverse, unit_rows, gain):
    scaled = incoming * gain
    return inverse * (scaled - unit_rows * jnp.mean(scaled * unit_rows, axis=-1, keepdims=True))


def spread(rows, factor):
    width = rows.shape[-1]
    owner = lax.broadcasted_iota(jnp.int32, (1, width), 1) // (width // HEADS)
    return jnp.concatenate(
        [rows * jnp.where(owner == h, factor, 0.0).astype(rows.dtype) for h in range(HEADS)], axis=0
    )


def own_channels(stacked, rows):
    width = stacked.shape[-1]
    owner = lax.broadcasted_iota(jnp.int32, (1, width), 1) // (width // HEADS)
    result = stacked[:rows]
    for h in range(1, HEADS):
        result = jnp.where(owner == h, stacked[h * rows : (h + 1) * rows], result)
    return result


def head_probs(scores, allowed):
    rows = scores.shape[0] // HEADS
    probs = []
    for h in range(HEADS):
        s = scores[h * rows : (h + 1) * rows]
        if allowed is not None:
            s = jnp.where(allowed, s, masked_score)
        e = jnp.exp(s - jnp.max(s, axis=-1, keepdims=True))
        probs.append(e * (1.0 / jnp.sum(e, axis=-1, keepdims=True)))
    return probs


def head_grads(probs, grad_probs, scale):
    rows = grad_probs.shape[0] // HEADS
    grad_scores = []
    for h in range(HEADS):
        gp = grad_probs[h * rows : (h + 1) * rows]
        row_dot = jnp.sum(gp * probs[h], axis=-1, keepdims=True)
        grad_scores.append((probs[h] * (gp - row_dot) * scale).astype(bf16))
    return jnp.concatenate(grad_scores, axis=0)


def stacked_low(probs):
    return jnp.concatenate([p.astype(bf16) for p in probs], axis=0)


def slot_of(position, back, freq):
    return lax.rem(position - back + freq, freq)


def freq_forward_kernel(
    place_ref, own_ref, others_ref, w_ref, gain_ref, q_ref, k_ref, v_ref, o_ref, p_ref, h_hbm,
    hold, low, sem
):
    step = pl.program_id(0)
    freq, bins_dev, width = others_ref.shape[0] + 1, own_ref.shape[2], own_ref.shape[3]
    bins_time = hold.shape[2] // pl.num_programs(0)
    x = joined(own_ref, others_ref)
    _, unit = norm_parts(x)
    n = (unit * gain_ref[0:1, :]).astype(bf16)
    scale = (width // HEADS) ** (-0.5)
    q = dot(n, w_ref[0]).astype(bf16)
    k = dot(n, w_ref[1]).astype(bf16)
    v = dot(n, w_ref[2]).astype(bf16)
    probs = head_probs(dot_nt(spread(q, scale), k), None)
    o = own_channels(dot(stacked_low(probs), v), n.shape[0]).astype(bf16)
    hidden = x + dot(o, w_ref[3])
    q_ref[0] = q
    k_ref[0] = k
    v_ref[0] = v
    o_ref[0] = o
    for h in range(HEADS):
        p_ref[0, h] = probs[h]
    rows = pl.ds(pl.multiple_of(step * bins_time, bins_time), bins_time)
    for f in range(freq):
        part = hidden[f * bins_dev : (f + 1) * bins_dev].reshape(-1, bins_time, width)
        hold[:, slot_of(place_ref[0], f, freq), rows, :] = part

    @pl.when(step == pl.num_programs(0) - 1)
    def _():
        low[...] = hold[...].astype(bf16)
        copy = pltpu.make_async_copy(low, h_hbm, sem)
        copy.start()
        copy.wait()


def joined(own_ref, others_ref):
    width = own_ref.shape[-1]
    return jnp.concatenate(
        [own_ref[...].reshape(-1, width), others_ref[...].reshape(-1, width)], axis=0
    ).astype(f32)


def near(array):
    return pltpu.with_memory_space_constraint(array, pltpu.VMEM)


def far(array):
    return pltpu.with_memory_space_constraint(array, pltpu.HBM)


def frame_specs(freq, bins_dev, width):
    own = pl.BlockSpec((1, 1, bins_dev, width), lambda i, place: (place[0], i, 0, 0))
    others = pl.BlockSpec((freq - 1, 1, bins_dev, width), lambda i, place: (0, i, 0, 0))
    rows = pl.BlockSpec((1, freq * bins_dev, width), lambda i, place: (i, 0, 0))
    return own, others, rows


def fixed(shape):
    return pl.BlockSpec(shape, lambda i, place: (0,) * len(shape))


def freq_forward(place, features, others, weights, gains, group):
    freq, frames, bins_dev, width = features.shape
    bins = freq * bins_dev
    rows = frames * (bins_dev // group)
    own_spec, others_spec, row_spec = frame_specs(freq, bins_dev, width)
    rowshape = pltpu.HBM((frames, bins, width), bf16)
    whole = (group, freq, rows, width)
    flops = frames * 2 * bins * (4 * width * width + 2 * HEADS * bins * width)
    return pl.pallas_call(
        freq_forward_kernel,
        grid_spec=pltpu.PrefetchScalarGridSpec(
            num_scalar_prefetch=1,
            grid=(frames,),
            in_specs=[own_spec, others_spec, fixed(weights.shape), fixed(gains.shape)],
            out_specs=[row_spec] * 4
            + [
                pl.BlockSpec((1, HEADS, bins, bins), lambda i, place: (i, 0, 0, 0)),
                pl.BlockSpec(memory_space=pltpu.HBM),
            ],
            scratch_shapes=[
                pltpu.VMEM(whole, f32),
                pltpu.VMEM(whole, bf16),
                pltpu.SemaphoreType.DMA,
            ],
        ),
        out_shape=[rowshape] * 4
        + [pltpu.HBM((frames, HEADS, bins, bins), f32), pltpu.HBM(whole, bf16)],
        compiler_params=pltpu.CompilerParams(vmem_limit_bytes=VMEM_LIMIT),
        cost_estimate=pl.CostEstimate(
            flops=flops * FAKE,
            bytes_accessed=2 * 1024 * 1024,
            transcendentals=frames * HEADS * bins * bins,
        ),
        name="freq_forward",
    )(place, features, near(others), near(weights), gains)


FAKE = 1


def freq_backward_kernel(
    place_ref, own_ref, others_ref, q_ref, k_ref, v_ref, o_ref, p_ref, gh_ref, w_ref, gain_ref,
    gown_ref, gothers_ref, kept_ref, sent_ref, dg_ref, hold, total
):
    step = pl.program_id(0)
    freq, bins_dev, width = others_ref.shape[0] + 1, own_ref.shape[2], own_ref.shape[3]
    group = hold.shape[0]
    bins_time = bins_dev // group
    scale = (width // HEADS) ** (-0.5)

    @pl.when(step == 0)
    def _():
        hold[...] = gh_ref[...].astype(f32)
        total[...] = jnp.zeros_like(total)
        dg_ref[...] = jnp.zeros_like(dg_ref)

    grad_hidden = grad_hidden_rows(place_ref, hold, step, freq, bins_time)
    grad_hidden_low = grad_hidden.astype(bf16)
    grad_out = dot_nt(grad_hidden_low, w_ref[3]).astype(bf16)
    out_spread = spread(grad_out, 1.0)
    grad_probs = dot_nt(out_spread, v_ref[0])
    probs = [p_ref[0, h] for h in range(HEADS)]
    g_v = dot_tn(stacked_low(probs), out_spread).astype(bf16)
    grad_scores = head_grads(probs, grad_probs, scale)
    g_q = own_channels(dot(grad_scores, k_ref[0]), freq * bins_dev).astype(bf16)
    g_k = dot_tn(grad_scores, spread(q_ref[0], 1.0)).astype(bf16)
    inverse, unit = norm_parts(joined(own_ref, others_ref))
    gain = gain_ref[0:1, :]
    n = (unit * gain).astype(bf16)
    total[0] += dot_tn(n, g_q)
    total[1] += dot_tn(n, g_k)
    total[2] += dot_tn(n, g_v)
    total[3] += dot_tn(o_ref[0], grad_hidden_low)
    g_n = dot_nt(g_q, w_ref[0]) + dot_nt(g_k, w_ref[1]) + dot_nt(g_v, w_ref[2])
    grad_x = grad_hidden + norm_backward(g_n, inverse, unit, gain)
    grad_x = grad_x.astype(bf16)
    gown_ref[0] = grad_x[:bins_dev]
    gothers_ref[...] = grad_x[bins_dev:].reshape(gothers_ref.shape)
    dg_ref[...] += jnp.sum(g_n * unit, axis=0, keepdims=True)

    @pl.when(step == pl.num_programs(0) - 1)
    def _():
        put_halves(place_ref[1], total, kept_ref, sent_ref)


def put_halves(core, total, kept_ref, sent_ref):
    half = kept_ref.shape[0]
    kept_ref[...] = total[pl.ds(core * half, half)].astype(bf16)
    sent_ref[...] = total[pl.ds((1 - core) * half, half)].astype(bf16)


def grad_hidden_rows(place_ref, hold, step, freq, bins_time):
    width = hold.shape[-1]
    rows = pl.ds(pl.multiple_of(step * bins_time, bins_time), bins_time)
    return jnp.concatenate(
        [hold[:, slot_of(place_ref[0], f, freq), rows, :].reshape(-1, width) for f in range(freq)],
        axis=0,
    )


def freq_backward(place, features, others, q, k, v, o, probs, grad_hidden, weights, gains):
    freq, frames, bins_dev, width = features.shape
    bins = freq * bins_dev
    own_spec, others_spec, row_spec = frame_specs(freq, bins_dev, width)
    flops = frames * 2 * bins * (8 * width * width + 4 * HEADS * bins * width)
    half = (2, width, width)
    return pl.pallas_call(
        freq_backward_kernel,
        grid_spec=pltpu.PrefetchScalarGridSpec(
            num_scalar_prefetch=1,
            grid=(frames,),
            in_specs=[own_spec, others_spec]
            + [row_spec] * 4
            + [
                pl.BlockSpec((1, HEADS, bins, bins), lambda i, place: (i, 0, 0, 0)),
                fixed(grad_hidden.shape),
                fixed((4, width, width)),
                fixed(gains.shape),
            ],
            out_specs=[
                pl.BlockSpec((1, bins_dev, width), lambda i, place: (i, 0, 0)),
                others_spec,
                fixed(half),
                fixed(half),
                fixed((1, width)),
            ],
            scratch_shapes=[
                pltpu.VMEM(grad_hidden.shape, f32),
                pltpu.VMEM((4, width, width), f32),
            ],
        ),
        out_shape=[
            pltpu.HBM((frames, bins_dev, width), bf16),
            pltpu.HBM(others.shape, bf16),
            jax.ShapeDtypeStruct(half, bf16),
            jax.ShapeDtypeStruct(half, bf16),
            jax.ShapeDtypeStruct((1, width), f32),
        ],
        compiler_params=pltpu.CompilerParams(vmem_limit_bytes=VMEM_LIMIT),
        cost_estimate=pl.CostEstimate(
            flops=flops, bytes_accessed=8 * 1024 * 1024, transcendentals=0
        ),
        name="freq_backward",
    )(
        place, features, *map(far, (others, q, k, v, o, probs)), near(grad_hidden),
        near(weights), gains,
    )


def time_kernel(
    bins, own_start, total_frames, place_ref, first_ref, h_ref, up_ref, w_ref, gain_ref,
    gh_hbm, kept_ref, sent_ref, dg_ref,
    gh_ref, total, q_s, k_s, v_s, go_s, o_s, gq_s, gk_s, gv_s, sems
):
    span_rows, width = h_ref.shape
    span = span_rows // bins
    own_rows = gh_ref.shape[0]
    own = own_rows // bins
    scale = (width // HEADS) ** (-0.5)
    gain = gain_ref[1:2, :]
    chunk = own_rows
    while chunk > 256 and chunk % 32 == 0:
        chunk //= 2
    chunks = span_rows // chunk

    for i in range(chunks):
        rows = pl.ds(i * chunk, chunk)
        _, unit = norm_parts(h_ref[rows, :].astype(f32))
        n = (unit * gain).astype(bf16)
        put(q_s, rows, dot(n, w_ref[0]))
        put(k_s, rows, dot(n, w_ref[1]))
        put(v_s, rows, dot(n, w_ref[2]))
    for i in range(chunks):
        rows = pl.ds(i * chunk, chunk)
        put(go_s, rows, dot_nt(up_ref[rows, :], w_ref[3]))

    query = lax.broadcasted_iota(jnp.int32, (span, span), 0)
    key = lax.broadcasted_iota(jnp.int32, (span, span), 1)
    distance = key - query
    allowed = (distance >= -(WINDOW // 2)) & (distance < WINDOW // 2)
    if own != span:
        frame = first_ref[0] + key
        allowed = allowed & (frame >= 0) & (frame < total_frames)

    def one_bin(b, carry):
        rows = pl.ds(b, span, stride=bins)
        q = get(q_s, rows).astype(bf16)
        k = get(k_s, rows).astype(bf16)
        v = get(v_s, rows).astype(bf16)
        grad_out = get(go_s, rows).astype(bf16)
        out_spread = spread(grad_out, 1.0)
        scores = dot_nt(spread(q, scale), k)
        grad_probs = dot_nt(out_spread, v)
        probs = head_probs(scores, allowed)
        low = stacked_low(probs)
        grad_scores = head_grads(probs, grad_probs, scale)
        o = own_channels(dot(low, v), span)
        g_q = own_channels(dot(grad_scores, k), span)
        g_k = dot_tn(grad_scores, spread(q, 1.0))
        g_v = dot_tn(low, out_spread)
        put(o_s, rows, o)
        put(gq_s, rows, g_q)
        put(gk_s, rows, g_k)
        put(gv_s, rows, g_v)
        return carry

    lax.fori_loop(0, bins, one_bin, 0, unroll=UNROLL)

    dg_ref[...] = jnp.zeros_like(dg_ref)
    stores = []
    for i in range(own_rows // chunk):
        mine = pl.ds(i * chunk, chunk)
        rows = pl.ds(own_start + i * chunk, chunk)
        g_q = get(gq_s, rows).astype(bf16)
        g_k = get(gk_s, rows).astype(bf16)
        g_v = get(gv_s, rows).astype(bf16)
        g_n = dot_nt(g_q, w_ref[0]) + dot_nt(g_k, w_ref[1]) + dot_nt(g_v, w_ref[2])
        inverse, unit = norm_parts(h_ref[rows, :].astype(f32))
        n = (unit * gain).astype(bf16)
        up = up_ref[rows, :]
        grad_hidden = up.astype(f32) + norm_backward(g_n, inverse, unit, gain)
        gh_ref[mine, :] = grad_hidden.astype(bf16)
        stores.append(pltpu.make_async_copy(gh_ref.at[mine], gh_hbm.at[mine], sems.at[3 + i]))
        stores[-1].start()
        dg_ref[...] += jnp.sum(g_n * unit, axis=0, keepdims=True)
        parts = (dot_tn(n, g_q), dot_tn(n, g_k), dot_tn(n, g_v), dot_tn(get(o_s, rows).astype(bf16), up))
        for m, part in enumerate(parts):
            total[m] = part if i == 0 else total[m] + part
    put_halves(place_ref[1], total, kept_ref, sent_ref)
    for store in stores:
        store.wait()


UNROLL = 4


def time_attention(place, first, hidden, upstream, weights, gains, bins, own_start, own_rows, total):
    span_rows, width = hidden.shape
    vmem = pl.BlockSpec(memory_space=pltpu.VMEM)
    hbm = pl.BlockSpec(memory_space=pltpu.HBM)
    smem = pl.BlockSpec(memory_space=pltpu.SMEM)
    span = span_rows // bins
    flops = 2 * span_rows * (11 * width * width + 6 * HEADS * span * width)
    return pl.pallas_call(
        functools.partial(time_kernel, bins, own_start, total),
        in_specs=[smem, smem, vmem, vmem, vmem, vmem],
        out_specs=[hbm] + [vmem] * 3,
        out_shape=[pltpu.HBM((own_rows, width), bf16)]
        + [jax.ShapeDtypeStruct((2, width, width), bf16)] * 2
        + [jax.ShapeDtypeStruct((1, width), f32)],
        scratch_shapes=[
            pltpu.VMEM((own_rows, width), bf16),
            pltpu.VMEM((4, width, width), f32),
        ]
        + [pltpu.VMEM((width // LANES, span_rows, LANES), f32)] * 8
        + [pltpu.SemaphoreType.DMA((16,))],
        compiler_params=pltpu.CompilerParams(vmem_limit_bytes=VMEM_LIMIT),
        cost_estimate=pl.CostEstimate(
            flops=flops,
            bytes_accessed=4 * 1024 * 1024,
            transcendentals=bins * HEADS * span * span,
        ),
        name="time_attention",
    )(place, first, near(hidden), near(upstream), near(weights), gains)


def pair_kernel(kept_ref, arrived_ref, out_ref):
    out_ref[...] = (kept_ref[...].astype(f32) + arrived_ref[...].astype(f32)).astype(bf16)


def pair_sum(kept, arrived):
    vmem = pl.BlockSpec(memory_space=pltpu.VMEM)
    return pl.pallas_call(
        pair_kernel,
        in_specs=[vmem] * 2,
        out_specs=vmem,
        out_shape=pltpu.HBM(kept.shape, bf16),
        compiler_params=pltpu.CompilerParams(vmem_limit_bytes=VMEM_LIMIT),
        cost_estimate=pl.CostEstimate(
            flops=kept.size, bytes_accessed=6 * kept.size, transcendentals=0
        ),
        name="pair_sum",
    )(kept, arrived)


def group_size(devices, bins_dev):
    best = 1
    for size in range(1, devices + 1):
        if devices % size == 0 and bins_dev % (8 * size) == 0:
            best = size
    return best


def per_device(features, upstream, weights, gains):
    frames_dev, bins_dev, width = features.shape
    tm, freq = lax.axis_size("tm"), lax.axis_size("freq")
    total_frames = frames_dev * tm
    frames = frames_dev // freq
    group = group_size(tm, bins_dev)
    bins_time = bins_dev // group
    group_frames = group * frames_dev
    whole = group == tm
    sides = 0 if whole else -(-WINDOW // group_frames)
    groups = (
        None
        if whole
        else [list(range(g * group, (g + 1) * group)) for g in range(tm // group)]
    )

    def over_tm(blocks):
        return lax.all_to_all(blocks, "tm", 0, 0, tiled=True, axis_index_groups=groups)

    def over_all(blocks):
        if whole:
            flat = blocks.reshape((tm * freq,) + blocks.shape[2:])
            return lax.all_to_all(flat, ("tm", "freq"), 0, 0, tiled=True).reshape(blocks.shape)
        return over_tm(lax.all_to_all(blocks, "freq", 1, 1, tiled=True))

    def with_sides(rows):
        parts = [rows]
        for away in range(1, sides + 1):
            shift = away * group
            before = lax.ppermute(rows, "tm", [(i, i + shift) for i in range(tm - shift)])
            after = lax.ppermute(rows, "tm", [(i + shift, i) for i in range(tm - shift)])
            parts = [before] + parts + [after]
        return jnp.concatenate(parts, axis=0) if sides else rows

    core = lax.axis_index("tm") % 2
    place = jnp.stack([lax.axis_index("freq"), core]).astype(jnp.int32)
    by_target = features.reshape(freq, frames, bins_dev, width)

    def along_freq(block, steps):
        return lax.ppermute(block, "freq", [(i, (i + steps) % freq) for i in range(freq)])

    others = jnp.stack(
        [
            along_freq(lax.dynamic_index_in_dim(by_target, (place[0] + j) % freq, 0, False), j)
            for j in range(1, freq)
        ]
    )
    up_blocks = jnp.swapaxes(upstream.reshape(frames_dev, group, bins_time, width), 0, 1)
    up_rows = over_tm(up_blocks).reshape(-1, width)
    freq_w = weights[:4]
    q, k, v, o, probs, hidden_blocks = freq_forward(place, by_target, others, freq_w, gains, group)
    time_w, hidden_blocks = lax.optimization_barrier((weights, hidden_blocks))
    time_w = time_w[4:]
    hidden_rows = over_all(hidden_blocks).reshape(-1, width)
    own_rows = hidden_rows.shape[0]
    position = lax.axis_index("tm") // group
    first = ((position - sides) * group_frames).astype(jnp.int32).reshape(1)
    grad_rows, time_kept, time_sent, time_dg = time_attention(
        place,
        first,
        with_sides(hidden_rows),
        with_sides(up_rows),
        time_w,
        gains,
        bins_time,
        sides * own_rows,
        own_rows,
        total_frames,
    )
    grad_hidden = over_all(grad_rows.reshape(hidden_blocks.shape))

    pairs = [(i, i ^ 1) for i in range(tm)]
    same = [
        [t * freq + f for t in range(c, tm, 2) for f in range(freq)] for c in range(2)
    ]
    peers = len(same[0])

    def scattered(partial):
        bits = [("tm", k) for k in reversed(range(1, tm.bit_length() - 1))]
        bits += [("freq", k) for k in reversed(range(freq.bit_length() - 1))]
        partial = partial.reshape((2,) * len(bits) + (-1, width))
        order = sorted(range(len(bits)), key=lambda i: (bits[i][1] > 1, bits[i][0] != "tm", bits[i][1]))
        left = list(range(len(bits)))
        for i in order:
            axis, k = bits[i]
            place_in = left.index(i)
            left.remove(i)
            mine = (lax.axis_index(axis) >> k) & 1
            devices = range(lax.axis_size(axis))
            sent = lax.dynamic_index_in_dim(partial, 1 - mine, place_in, False)
            kept = lax.dynamic_index_in_dim(partial, mine, place_in, False)
            came = lax.ppermute(sent, axis, [(d, d ^ (1 << k)) for d in devices])
            partial = (kept.astype(f32) + came.astype(f32)).astype(bf16)
        return partial

    def over_same(blocks):
        return lax.all_to_all(
            blocks, ("tm", "freq"), 0, 0, tiled=True, axis_index_groups=same
        )

    time_arrived = lax.ppermute(time_sent, "tm", pairs)
    time_block = scattered((time_kept.astype(f32) + time_arrived.astype(f32)).astype(bf16))
    grad_own, grad_others, freq_kept, freq_sent, freq_dg = freq_backward(
        place, by_target, others, q, k, v, o, probs, grad_hidden, freq_w, gains
    )
    freq_arrived = lax.ppermute(freq_sent, "tm", pairs)
    arrived = over_same(pair_sum(freq_kept, freq_arrived).reshape(peers, -1, width))
    returned = [grad_own] + [along_freq(grad_others[j - 1], -j) for j in range(1, freq)]
    returned, arrived = lax.optimization_barrier((returned, arrived))
    grad_input = jnp.roll(jnp.stack(returned), place[0], axis=0).reshape(features.shape)

    inv_root = (total_frames * bins_dev * freq) ** (-0.5)

    def split(rows):
        high = rows.astype(bf16)
        return [high, (rows - high.astype(f32)).astype(bf16)]

    summed = jnp.sum(arrived.astype(f32), axis=0) * inv_root
    summed = jnp.concatenate([summed, time_block.astype(f32) * inv_root], axis=0)
    count = summed.shape[0]
    gain_rows = jnp.concatenate([freq_dg, time_dg], axis=0) * inv_root
    sent = jnp.concatenate([summed.astype(bf16)] + split(gain_rows), axis=0)
    gathered = over_same(jnp.broadcast_to(sent[None], (peers,) + sent.shape))
    gain_sum = jnp.sum(gathered[:, count:].astype(f32), axis=0)
    gain_sum = gain_sum[:2] + gain_sum[2:]
    mine = jnp.concatenate(
        [gathered[:, : count // 2].reshape(-1, width), gathered[:, count // 2 : count].reshape(-1, width)],
        axis=0,
    )
    theirs = lax.ppermute(jnp.concatenate([mine] + split(gain_sum), axis=0), "tm", pairs)
    gain_high_low = split(gain_sum)
    other_gain = theirs[-4:].astype(f32)
    gain_grads = sum(g.astype(f32) for g in gain_high_low) + other_gain[:2] + other_gain[2:]
    theirs = theirs[:-4]
    first_core = core == 0
    first_half = jnp.where(first_core, mine, theirs).reshape(2, 2, width, width)
    second_half = jnp.where(first_core, theirs, mine).reshape(2, 2, width, width)
    weight_grads = jnp.concatenate(
        [first_half[0], second_half[0], first_half[1], second_half[1]], axis=0
    ).astype(f32)
    return (grad_input, weight_grads, gain_grads)


def solution(mesh):
    return jax.shard_map(
        per_device,
        mesh=mesh,
        in_specs=(P("tm", "freq", None), P("tm", "freq", None), P(), P()),
        out_specs=(P("tm", "freq", None), P(), P()),
        check_vma=False,
    )
```

```python
import functools

import jax
import jax.numpy as jnp
from jax import lax
from jax.experimental import pallas as pl
from jax.experimental.pallas import tpu as pltpu
from jax.sharding import PartitionSpec as P

HEADS = 4
WINDOW = 128

epsilon = 1e-06
masked_score = -1e30

f32 = jnp.float32
bf16 = jnp.bfloat16
LANES = 128
MIB = 1024 * 1024
VMEM_LIMIT = 24 * MIB
FORWARD_WEIGHT = 40

CONTRACT_LAST = (((1,), (1,)), ((), ()))
CONTRACT_FIRST = (((0,), (0,)), ((), ()))


def dot(left, right):
    return jnp.dot(left, right, preferred_element_type=f32)


def dot_nt(left, right):
    return lax.dot_general(left, right, CONTRACT_LAST, preferred_element_type=f32)


def dot_tn(left, right):
    return lax.dot_general(left, right, CONTRACT_FIRST, preferred_element_type=f32)


def put(ref, rows, value):
    for c in range(ref.shape[0]):
        ref[c, rows, :] = value[:, c * LANES : (c + 1) * LANES]


def get(ref, rows):
    return jnp.concatenate([ref[c, rows, :] for c in range(ref.shape[0])], axis=1)


def norm_parts(widened):
    inverse = lax.rsqrt(jnp.mean(widened * widened, axis=-1, keepdims=True) + epsilon)
    return inverse, widened * inverse


def norm_backward(incoming, inverse, unit_rows, gain):
    scaled = incoming * gain
    return inverse * (scaled - unit_rows * jnp.mean(scaled * unit_rows, axis=-1, keepdims=True))


def spread(rows, factor):
    width = rows.shape[-1]
    owner = lax.broadcasted_iota(jnp.int32, (1, width), 1) // (width // HEADS)
    return jnp.concatenate(
        [rows * jnp.where(owner == h, factor, 0.0).astype(rows.dtype) for h in range(HEADS)], axis=0
    )


def own_channels(stacked, rows):
    width = stacked.shape[-1]
    owner = lax.broadcasted_iota(jnp.int32, (1, width), 1) // (width // HEADS)
    result = stacked[:rows]
    for h in range(1, HEADS):
        result = jnp.where(owner == h, stacked[h * rows : (h + 1) * rows], result)
    return result


def head_probs(scores, allowed):
    rows = scores.shape[0] // HEADS
    probs = []
    for h in range(HEADS):
        s = scores[h * rows : (h + 1) * rows]
        if allowed is not None:
            s = jnp.where(allowed, s, masked_score)
        e = jnp.exp(s - jnp.max(s, axis=-1, keepdims=True))
        probs.append(e * (1.0 / jnp.sum(e, axis=-1, keepdims=True)))
    return probs


def head_grads(probs, grad_probs, scale):
    rows = grad_probs.shape[0] // HEADS
    grad_scores = []
    for h in range(HEADS):
        gp = grad_probs[h * rows : (h + 1) * rows]
        row_dot = jnp.sum(gp * probs[h], axis=-1, keepdims=True)
        grad_scores.append((probs[h] * (gp - row_dot) * scale).astype(bf16))
    return jnp.concatenate(grad_scores, axis=0)


def stacked_low(probs):
    return jnp.concatenate([p.astype(bf16) for p in probs], axis=0)


def slot_of(position, back, freq):
    return lax.rem(position - back + freq, freq)


def freq_forward_kernel(
    place_ref, own_ref, others_ref, w_ref, gain_ref, q_ref, k_ref, v_ref, o_ref, p_ref, h_hbm,
    hold, low, sem
):
    step = pl.program_id(0)
    freq, bins_dev, width = others_ref.shape[0] + 1, own_ref.shape[2], own_ref.shape[3]
    bins_time = hold.shape[2] // pl.num_programs(0)
    x = joined(own_ref, others_ref)
    _, unit = norm_parts(x)
    n = (unit * gain_ref[0:1, :]).astype(bf16)
    scale = (width // HEADS) ** (-0.5)
    q = dot(n, w_ref[0]).astype(bf16)
    k = dot(n, w_ref[1]).astype(bf16)
    v = dot(n, w_ref[2]).astype(bf16)
    probs = head_probs(dot_nt(spread(q, scale), k), None)
    o = own_channels(dot(stacked_low(probs), v), n.shape[0]).astype(bf16)
    hidden = x + dot(o, w_ref[3])
    q_ref[0] = q
    k_ref[0] = k
    v_ref[0] = v
    o_ref[0] = o
    for h in range(HEADS):
        p_ref[0, h] = probs[h]
    rows = pl.ds(pl.multiple_of(step * bins_time, bins_time), bins_time)
    for f in range(freq):
        part = hidden[f * bins_dev : (f + 1) * bins_dev].reshape(-1, bins_time, width)
        hold[:, slot_of(place_ref[0], f, freq), rows, :] = part

    @pl.when(step == pl.num_programs(0) - 1)
    def _():
        low[...] = hold[...].astype(bf16)
        copy = pltpu.make_async_copy(low, h_hbm, sem)
        copy.start()
        copy.wait()


def joined(own_ref, others_ref):
    width = own_ref.shape[-1]
    return jnp.concatenate(
        [own_ref[...].reshape(-1, width), others_ref[...].reshape(-1, width)], axis=0
    ).astype(f32)


def near(array):
    return pltpu.with_memory_space_constraint(array, pltpu.VMEM)


def far(array):
    return pltpu.with_memory_space_constraint(array, pltpu.HBM)


def frame_specs(freq, bins_dev, width):
    own = pl.BlockSpec((1, 1, bins_dev, width), lambda i, place: (place[0], i, 0, 0))
    others = pl.BlockSpec((freq - 1, 1, bins_dev, width), lambda i, place: (0, i, 0, 0))
    rows = pl.BlockSpec((1, freq * bins_dev, width), lambda i, place: (i, 0, 0))
    return own, others, rows


def fixed(shape):
    return pl.BlockSpec(shape, lambda i, place: (0,) * len(shape))


def freq_forward(place, features, others, weights, gains, group):
    freq, frames, bins_dev, width = features.shape
    bins = freq * bins_dev
    rows = frames * (bins_dev // group)
    own_spec, others_spec, row_spec = frame_specs(freq, bins_dev, width)
    rowshape = pltpu.HBM((frames, bins, width), bf16)
    whole = (group, freq, rows, width)
    flops = frames * 2 * bins * (4 * width * width + 2 * HEADS * bins * width)
    return pl.pallas_call(
        freq_forward_kernel,
        grid_spec=pltpu.PrefetchScalarGridSpec(
            num_scalar_prefetch=1,
            grid=(frames,),
            in_specs=[own_spec, others_spec, fixed(weights.shape), fixed(gains.shape)],
            out_specs=[row_spec] * 4
            + [
                pl.BlockSpec((1, HEADS, bins, bins), lambda i, place: (i, 0, 0, 0)),
                pl.BlockSpec(memory_space=pltpu.HBM),
            ],
            scratch_shapes=[
                pltpu.VMEM(whole, f32),
                pltpu.VMEM(whole, bf16),
                pltpu.SemaphoreType.DMA,
            ],
        ),
        out_shape=[rowshape] * 4
        + [pltpu.HBM((frames, HEADS, bins, bins), f32), pltpu.HBM(whole, bf16)],
        compiler_params=pltpu.CompilerParams(vmem_limit_bytes=VMEM_LIMIT),
        cost_estimate=pl.CostEstimate(
            flops=flops * FORWARD_WEIGHT,
            bytes_accessed=2 * 1024 * 1024,
            transcendentals=frames * HEADS * bins * bins,
        ),
        name="freq_forward",
    )(place, features, near(others), near(weights), gains)


def freq_backward_kernel(
    place_ref, own_ref, others_ref, q_ref, k_ref, v_ref, o_ref, p_ref, gh_ref, w_ref, gain_ref,
    gown_ref, gothers_ref, kept_ref, sent_ref, dg_ref, hold, total
):
    step = pl.program_id(0)
    freq, bins_dev, width = others_ref.shape[0] + 1, own_ref.shape[2], own_ref.shape[3]
    group = hold.shape[0]
    bins_time = bins_dev // group
    scale = (width // HEADS) ** (-0.5)

    @pl.when(step == 0)
    def _():
        hold[...] = gh_ref[...].astype(f32)
        total[...] = jnp.zeros_like(total)
        dg_ref[...] = jnp.zeros_like(dg_ref)

    grad_hidden = grad_hidden_rows(place_ref, hold, step, freq, bins_time)
    grad_hidden_low = grad_hidden.astype(bf16)
    grad_out = dot_nt(grad_hidden_low, w_ref[3]).astype(bf16)
    out_spread = spread(grad_out, 1.0)
    grad_probs = dot_nt(out_spread, v_ref[0])
    probs = [p_ref[0, h] for h in range(HEADS)]
    g_v = dot_tn(stacked_low(probs), out_spread).astype(bf16)
    grad_scores = head_grads(probs, grad_probs, scale)
    g_q = own_channels(dot(grad_scores, k_ref[0]), freq * bins_dev).astype(bf16)
    g_k = dot_tn(grad_scores, spread(q_ref[0], 1.0)).astype(bf16)
    inverse, unit = norm_parts(joined(own_ref, others_ref))
    gain = gain_ref[0:1, :]
    n = (unit * gain).astype(bf16)
    total[0] += dot_tn(n, g_q)
    total[1] += dot_tn(n, g_k)
    total[2] += dot_tn(n, g_v)
    total[3] += dot_tn(o_ref[0], grad_hidden_low)
    g_n = dot_nt(g_q, w_ref[0]) + dot_nt(g_k, w_ref[1]) + dot_nt(g_v, w_ref[2])
    grad_x = grad_hidden + norm_backward(g_n, inverse, unit, gain)
    grad_x = grad_x.astype(bf16)
    gown_ref[0] = grad_x[:bins_dev]
    gothers_ref[...] = grad_x[bins_dev:].reshape(gothers_ref.shape)
    dg_ref[...] += jnp.sum(g_n * unit, axis=0, keepdims=True)

    @pl.when(step == pl.num_programs(0) - 1)
    def _():
        put_halves(place_ref[1], total, kept_ref, sent_ref)


def put_halves(core, total, kept_ref, sent_ref):
    half = kept_ref.shape[0]
    kept_ref[...] = total[pl.ds(core * half, half)].astype(bf16)
    sent_ref[...] = total[pl.ds((1 - core) * half, half)].astype(bf16)


def grad_hidden_rows(place_ref, hold, step, freq, bins_time):
    width = hold.shape[-1]
    rows = pl.ds(pl.multiple_of(step * bins_time, bins_time), bins_time)
    return jnp.concatenate(
        [hold[:, slot_of(place_ref[0], f, freq), rows, :].reshape(-1, width) for f in range(freq)],
        axis=0,
    )


def freq_backward(place, features, others, q, k, v, o, probs, grad_hidden, weights, gains):
    freq, frames, bins_dev, width = features.shape
    bins = freq * bins_dev
    own_spec, others_spec, row_spec = frame_specs(freq, bins_dev, width)
    flops = frames * 2 * bins * (8 * width * width + 4 * HEADS * bins * width)
    half = (2, width, width)
    return pl.pallas_call(
        freq_backward_kernel,
        grid_spec=pltpu.PrefetchScalarGridSpec(
            num_scalar_prefetch=1,
            grid=(frames,),
            in_specs=[own_spec, others_spec]
            + [row_spec] * 4
            + [
                pl.BlockSpec((1, HEADS, bins, bins), lambda i, place: (i, 0, 0, 0)),
                fixed(grad_hidden.shape),
                fixed((4, width, width)),
                fixed(gains.shape),
            ],
            out_specs=[
                pl.BlockSpec((1, bins_dev, width), lambda i, place: (i, 0, 0)),
                others_spec,
                fixed(half),
                fixed(half),
                fixed((1, width)),
            ],
            scratch_shapes=[
                pltpu.VMEM(grad_hidden.shape, f32),
                pltpu.VMEM((4, width, width), f32),
            ],
        ),
        out_shape=[
            pltpu.VMEM((frames, bins_dev, width), bf16),
            pltpu.VMEM(others.shape, bf16),
            pltpu.VMEM(half, bf16),
            pltpu.VMEM(half, bf16),
            jax.ShapeDtypeStruct((1, width), f32),
        ],
        compiler_params=pltpu.CompilerParams(vmem_limit_bytes=VMEM_LIMIT),
        cost_estimate=pl.CostEstimate(
            flops=flops, bytes_accessed=8 * 1024 * 1024, transcendentals=0
        ),
        name="freq_backward",
    )(
        place, features, *map(far, (others, q, k, v, o, probs)), near(grad_hidden),
        near(weights), gains,
    )


def time_kernel(
    bins, own_start, total_frames, place_ref, first_ref, h_ref, up_ref, w_ref, gain_ref,
    gh_hbm, kept_ref, sent_ref, dg_ref,
    gh_ref, total, q_s, k_s, v_s, go_s, o_s, gq_s, gk_s, gv_s, sems
):
    span_rows, width = h_ref.shape
    span = span_rows // bins
    own_rows = gh_ref.shape[0]
    own = own_rows // bins
    scale = (width // HEADS) ** (-0.5)
    gain = gain_ref[1:2, :]
    chunk = own_rows
    while chunk > 256 and chunk % 32 == 0:
        chunk //= 2
    chunks = span_rows // chunk

    for i in range(chunks):
        rows = pl.ds(i * chunk, chunk)
        _, unit = norm_parts(h_ref[rows, :].astype(f32))
        n = (unit * gain).astype(bf16)
        put(q_s, rows, dot(n, w_ref[0]))
        put(k_s, rows, dot(n, w_ref[1]))
        put(v_s, rows, dot(n, w_ref[2]))
    for i in range(chunks):
        rows = pl.ds(i * chunk, chunk)
        put(go_s, rows, dot_nt(up_ref[rows, :], w_ref[3]))

    query = lax.broadcasted_iota(jnp.int32, (span, span), 0)
    key = lax.broadcasted_iota(jnp.int32, (span, span), 1)
    distance = key - query
    allowed = (distance >= -(WINDOW // 2)) & (distance < WINDOW // 2)
    if own != span:
        frame = first_ref[0] + key
        allowed = allowed & (frame >= 0) & (frame < total_frames)

    def one_bin(b, carry):
        rows = pl.ds(b, span, stride=bins)
        q = get(q_s, rows).astype(bf16)
        k = get(k_s, rows).astype(bf16)
        v = get(v_s, rows).astype(bf16)
        grad_out = get(go_s, rows).astype(bf16)
        out_spread = spread(grad_out, 1.0)
        scores = dot_nt(spread(q, scale), k)
        grad_probs = dot_nt(out_spread, v)
        probs = head_probs(scores, allowed)
        low = stacked_low(probs)
        grad_scores = head_grads(probs, grad_probs, scale)
        o = own_channels(dot(low, v), span)
        g_q = own_channels(dot(grad_scores, k), span)
        g_k = dot_tn(grad_scores, spread(q, 1.0))
        g_v = dot_tn(low, out_spread)
        put(o_s, rows, o)
        put(gq_s, rows, g_q)
        put(gk_s, rows, g_k)
        put(gv_s, rows, g_v)
        return carry

    lax.fori_loop(0, bins, one_bin, 0, unroll=UNROLL)

    dg_ref[...] = jnp.zeros_like(dg_ref)
    stores = []
    for i in range(own_rows // chunk):
        mine = pl.ds(i * chunk, chunk)
        rows = pl.ds(own_start + i * chunk, chunk)
        g_q = get(gq_s, rows).astype(bf16)
        g_k = get(gk_s, rows).astype(bf16)
        g_v = get(gv_s, rows).astype(bf16)
        g_n = dot_nt(g_q, w_ref[0]) + dot_nt(g_k, w_ref[1]) + dot_nt(g_v, w_ref[2])
        inverse, unit = norm_parts(h_ref[rows, :].astype(f32))
        n = (unit * gain).astype(bf16)
        up = up_ref[rows, :]
        grad_hidden = up.astype(f32) + norm_backward(g_n, inverse, unit, gain)
        gh_ref[mine, :] = grad_hidden.astype(bf16)
        stores.append(pltpu.make_async_copy(gh_ref.at[mine], gh_hbm.at[mine], sems.at[3 + i]))
        stores[-1].start()
        dg_ref[...] += jnp.sum(g_n * unit, axis=0, keepdims=True)
        parts = (dot_tn(n, g_q), dot_tn(n, g_k), dot_tn(n, g_v), dot_tn(get(o_s, rows).astype(bf16), up))
        for m, part in enumerate(parts):
            total[m] = part if i == 0 else total[m] + part
    put_halves(place_ref[1], total, kept_ref, sent_ref)
    for store in stores:
        store.wait()


UNROLL = 4


def time_attention(place, first, hidden, upstream, weights, gains, bins, own_start, own_rows, total):
    span_rows, width = hidden.shape
    vmem = pl.BlockSpec(memory_space=pltpu.VMEM)
    hbm = pl.BlockSpec(memory_space=pltpu.HBM)
    smem = pl.BlockSpec(memory_space=pltpu.SMEM)
    span = span_rows // bins
    flops = 2 * span_rows * (11 * width * width + 6 * HEADS * span * width)
    return pl.pallas_call(
        functools.partial(time_kernel, bins, own_start, total),
        in_specs=[smem, smem, vmem, vmem, vmem, vmem],
        out_specs=[hbm] + [vmem] * 3,
        out_shape=[pltpu.HBM((own_rows, width), bf16)]
        + [pltpu.VMEM((2, width, width), bf16)] * 2
        + [jax.ShapeDtypeStruct((1, width), f32)],
        scratch_shapes=[
            pltpu.VMEM((own_rows, width), bf16),
            pltpu.VMEM((4, width, width), f32),
        ]
        + [pltpu.VMEM((width // LANES, span_rows, LANES), f32)] * 8
        + [pltpu.SemaphoreType.DMA((16,))],
        compiler_params=pltpu.CompilerParams(vmem_limit_bytes=VMEM_LIMIT),
        cost_estimate=pl.CostEstimate(
            flops=flops,
            bytes_accessed=4 * 1024 * 1024,
            transcendentals=bins * HEADS * span * span,
        ),
        name="time_attention",
    )(place, first, near(hidden), near(upstream), near(weights), gains)


def sums_kernel(kept_ref, arrived_ref, time_ref, freq_gain_ref, time_gain_ref, out_ref, gain_rows):
    peers, _, width = out_ref.shape
    total = kept_ref[...].astype(f32) + arrived_ref[...].astype(f32)
    gain_rows[...] = jnp.zeros_like(gain_rows)
    for m, ref in enumerate((freq_gain_ref, time_gain_ref)):
        high = ref[...].astype(bf16).astype(f32)
        gain_rows[m : m + 1] = high
        gain_rows[m + 2 : m + 3] = ref[...] - high
    parts = [
        total.reshape(peers, -1, width),
        time_ref[...].astype(f32).reshape(peers, -1, width),
        jnp.broadcast_to(gain_rows[...][None], (peers,) + gain_rows.shape),
    ]
    out_ref[...] = jnp.concatenate(parts, axis=1).astype(bf16)


def sums_by_peer(kept, arrived, time_rows, freq_gain, time_gain, peers):
    width = kept.shape[-1]
    freq_count = kept.size // (peers * width)
    time_count = time_rows.size // (peers * width)
    if freq_count % 8 or time_count % 8:
        total = (kept.astype(f32) + arrived.astype(f32)).astype(bf16)
        gains = jnp.concatenate([freq_gain, time_gain], axis=0)
        high = gains.astype(bf16)
        gains = jnp.concatenate([high, (gains - high.astype(f32)).astype(bf16)], axis=0)
        parts = [
            total.reshape(peers, -1, width),
            time_rows.reshape(peers, -1, width),
            jnp.broadcast_to(gains[None], (peers,) + gains.shape),
        ]
        return jnp.concatenate(parts, axis=1), freq_count, time_count
    vmem = pl.BlockSpec(memory_space=pltpu.VMEM)
    sums = pl.pallas_call(
        sums_kernel,
        in_specs=[vmem] * 5,
        out_specs=vmem,
        out_shape=pltpu.HBM((peers, freq_count + time_count + 8, width), bf16),
        scratch_shapes=[pltpu.VMEM((8, width), f32)],
        compiler_params=pltpu.CompilerParams(vmem_limit_bytes=VMEM_LIMIT),
        cost_estimate=pl.CostEstimate(
            flops=kept.size, bytes_accessed=6 * kept.size, transcendentals=0
        ),
        name="sums_by_peer",
    )(kept, arrived, time_rows, freq_gain, time_gain)
    return sums, freq_count, time_count


def group_size(devices, bins_dev):
    best = 1
    for size in range(1, devices + 1):
        if devices % size == 0 and bins_dev % (8 * size) == 0:
            best = size
    return best


def per_device(features, upstream, weights, gains):
    frames_dev, bins_dev, width = features.shape
    tm, freq = lax.axis_size("tm"), lax.axis_size("freq")
    total_frames = frames_dev * tm
    frames = frames_dev // freq
    group = group_size(tm, bins_dev)
    bins_time = bins_dev // group
    group_frames = group * frames_dev
    whole = group == tm
    sides = 0 if whole else -(-WINDOW // group_frames)
    groups = (
        None
        if whole
        else [list(range(g * group, (g + 1) * group)) for g in range(tm // group)]
    )

    def over_tm(blocks):
        return lax.all_to_all(blocks, "tm", 0, 0, tiled=True, axis_index_groups=groups)

    def over_all(blocks):
        if whole:
            flat = blocks.reshape((tm * freq,) + blocks.shape[2:])
            return lax.all_to_all(flat, ("tm", "freq"), 0, 0, tiled=True).reshape(blocks.shape)
        return over_tm(lax.all_to_all(blocks, "freq", 1, 1, tiled=True))

    def with_sides(rows):
        parts = [rows]
        for away in range(1, sides + 1):
            shift = away * group
            before = lax.ppermute(rows, "tm", [(i, i + shift) for i in range(tm - shift)])
            after = lax.ppermute(rows, "tm", [(i + shift, i) for i in range(tm - shift)])
            parts = [before] + parts + [after]
        return jnp.concatenate(parts, axis=0) if sides else rows

    core = lax.axis_index("tm") % 2
    place = jnp.stack([lax.axis_index("freq"), core]).astype(jnp.int32)
    by_target = features.reshape(freq, frames, bins_dev, width)

    def along_freq(block, steps):
        return lax.ppermute(block, "freq", [(i, (i + steps) % freq) for i in range(freq)])

    others = jnp.stack(
        [
            along_freq(lax.dynamic_index_in_dim(by_target, (place[0] + j) % freq, 0, False), j)
            for j in range(1, freq)
        ]
    )
    up_blocks = jnp.swapaxes(upstream.reshape(frames_dev, group, bins_time, width), 0, 1)
    up_rows = over_tm(up_blocks).reshape(-1, width)
    freq_w = weights[:4]
    q, k, v, o, probs, hidden_blocks = freq_forward(place, by_target, others, freq_w, gains, group)
    time_w, hidden_blocks = lax.optimization_barrier((weights, hidden_blocks))
    time_w = time_w[4:]
    hidden_rows = over_all(hidden_blocks).reshape(-1, width)
    own_rows = hidden_rows.shape[0]
    position = lax.axis_index("tm") // group
    first = ((position - sides) * group_frames).astype(jnp.int32).reshape(1)
    grad_rows, time_kept, time_sent, time_dg = time_attention(
        place,
        first,
        with_sides(hidden_rows),
        with_sides(up_rows),
        time_w,
        gains,
        bins_time,
        sides * own_rows,
        own_rows,
        total_frames,
    )
    grad_hidden = over_all(grad_rows.reshape(hidden_blocks.shape))

    pairs = [(i, i ^ 1) for i in range(tm)]
    same = [
        [t * freq + f for t in range(c, tm, 2) for f in range(freq)] for c in range(2)
    ]
    peers = len(same[0])

    rows = 2 * width
    sets = 2 * freq
    halved = tm % 4 == 0 and freq & (freq - 1) == 0 and rows % (8 * sets * peers) == 0
    steps = [("tm", 1)] + [("freq", k) for k in reversed(range(freq.bit_length() - 1))]
    if not halved:
        sets, steps = 1, []

    def scattered(partial):
        partial = partial.reshape((2,) * len(steps) + (-1, width))
        for axis, k in steps:
            mine = (lax.axis_index(axis) >> k) & 1
            sent = lax.dynamic_index_in_dim(partial, 1 - mine, 0, False)
            kept = lax.dynamic_index_in_dim(partial, mine, 0, False)
            devices = range(lax.axis_size(axis))
            came = lax.ppermute(sent, axis, [(d, d ^ (1 << k)) for d in devices])
            partial = (kept.astype(f32) + came.astype(f32)).astype(bf16)
        return partial

    def over_same(blocks):
        return lax.all_to_all(
            blocks, ("tm", "freq"), 0, 0, tiled=True, axis_index_groups=same
        )

    time_arrived = lax.ppermute(time_sent, "tm", pairs)
    time_rows = scattered((time_kept.astype(f32) + time_arrived.astype(f32)).astype(bf16))
    grad_own, grad_others, freq_kept, freq_sent, freq_dg = freq_backward(
        place, by_target, others, q, k, v, o, probs, grad_hidden, freq_w, gains
    )
    freq_arrived = lax.ppermute(freq_sent, "tm", pairs)
    sums, freq_count, time_count = sums_by_peer(
        freq_kept, freq_arrived, time_rows, freq_dg, time_dg, peers
    )
    arrived = over_same(sums)
    returned = [grad_own] + [along_freq(grad_others[j - 1], -j) for j in range(1, freq)]
    returned, arrived = lax.optimization_barrier((returned, arrived))
    grad_input = jnp.roll(jnp.stack(returned), place[0], axis=0).reshape(features.shape)

    inv_root = (total_frames * bins_dev * freq) ** (-0.5)
    summed = jnp.sum(arrived.astype(f32), axis=0) * inv_root
    gain_sum = summed[freq_count + time_count :]
    gain_sum = gain_sum[:2] + gain_sum[2:4]
    time_arrived = arrived[:, freq_count : freq_count + time_count].astype(f32)
    time_sum = jnp.sum(time_arrived.reshape(-1, sets, time_count, width), axis=0) * inv_root
    block = jnp.concatenate([summed[:freq_count], time_sum.reshape(-1, width)], axis=0)
    block, gain_sum = lax.optimization_barrier((block.astype(bf16), gain_sum))
    gathered = over_same(jnp.broadcast_to(block[None], (peers,) + block.shape))
    gathered, gain_sum = lax.optimization_barrier((gathered, gain_sum))
    gain_grads = gain_sum + lax.ppermute(gain_sum, "tm", pairs)
    theirs = lax.ppermute(gathered, "tm", pairs)
    first_core = core == 0
    halves = jnp.stack(
        [jnp.where(first_core, gathered, theirs), jnp.where(first_core, theirs, gathered)]
    )
    freq_grads = halves[:, :, :freq_count].reshape(4, width, width)
    time_grads = halves[:, :, freq_count:].reshape(2, peers, sets, time_count, width)
    time_grads = jnp.swapaxes(time_grads, 1, 2).reshape(4, width, width)
    weight_grads = jnp.concatenate([freq_grads, time_grads], axis=0).astype(f32)
    return (grad_input, weight_grads, gain_grads)


def solution(mesh):
    return jax.shard_map(
        per_device,
        mesh=mesh,
        in_specs=(P("tm", "freq", None), P("tm", "freq", None), P(), P()),
        out_specs=(P("tm", "freq", None), P(), P()),
        check_vma=False,
    )
```

```python
import functools

import jax
import jax.numpy as jnp
from jax import lax
from jax.experimental import pallas as pl
from jax.experimental.pallas import tpu as pltpu
from jax.sharding import PartitionSpec as P

HEADS = 4
WINDOW = 128

epsilon = 1e-06
masked_score = -1e30

f32 = jnp.float32
bf16 = jnp.bfloat16
LANES = 128
MIB = 1024 * 1024
VMEM_LIMIT = 24 * MIB
FORWARD_WEIGHT = 40

CONTRACT_LAST = (((1,), (1,)), ((), ()))
CONTRACT_FIRST = (((0,), (0,)), ((), ()))


def dot(left, right):
    return jnp.dot(left, right, preferred_element_type=f32)


def dot_nt(left, right):
    return lax.dot_general(left, right, CONTRACT_LAST, preferred_element_type=f32)


def dot_tn(left, right):
    return lax.dot_general(left, right, CONTRACT_FIRST, preferred_element_type=f32)


def put(ref, rows, value):
    for c in range(ref.shape[0]):
        ref[c, rows, :] = value[:, c * LANES : (c + 1) * LANES]


def get(ref, rows):
    return jnp.concatenate([ref[c, rows, :] for c in range(ref.shape[0])], axis=1)


def norm_parts(widened):
    inverse = lax.rsqrt(jnp.mean(widened * widened, axis=-1, keepdims=True) + epsilon)
    return inverse, widened * inverse


def norm_backward(incoming, inverse, unit_rows, gain):
    scaled = incoming * gain
    return inverse * (scaled - unit_rows * jnp.mean(scaled * unit_rows, axis=-1, keepdims=True))


def spread(rows, factor):
    width = rows.shape[-1]
    owner = lax.broadcasted_iota(jnp.int32, (1, width), 1) // (width // HEADS)
    return jnp.concatenate(
        [rows * jnp.where(owner == h, factor, 0.0).astype(rows.dtype) for h in range(HEADS)], axis=0
    )


def own_channels(stacked, rows):
    width = stacked.shape[-1]
    owner = lax.broadcasted_iota(jnp.int32, (1, width), 1) // (width // HEADS)
    result = stacked[:rows]
    for h in range(1, HEADS):
        result = jnp.where(owner == h, stacked[h * rows : (h + 1) * rows], result)
    return result


def head_probs(scores, allowed):
    rows = scores.shape[0] // HEADS
    probs = []
    for h in range(HEADS):
        s = scores[h * rows : (h + 1) * rows]
        if allowed is not None:
            s = jnp.where(allowed, s, masked_score)
        e = jnp.exp(s - jnp.max(s, axis=-1, keepdims=True))
        probs.append(e * (1.0 / jnp.sum(e, axis=-1, keepdims=True)))
    return probs


def head_grads(probs, grad_probs, scale):
    rows = grad_probs.shape[0] // HEADS
    grad_scores = []
    for h in range(HEADS):
        gp = grad_probs[h * rows : (h + 1) * rows]
        row_dot = jnp.sum(gp * probs[h], axis=-1, keepdims=True)
        grad_scores.append((probs[h] * (gp - row_dot) * scale).astype(bf16))
    return jnp.concatenate(grad_scores, axis=0)


def stacked_low(probs):
    return jnp.concatenate([p.astype(bf16) for p in probs], axis=0)


def slot_of(position, back, freq):
    return lax.rem(position - back + freq, freq)


def freq_forward_kernel(
    place_ref, own_ref, others_ref, w_ref, gain_ref, q_ref, k_ref, v_ref, o_ref, p_ref, h_hbm,
    hold, low, sem
):
    step = pl.program_id(0)
    freq, bins_dev, width = others_ref.shape[0] + 1, own_ref.shape[2], own_ref.shape[3]
    bins_time = hold.shape[2] // pl.num_programs(0)
    x = joined(own_ref.at[0, 0], others_ref.at[:, 0])
    _, unit = norm_parts(x)
    n = (unit * gain_ref[0:1, :]).astype(bf16)
    scale = (width // HEADS) ** (-0.5)
    q = dot(n, w_ref[0]).astype(bf16)
    k = dot(n, w_ref[1]).astype(bf16)
    v = dot(n, w_ref[2]).astype(bf16)
    probs = head_probs(dot_nt(spread(q, scale), k), None)
    o = own_channels(dot(stacked_low(probs), v), n.shape[0]).astype(bf16)
    hidden = x + dot(o, w_ref[3])
    q_ref[0] = q
    k_ref[0] = k
    v_ref[0] = v
    o_ref[0] = o
    for h in range(HEADS):
        p_ref[0, h] = probs[h].astype(bf16)
    rows = pl.ds(pl.multiple_of(step * bins_time, bins_time), bins_time)
    for f in range(freq):
        part = hidden[f * bins_dev : (f + 1) * bins_dev].reshape(-1, bins_time, width)
        hold[:, slot_of(place_ref[0], f, freq), rows, :] = part

    @pl.when(step == pl.num_programs(0) - 1)
    def _():
        low[...] = hold[...].astype(bf16)
        copy = pltpu.make_async_copy(low, h_hbm, sem)
        copy.start()
        copy.wait()


def joined(own_ref, others_ref):
    width = own_ref.shape[-1]
    return jnp.concatenate(
        [own_ref[...].reshape(-1, width), others_ref[...].reshape(-1, width)], axis=0
    ).astype(f32)


def near(array):
    return pltpu.with_memory_space_constraint(array, pltpu.VMEM)


def far(array):
    return pltpu.with_memory_space_constraint(array, pltpu.HBM)


def frame_specs(freq, bins_dev, width, count=1):
    own = pl.BlockSpec((1, count, bins_dev, width), lambda i, place: (place[0], i, 0, 0))
    others = pl.BlockSpec((freq - 1, count, bins_dev, width), lambda i, place: (0, i, 0, 0))
    rows = pl.BlockSpec((count, freq * bins_dev, width), lambda i, place: (i, 0, 0))
    return own, others, rows


def fixed(shape):
    return pl.BlockSpec(shape, lambda i, place: (0,) * len(shape))


def freq_forward(place, features, others, weights, gains, group):
    freq, frames, bins_dev, width = features.shape
    bins = freq * bins_dev
    rows = frames * (bins_dev // group)
    own_spec, others_spec, row_spec = frame_specs(freq, bins_dev, width)
    rowshape = pltpu.HBM((frames, bins, width), bf16)
    whole = (group, freq, rows, width)
    flops = frames * 2 * bins * (4 * width * width + 2 * HEADS * bins * width)
    return pl.pallas_call(
        freq_forward_kernel,
        grid_spec=pltpu.PrefetchScalarGridSpec(
            num_scalar_prefetch=1,
            grid=(frames,),
            in_specs=[own_spec, others_spec, fixed(weights.shape), fixed(gains.shape)],
            out_specs=[row_spec] * 4
            + [
                pl.BlockSpec((1, HEADS, bins, bins), lambda i, place: (i, 0, 0, 0)),
                pl.BlockSpec(memory_space=pltpu.HBM),
            ],
            scratch_shapes=[
                pltpu.VMEM(whole, f32),
                pltpu.VMEM(whole, bf16),
                pltpu.SemaphoreType.DMA,
            ],
        ),
        out_shape=[rowshape] * 4
        + [pltpu.HBM((frames, HEADS, bins, bins), bf16), pltpu.HBM(whole, bf16)],
        compiler_params=pltpu.CompilerParams(vmem_limit_bytes=VMEM_LIMIT),
        cost_estimate=pl.CostEstimate(
            flops=flops * FORWARD_WEIGHT,
            bytes_accessed=2 * 1024 * 1024,
            transcendentals=frames * HEADS * bins * bins,
        ),
        name="freq_forward",
    )(place, features, near(others), near(weights), gains)


def freq_backward_kernel(
    place_ref, x_hbm, others_hbm, q_hbm, k_hbm, v_hbm, o_hbm, p_hbm, gh_ref, w_ref, gain_ref,
    gown_ref, gothers_ref, kept_ref, sent_ref, dg_ref,
    own_ref, others_ref, q_ref, k_ref, v_ref, o_ref, p_ref, hold, total, sems
):
    frames, bins_dev, width = own_ref.shape
    freq = others_ref.shape[0] + 1
    bins_time = bins_dev // hold.shape[0]
    scale = (width // HEADS) ** (-0.5)
    gain = gain_ref[0:1, :]
    loads = {}
    for name, source, target in (
        ("v", v_hbm, v_ref),
        ("p", p_hbm, p_ref),
        ("k", k_hbm, k_ref),
        ("q", q_hbm, q_ref),
        ("own", x_hbm.at[place_ref[0]], own_ref),
        ("others", others_hbm, others_ref),
        ("o", o_hbm, o_ref),
    ):
        loads[name] = pltpu.make_async_copy(source, target, sems.at[len(loads)])
        loads[name].start()
    hold[...] = gh_ref[...].astype(f32)
    first = []
    for f in range(frames):
        grad_hidden = grad_hidden_rows(place_ref, hold, f, freq, bins_time)
        low = grad_hidden.astype(bf16)
        out_spread = spread(dot_nt(low, w_ref[3]).astype(bf16), 1.0)
        first.append((grad_hidden, low, out_spread))
    loads["v"].wait()
    first = [parts + (dot_nt(parts[2], v_ref[f]),) for f, parts in enumerate(first)]
    loads["p"].wait()
    second = []
    for f, (_, _, out_spread, grad_probs) in enumerate(first):
        probs = [p_ref[f, h].astype(f32) for h in range(HEADS)]
        g_v = dot_tn(p_ref[f].reshape(-1, p_ref.shape[3]), out_spread).astype(bf16)
        second.append((g_v, head_grads(probs, grad_probs, scale)))
    for name in ("k", "q", "own", "others", "o"):
        loads[name].wait()
    third = []
    for f, (g_v, grad_scores) in enumerate(second):
        g_q = own_channels(dot(grad_scores, k_ref[f]), freq * bins_dev).astype(bf16)
        g_k = dot_tn(grad_scores, spread(q_ref[f], 1.0)).astype(bf16)
        third.append((g_q, g_k, g_v))
    dg_ref[...] = jnp.zeros_like(dg_ref)
    for f, ((grad_hidden, low, _, _), (g_q, g_k, g_v)) in enumerate(zip(first, third)):
        inverse, unit = norm_parts(joined(own_ref.at[f], others_ref.at[:, f]))
        n = (unit * gain).astype(bf16)
        parts = (dot_tn(n, g_q), dot_tn(n, g_k), dot_tn(n, g_v), dot_tn(o_ref[f], low))
        for m, part in enumerate(parts):
            total[m] = part if f == 0 else total[m] + part
        g_n = dot_nt(g_q, w_ref[0]) + dot_nt(g_k, w_ref[1]) + dot_nt(g_v, w_ref[2])
        grad_x = (grad_hidden + norm_backward(g_n, inverse, unit, gain)).astype(bf16)
        gown_ref[f] = grad_x[:bins_dev]
        gothers_ref[:, f] = grad_x[bins_dev:].reshape(freq - 1, bins_dev, width)
        dg_ref[...] += jnp.sum(g_n * unit, axis=0, keepdims=True)
    put_halves(place_ref[1], total, kept_ref, sent_ref)


def put_halves(core, total, kept_ref, sent_ref):
    half = kept_ref.shape[0]
    kept_ref[...] = total[pl.ds(core * half, half)].astype(bf16)
    sent_ref[...] = total[pl.ds((1 - core) * half, half)].astype(bf16)


def grad_hidden_rows(place_ref, hold, frame, freq, bins_time):
    width = hold.shape[-1]
    rows = pl.ds(frame * bins_time, bins_time)
    return jnp.concatenate(
        [hold[:, slot_of(place_ref[0], f, freq), rows, :].reshape(-1, width) for f in range(freq)],
        axis=0,
    )


def freq_backward(place, features, others, q, k, v, o, probs, grad_hidden, weights, gains):
    freq, frames, bins_dev, width = features.shape
    bins = freq * bins_dev
    flops = frames * 2 * bins * (8 * width * width + 4 * HEADS * bins * width)
    half = (2, width, width)
    vmem = pl.BlockSpec(memory_space=pltpu.VMEM)
    hbm = pl.BlockSpec(memory_space=pltpu.HBM)
    rows = pltpu.VMEM((frames, bins, width), bf16)
    return pl.pallas_call(
        freq_backward_kernel,
        in_specs=[pl.BlockSpec(memory_space=pltpu.SMEM)] + [hbm] * 7 + [vmem] * 3,
        out_specs=[vmem] * 5,
        out_shape=[
            pltpu.VMEM((frames, bins_dev, width), bf16),
            pltpu.VMEM(others.shape, bf16),
            pltpu.VMEM(half, bf16),
            pltpu.VMEM(half, bf16),
            jax.ShapeDtypeStruct((1, width), f32),
        ],
        scratch_shapes=[
            pltpu.VMEM((frames, bins_dev, width), bf16),
            pltpu.VMEM(others.shape, bf16),
            rows,
            rows,
            rows,
            rows,
            pltpu.VMEM(probs.shape, bf16),
            pltpu.VMEM(grad_hidden.shape, f32),
            pltpu.VMEM((4, width, width), f32),
            pltpu.SemaphoreType.DMA((7,)),
        ],
        compiler_params=pltpu.CompilerParams(vmem_limit_bytes=VMEM_LIMIT),
        cost_estimate=pl.CostEstimate(
            flops=flops, bytes_accessed=8 * 1024 * 1024, transcendentals=0
        ),
        name="freq_backward",
    )(
        place, *map(far, (features, others, q, k, v, o, probs)), near(grad_hidden),
        near(weights), gains,
    )


def time_kernel(
    bins, own_start, total_frames, place_ref, first_ref, h_ref, up_ref, w_ref, gain_ref,
    gh_hbm, kept_ref, sent_ref, dg_ref,
    gh_ref, total, q_s, k_s, v_s, go_s, o_s, gq_s, gk_s, gv_s, sems
):
    span_rows, width = h_ref.shape
    span = span_rows // bins
    own_rows = gh_ref.shape[0]
    own = own_rows // bins
    scale = (width // HEADS) ** (-0.5)
    gain = gain_ref[1:2, :]
    chunk = own_rows
    while chunk > 256 and chunk % 32 == 0:
        chunk //= 2
    chunks = span_rows // chunk

    for i in range(chunks):
        rows = pl.ds(i * chunk, chunk)
        _, unit = norm_parts(h_ref[rows, :].astype(f32))
        n = (unit * gain).astype(bf16)
        put(q_s, rows, dot(n, w_ref[0]))
        put(k_s, rows, dot(n, w_ref[1]))
        put(v_s, rows, dot(n, w_ref[2]))
    for i in range(chunks):
        rows = pl.ds(i * chunk, chunk)
        put(go_s, rows, dot_nt(up_ref[rows, :], w_ref[3]))

    query = lax.broadcasted_iota(jnp.int32, (span, span), 0)
    key = lax.broadcasted_iota(jnp.int32, (span, span), 1)
    distance = key - query
    allowed = (distance >= -(WINDOW // 2)) & (distance < WINDOW // 2)
    if own != span:
        frame = first_ref[0] + key
        allowed = allowed & (frame >= 0) & (frame < total_frames)

    together = max(n for n in (1, 2, 4) if bins % n == 0 and (n == 1 or n * span <= 512))

    def some_bins(start):
        places = [pl.ds(start + b, span, stride=bins) for b in range(together)]
        first = []
        for rows in places:
            q, k, v, grad_out = (get(ref, rows).astype(bf16) for ref in (q_s, k_s, v_s, go_s))
            out_spread = spread(grad_out, 1.0)
            first.append((q, k, v, out_spread, dot_nt(spread(q, scale), k), dot_nt(out_spread, v)))
        second = []
        for q, k, v, out_spread, scores, grad_probs in first:
            probs = head_probs(scores, allowed)
            second.append((stacked_low(probs), head_grads(probs, grad_probs, scale)))
        for rows, (q, k, v, out_spread, _, _), (low, grad_scores) in zip(places, first, second):
            put(o_s, rows, own_channels(dot(low, v), span))
            put(gq_s, rows, own_channels(dot(grad_scores, k), span))
            put(gk_s, rows, dot_tn(grad_scores, spread(q, 1.0)))
            put(gv_s, rows, dot_tn(low, out_spread))

    for start in range(0, bins, together):
        some_bins(start)

    dg_ref[...] = jnp.zeros_like(dg_ref)
    stores = []
    for i in range(own_rows // chunk):
        mine = pl.ds(i * chunk, chunk)
        rows = pl.ds(own_start + i * chunk, chunk)
        g_q = get(gq_s, rows).astype(bf16)
        g_k = get(gk_s, rows).astype(bf16)
        g_v = get(gv_s, rows).astype(bf16)
        g_n = dot_nt(g_q, w_ref[0]) + dot_nt(g_k, w_ref[1]) + dot_nt(g_v, w_ref[2])
        inverse, unit = norm_parts(h_ref[rows, :].astype(f32))
        n = (unit * gain).astype(bf16)
        up = up_ref[rows, :]
        grad_hidden = up.astype(f32) + norm_backward(g_n, inverse, unit, gain)
        gh_ref[mine, :] = grad_hidden.astype(bf16)
        stores.append(pltpu.make_async_copy(gh_ref.at[mine], gh_hbm.at[mine], sems.at[3 + i]))
        stores[-1].start()
        dg_ref[...] += jnp.sum(g_n * unit, axis=0, keepdims=True)
        parts = (dot_tn(n, g_q), dot_tn(n, g_k), dot_tn(n, g_v), dot_tn(get(o_s, rows).astype(bf16), up))
        for m, part in enumerate(parts):
            total[m] = part if i == 0 else total[m] + part
    put_halves(place_ref[1], total, kept_ref, sent_ref)
    for store in stores:
        store.wait()


def time_attention(place, first, hidden, upstream, weights, gains, bins, own_start, own_rows, total):
    span_rows, width = hidden.shape
    vmem = pl.BlockSpec(memory_space=pltpu.VMEM)
    hbm = pl.BlockSpec(memory_space=pltpu.HBM)
    smem = pl.BlockSpec(memory_space=pltpu.SMEM)
    span = span_rows // bins
    flops = 2 * span_rows * (11 * width * width + 6 * HEADS * span * width)
    return pl.pallas_call(
        functools.partial(time_kernel, bins, own_start, total),
        in_specs=[smem, smem, vmem, vmem, vmem, vmem],
        out_specs=[hbm] + [vmem] * 3,
        out_shape=[pltpu.HBM((own_rows, width), bf16)]
        + [pltpu.VMEM((2, width, width), bf16)] * 2
        + [jax.ShapeDtypeStruct((1, width), f32)],
        scratch_shapes=[
            pltpu.VMEM((own_rows, width), bf16),
            pltpu.VMEM((4, width, width), f32),
        ]
        + [pltpu.VMEM((width // LANES, span_rows, LANES), f32)] * 8
        + [pltpu.SemaphoreType.DMA((16,))],
        compiler_params=pltpu.CompilerParams(vmem_limit_bytes=VMEM_LIMIT),
        cost_estimate=pl.CostEstimate(
            flops=flops,
            bytes_accessed=4 * 1024 * 1024,
            transcendentals=bins * HEADS * span * span,
        ),
        name="time_attention",
    )(place, first, near(hidden), near(upstream), near(weights), gains)


def sums_kernel(kept_ref, arrived_ref, time_ref, freq_gain_ref, time_gain_ref, out_ref, gain_rows):
    peers, _, width = out_ref.shape
    total = kept_ref[...].astype(f32) + arrived_ref[...].astype(f32)
    gain_rows[...] = jnp.zeros_like(gain_rows)
    for m, ref in enumerate((freq_gain_ref, time_gain_ref)):
        high = ref[...].astype(bf16).astype(f32)
        gain_rows[m : m + 1] = high
        gain_rows[m + 2 : m + 3] = ref[...] - high
    parts = [
        total.reshape(peers, -1, width),
        time_ref[...].astype(f32).reshape(peers, -1, width),
        jnp.broadcast_to(gain_rows[...][None], (peers,) + gain_rows.shape),
    ]
    out_ref[...] = jnp.concatenate(parts, axis=1).astype(bf16)


def sums_by_peer(kept, arrived, time_rows, freq_gain, time_gain, peers):
    width = kept.shape[-1]
    freq_count = kept.size // (peers * width)
    time_count = time_rows.size // (peers * width)
    if freq_count % 8 or time_count % 8:
        total = (kept.astype(f32) + arrived.astype(f32)).astype(bf16)
        gains = jnp.concatenate([freq_gain, time_gain], axis=0)
        high = gains.astype(bf16)
        gains = jnp.concatenate([high, (gains - high.astype(f32)).astype(bf16)], axis=0)
        parts = [
            total.reshape(peers, -1, width),
            time_rows.reshape(peers, -1, width),
            jnp.broadcast_to(gains[None], (peers,) + gains.shape),
        ]
        return jnp.concatenate(parts, axis=1), freq_count, time_count
    vmem = pl.BlockSpec(memory_space=pltpu.VMEM)
    sums = pl.pallas_call(
        sums_kernel,
        in_specs=[vmem] * 5,
        out_specs=vmem,
        out_shape=pltpu.HBM((peers, freq_count + time_count + 8, width), bf16),
        scratch_shapes=[pltpu.VMEM((8, width), f32)],
        compiler_params=pltpu.CompilerParams(vmem_limit_bytes=VMEM_LIMIT),
        cost_estimate=pl.CostEstimate(
            flops=kept.size, bytes_accessed=6 * kept.size, transcendentals=0
        ),
        name="sums_by_peer",
    )(kept, arrived, time_rows, freq_gain, time_gain)
    return sums, freq_count, time_count


def group_size(devices, bins_dev):
    best = 1
    for size in range(1, devices + 1):
        if devices % size == 0 and bins_dev % (8 * size) == 0:
            best = size
    return best


def per_device(features, upstream, weights, gains):
    frames_dev, bins_dev, width = features.shape
    tm, freq = lax.axis_size("tm"), lax.axis_size("freq")
    total_frames = frames_dev * tm
    frames = frames_dev // freq
    group = group_size(tm, bins_dev)
    bins_time = bins_dev // group
    group_frames = group * frames_dev
    whole = group == tm
    sides = 0 if whole else -(-WINDOW // group_frames)
    groups = (
        None
        if whole
        else [list(range(g * group, (g + 1) * group)) for g in range(tm // group)]
    )

    def over_tm(blocks):
        return lax.all_to_all(blocks, "tm", 0, 0, tiled=True, axis_index_groups=groups)

    def over_all(blocks):
        if whole:
            flat = blocks.reshape((tm * freq,) + blocks.shape[2:])
            return lax.all_to_all(flat, ("tm", "freq"), 0, 0, tiled=True).reshape(blocks.shape)
        return over_tm(lax.all_to_all(blocks, "freq", 1, 1, tiled=True))

    def with_sides(rows):
        parts = [rows]
        for away in range(1, sides + 1):
            shift = away * group
            before = lax.ppermute(rows, "tm", [(i, i + shift) for i in range(tm - shift)])
            after = lax.ppermute(rows, "tm", [(i + shift, i) for i in range(tm - shift)])
            parts = [before] + parts + [after]
        return jnp.concatenate(parts, axis=0) if sides else rows

    core = lax.axis_index("tm") % 2
    place = jnp.stack([lax.axis_index("freq"), core]).astype(jnp.int32)
    by_target = features.reshape(freq, frames, bins_dev, width)

    def along_freq(block, steps):
        return lax.ppermute(block, "freq", [(i, (i + steps) % freq) for i in range(freq)])

    others = jnp.stack(
        [
            along_freq(lax.dynamic_index_in_dim(by_target, (place[0] + j) % freq, 0, False), j)
            for j in range(1, freq)
        ]
    )
    up_blocks = jnp.swapaxes(upstream.reshape(frames_dev, group, bins_time, width), 0, 1)
    up_rows = over_tm(up_blocks).reshape(-1, width)
    freq_w = weights[:4]
    q, k, v, o, probs, hidden_blocks = freq_forward(place, by_target, others, freq_w, gains, group)
    time_w, hidden_blocks = lax.optimization_barrier((weights, hidden_blocks))
    time_w = time_w[4:]
    hidden_rows = over_all(hidden_blocks).reshape(-1, width)
    own_rows = hidden_rows.shape[0]
    position = lax.axis_index("tm") // group
    first = ((position - sides) * group_frames).astype(jnp.int32).reshape(1)
    grad_rows, time_kept, time_sent, time_dg = time_attention(
        place,
        first,
        with_sides(hidden_rows),
        with_sides(up_rows),
        time_w,
        gains,
        bins_time,
        sides * own_rows,
        own_rows,
        total_frames,
    )
    grad_hidden = over_all(grad_rows.reshape(hidden_blocks.shape))

    pairs = [(i, i ^ 1) for i in range(tm)]
    same = [
        [t * freq + f for t in range(c, tm, 2) for f in range(freq)] for c in range(2)
    ]
    peers = len(same[0])

    rows = 2 * width
    sets = 2 * freq
    halved = tm % 4 == 0 and freq & (freq - 1) == 0 and rows % (8 * sets * peers) == 0
    steps = [("tm", 1)] + [("freq", k) for k in reversed(range(freq.bit_length() - 1))]
    if not halved:
        sets, steps = 1, []

    def scattered(partial):
        partial = partial.reshape((2,) * len(steps) + (-1, width))
        for axis, k in steps:
            mine = (lax.axis_index(axis) >> k) & 1
            sent = lax.dynamic_index_in_dim(partial, 1 - mine, 0, False)
            kept = lax.dynamic_index_in_dim(partial, mine, 0, False)
            devices = range(lax.axis_size(axis))
            came = lax.ppermute(sent, axis, [(d, d ^ (1 << k)) for d in devices])
            partial = (kept.astype(f32) + came.astype(f32)).astype(bf16)
        return partial

    def over_same(blocks):
        return lax.all_to_all(
            blocks, ("tm", "freq"), 0, 0, tiled=True, axis_index_groups=same
        )

    time_arrived = lax.ppermute(time_sent, "tm", pairs)
    time_rows = scattered((time_kept.astype(f32) + time_arrived.astype(f32)).astype(bf16))
    grad_own, grad_others, freq_kept, freq_sent, freq_dg = freq_backward(
        place, by_target, others, q, k, v, o, probs, grad_hidden, freq_w, gains
    )
    freq_arrived = lax.ppermute(freq_sent, "tm", pairs)
    sums, freq_count, time_count = sums_by_peer(
        freq_kept, freq_arrived, time_rows, freq_dg, time_dg, peers
    )
    arrived = over_same(sums)
    returned = [grad_own] + [along_freq(grad_others[j - 1], -j) for j in range(1, freq)]
    returned, arrived = lax.optimization_barrier((returned, arrived))
    grad_input = jnp.roll(jnp.stack(returned), place[0], axis=0).reshape(features.shape)

    inv_root = (total_frames * bins_dev * freq) ** (-0.5)
    summed = jnp.sum(arrived.astype(f32), axis=0) * inv_root
    gain_sum = summed[freq_count + time_count :]
    gain_sum = gain_sum[:2] + gain_sum[2:4]
    time_arrived = arrived[:, freq_count : freq_count + time_count].astype(f32)
    time_sum = jnp.sum(time_arrived.reshape(-1, sets, time_count, width), axis=0) * inv_root
    block = jnp.concatenate([summed[:freq_count], time_sum.reshape(-1, width)], axis=0)
    block, gain_sum = lax.optimization_barrier((block.astype(bf16), gain_sum))
    gathered = over_same(jnp.broadcast_to(block[None], (peers,) + block.shape))
    gathered, gain_sum = lax.optimization_barrier((gathered, gain_sum))
    gain_grads = gain_sum + lax.ppermute(gain_sum, "tm", pairs)
    theirs = lax.ppermute(gathered, "tm", pairs)
    first_core = core == 0
    halves = jnp.stack(
        [jnp.where(first_core, gathered, theirs), jnp.where(first_core, theirs, gathered)]
    )
    freq_grads = halves[:, :, :freq_count].reshape(4, width, width)
    time_grads = halves[:, :, freq_count:].reshape(2, peers, sets, time_count, width)
    time_grads = jnp.swapaxes(time_grads, 1, 2).reshape(4, width, width)
    weight_grads = jnp.concatenate([freq_grads, time_grads], axis=0).astype(f32)
    return (grad_input, weight_grads, gain_grads)


def solution(mesh):
    return jax.shard_map(
        per_device,
        mesh=mesh,
        in_specs=(P("tm", "freq", None), P("tm", "freq", None), P(), P()),
        out_specs=(P("tm", "freq", None), P(), P()),
        check_vma=False,
    )
```

```python
import functools

import jax
import jax.numpy as jnp
from jax import lax
from jax.experimental import pallas as pl
from jax.experimental.pallas import tpu as pltpu
from jax.sharding import PartitionSpec as P

HEADS = 4
WINDOW = 128

epsilon = 1e-06
masked_score = -1e30

f32 = jnp.float32
bf16 = jnp.bfloat16
LANES = 128
GAIN_ROWS = 16
MIB = 1024 * 1024
VMEM_LIMIT = 24 * MIB
FORWARD_WEIGHT = 40

CONTRACT_LAST = (((1,), (1,)), ((), ()))
CONTRACT_FIRST = (((0,), (0,)), ((), ()))


def dot(left, right):
    return jnp.dot(left, right, preferred_element_type=f32)


def dot_nt(left, right):
    return lax.dot_general(left, right, CONTRACT_LAST, preferred_element_type=f32)


def dot_tn(left, right):
    return lax.dot_general(left, right, CONTRACT_FIRST, preferred_element_type=f32)


def put(ref, rows, value):
    for c in range(ref.shape[0]):
        ref[c, rows, :] = value[:, c * LANES : (c + 1) * LANES]


def get(ref, rows):
    return jnp.concatenate([ref[c, rows, :] for c in range(ref.shape[0])], axis=1)


def norm_parts(widened):
    inverse = lax.rsqrt(jnp.mean(widened * widened, axis=-1, keepdims=True) + epsilon)
    return inverse, widened * inverse


def norm_backward(incoming, inverse, unit_rows, gain):
    scaled = incoming * gain
    return inverse * (scaled - unit_rows * jnp.mean(scaled * unit_rows, axis=-1, keepdims=True))


def spread(rows, factor):
    width = rows.shape[-1]
    owner = lax.broadcasted_iota(jnp.int32, (1, width), 1) // (width // HEADS)
    return jnp.concatenate(
        [rows * jnp.where(owner == h, factor, 0.0).astype(rows.dtype) for h in range(HEADS)], axis=0
    )


def own_channels(stacked, rows):
    width = stacked.shape[-1]
    owner = lax.broadcasted_iota(jnp.int32, (1, width), 1) // (width // HEADS)
    result = stacked[:rows]
    for h in range(1, HEADS):
        result = jnp.where(owner == h, stacked[h * rows : (h + 1) * rows], result)
    return result


def head_probs(scores, allowed):
    rows = scores.shape[0] // HEADS
    probs = []
    for h in range(HEADS):
        s = scores[h * rows : (h + 1) * rows]
        if allowed is not None:
            s = jnp.where(allowed, s, masked_score)
        e = jnp.exp(s - jnp.max(s, axis=-1, keepdims=True))
        probs.append(e * (1.0 / jnp.sum(e, axis=-1, keepdims=True)))
    return probs


def head_grads(probs, grad_probs, scale):
    rows = grad_probs.shape[0] // HEADS
    grad_scores = []
    for h in range(HEADS):
        gp = grad_probs[h * rows : (h + 1) * rows]
        row_dot = jnp.sum(gp * probs[h], axis=-1, keepdims=True)
        grad_scores.append((probs[h] * (gp - row_dot) * scale).astype(bf16))
    return jnp.concatenate(grad_scores, axis=0)


def stacked_low(probs):
    return jnp.concatenate([p.astype(bf16) for p in probs], axis=0)


def slot_of(position, back, freq):
    return lax.rem(position - back + freq, freq)


def pick_kernel(x_hbm, out_ref, sems):
    freq = x_hbm.shape[0]
    place = lax.axis_index("freq")
    copies = [
        pltpu.make_async_copy(x_hbm.at[lax.rem(place + j, freq)], out_ref.at[j - 1], sems.at[j - 1])
        for j in range(1, freq)
    ]
    for copy in copies:
        copy.start()
    for copy in copies:
        copy.wait()


def pick_others(features):
    freq = features.shape[0]
    return pl.pallas_call(
        pick_kernel,
        in_specs=[pl.BlockSpec(memory_space=pltpu.HBM)],
        out_specs=pl.BlockSpec(memory_space=pltpu.VMEM),
        out_shape=pltpu.VMEM((freq - 1,) + features.shape[1:], bf16),
        scratch_shapes=[pltpu.SemaphoreType.DMA((freq - 1,))],
        name="pick_others",
    )(far(features))


def freq_forward_kernel(
    place_ref, own_ref, others_ref, w_ref, gain_ref, q_ref, k_ref, v_ref, o_ref, p_ref, h_hbm,
    hold, low, sem
):
    step = pl.program_id(0)
    freq, bins_dev, width = others_ref.shape[0] + 1, own_ref.shape[2], own_ref.shape[3]
    bins_time = hold.shape[2] // pl.num_programs(0)
    x = joined(own_ref.at[0, 0], others_ref.at[:, 0])
    _, unit = norm_parts(x)
    n = (unit * gain_ref[0:1, :]).astype(bf16)
    scale = (width // HEADS) ** (-0.5)
    q = dot(n, w_ref[0]).astype(bf16)
    k = dot(n, w_ref[1]).astype(bf16)
    v = dot(n, w_ref[2]).astype(bf16)
    probs = head_probs(dot_nt(spread(q, scale), k), None)
    o = own_channels(dot(stacked_low(probs), v), n.shape[0]).astype(bf16)
    hidden = x + dot(o, w_ref[3])
    q_ref[0] = q
    k_ref[0] = k
    v_ref[0] = v
    o_ref[0] = o
    for h in range(HEADS):
        p_ref[0, h] = probs[h].astype(bf16)
    rows = pl.ds(pl.multiple_of(step * bins_time, bins_time), bins_time)
    for f in range(freq):
        part = hidden[f * bins_dev : (f + 1) * bins_dev].reshape(-1, bins_time, width)
        hold[:, slot_of(place_ref[0], f, freq), rows, :] = part

    @pl.when(step == pl.num_programs(0) - 1)
    def _():
        low[...] = hold[...].astype(bf16)
        copy = pltpu.make_async_copy(low, h_hbm, sem)
        copy.start()
        copy.wait()


def joined(own_ref, others_ref):
    width = own_ref.shape[-1]
    return jnp.concatenate(
        [own_ref[...].reshape(-1, width), others_ref[...].reshape(-1, width)], axis=0
    ).astype(f32)


def near(array):
    return pltpu.with_memory_space_constraint(array, pltpu.VMEM)


def far(array):
    return pltpu.with_memory_space_constraint(array, pltpu.HBM)


def frame_specs(freq, bins_dev, width, count=1):
    own = pl.BlockSpec((1, count, bins_dev, width), lambda i, place: (place[0], i, 0, 0))
    others = pl.BlockSpec((freq - 1, count, bins_dev, width), lambda i, place: (0, i, 0, 0))
    rows = pl.BlockSpec((count, freq * bins_dev, width), lambda i, place: (i, 0, 0))
    return own, others, rows


def fixed(shape):
    return pl.BlockSpec(shape, lambda i, place: (0,) * len(shape))


def freq_forward(place, features, others, weights, gains, group):
    freq, frames, bins_dev, width = features.shape
    bins = freq * bins_dev
    rows = frames * (bins_dev // group)
    own_spec, others_spec, row_spec = frame_specs(freq, bins_dev, width)
    rowshape = pltpu.HBM((frames, bins, width), bf16)
    whole = (group, freq, rows, width)
    flops = frames * 2 * bins * (4 * width * width + 2 * HEADS * bins * width)
    return pl.pallas_call(
        freq_forward_kernel,
        grid_spec=pltpu.PrefetchScalarGridSpec(
            num_scalar_prefetch=1,
            grid=(frames,),
            in_specs=[own_spec, others_spec, fixed(weights.shape), fixed(gains.shape)],
            out_specs=[row_spec] * 4
            + [
                pl.BlockSpec((1, HEADS, bins, bins), lambda i, place: (i, 0, 0, 0)),
                pl.BlockSpec(memory_space=pltpu.HBM),
            ],
            scratch_shapes=[
                pltpu.VMEM(whole, f32),
                pltpu.VMEM(whole, bf16),
                pltpu.SemaphoreType.DMA,
            ],
        ),
        out_shape=[rowshape] * 4
        + [pltpu.HBM((frames, HEADS, bins, bins), bf16), pltpu.HBM(whole, bf16)],
        compiler_params=pltpu.CompilerParams(vmem_limit_bytes=VMEM_LIMIT),
        cost_estimate=pl.CostEstimate(
            flops=flops * FORWARD_WEIGHT,
            bytes_accessed=2 * 1024 * 1024,
            transcendentals=frames * HEADS * bins * bins,
        ),
        name="freq_forward",
    )(place, features, near(others), near(weights), gains)


def freq_backward_kernel(
    place_ref, x_hbm, others_hbm, q_hbm, k_hbm, v_hbm, o_hbm, p_hbm, gh_ref, w_ref, gain_ref,
    time_dg_ref, gown_ref, gothers_ref, kept_ref, sent_ref, gains_ref,
    own_ref, others_ref, q_ref, k_ref, v_ref, o_ref, p_ref, hold, total, sems
):
    frames, bins_dev, width = own_ref.shape
    freq = others_ref.shape[0] + 1
    bins_time = bins_dev // hold.shape[0]
    scale = (width // HEADS) ** (-0.5)
    gain = gain_ref[0:1, :]
    loads = {}
    for name, source, target in (
        ("v", v_hbm, v_ref),
        ("p", p_hbm, p_ref),
        ("k", k_hbm, k_ref),
        ("q", q_hbm, q_ref),
        ("own", x_hbm.at[place_ref[0]], own_ref),
        ("others", others_hbm, others_ref),
        ("o", o_hbm, o_ref),
    ):
        loads[name] = pltpu.make_async_copy(source, target, sems.at[len(loads)])
        loads[name].start()
    hold[...] = gh_ref[...].astype(f32)
    first = []
    for f in range(frames):
        grad_hidden = grad_hidden_rows(place_ref, hold, f, freq, bins_time)
        low = grad_hidden.astype(bf16)
        out_spread = spread(dot_nt(low, w_ref[3]).astype(bf16), 1.0)
        first.append((grad_hidden, low, out_spread))
    loads["v"].wait()
    first = [parts + (dot_nt(parts[2], v_ref[f]),) for f, parts in enumerate(first)]
    loads["p"].wait()
    second = []
    for f, (_, _, out_spread, grad_probs) in enumerate(first):
        probs = [p_ref[f, h].astype(f32) for h in range(HEADS)]
        g_v = dot_tn(p_ref[f].reshape(-1, p_ref.shape[3]), out_spread).astype(bf16)
        second.append((g_v, head_grads(probs, grad_probs, scale)))
    for name in ("k", "q", "own", "others", "o"):
        loads[name].wait()
    third = []
    for f, (g_v, grad_scores) in enumerate(second):
        g_q = own_channels(dot(grad_scores, k_ref[f]), freq * bins_dev).astype(bf16)
        g_k = dot_tn(grad_scores, spread(q_ref[f], 1.0)).astype(bf16)
        third.append((g_q, g_k, g_v))
    gains_ref[...] = jnp.zeros_like(gains_ref)
    for f, ((grad_hidden, low, _, _), (g_q, g_k, g_v)) in enumerate(zip(first, third)):
        inverse, unit = norm_parts(joined(own_ref.at[f], others_ref.at[:, f]))
        n = (unit * gain).astype(bf16)
        parts = (dot_tn(n, g_q), dot_tn(n, g_k), dot_tn(n, g_v), dot_tn(o_ref[f], low))
        for m, part in enumerate(parts):
            total[m] = part if f == 0 else total[m] + part
        g_n = dot_nt(g_q, w_ref[0]) + dot_nt(g_k, w_ref[1]) + dot_nt(g_v, w_ref[2])
        grad_x = (grad_hidden + norm_backward(g_n, inverse, unit, gain)).astype(bf16)
        gown_ref[f] = grad_x[:bins_dev]
        gothers_ref[:, f] = grad_x[bins_dev:].reshape(freq - 1, bins_dev, width)
        gains_ref[0:1] += jnp.sum(g_n * unit, axis=0, keepdims=True)
    gains_ref[1:2] = time_dg_ref[...]
    gains = gains_ref[0:2]
    high = gains.astype(bf16).astype(f32)
    gains_ref[0:2] = high
    gains_ref[2:4] = gains - high
    matrices = kept_ref.shape[0]
    kept_ref[...] = total[pl.ds(place_ref[1] * matrices, matrices)].astype(bf16)
    sent = total[pl.ds((1 - place_ref[1]) * matrices, matrices)].reshape(-1, width)
    sent_ref[...] = jnp.concatenate([sent, gains_ref[...]], axis=0).astype(bf16)


def put_halves(core, total, kept_ref, sent_ref):
    half = kept_ref.shape[0]
    kept_ref[...] = total[pl.ds(core * half, half)].astype(bf16)
    sent_ref[...] = total[pl.ds((1 - core) * half, half)].astype(bf16)


def grad_hidden_rows(place_ref, hold, frame, freq, bins_time):
    width = hold.shape[-1]
    rows = pl.ds(frame * bins_time, bins_time)
    return jnp.concatenate(
        [hold[:, slot_of(place_ref[0], f, freq), rows, :].reshape(-1, width) for f in range(freq)],
        axis=0,
    )


def freq_backward(
    place, features, others, q, k, v, o, probs, grad_hidden, weights, gains, time_dg
):
    freq, frames, bins_dev, width = features.shape
    bins = freq * bins_dev
    flops = frames * 2 * bins * (8 * width * width + 4 * HEADS * bins * width)
    half = (2, width, width)
    vmem = pl.BlockSpec(memory_space=pltpu.VMEM)
    hbm = pl.BlockSpec(memory_space=pltpu.HBM)
    rows = pltpu.VMEM((frames, bins, width), bf16)
    return pl.pallas_call(
        freq_backward_kernel,
        in_specs=[pl.BlockSpec(memory_space=pltpu.SMEM)] + [hbm] * 7 + [vmem] * 4,
        out_specs=[vmem] * 5,
        out_shape=[
            pltpu.VMEM((frames, bins_dev, width), bf16),
            pltpu.VMEM(others.shape, bf16),
            pltpu.VMEM(half, bf16),
            pltpu.VMEM((2 * width + GAIN_ROWS, width), bf16),
            pltpu.VMEM((GAIN_ROWS, width), f32),
        ],
        scratch_shapes=[
            pltpu.VMEM((frames, bins_dev, width), bf16),
            pltpu.VMEM(others.shape, bf16),
            rows,
            rows,
            rows,
            rows,
            pltpu.VMEM(probs.shape, bf16),
            pltpu.VMEM(grad_hidden.shape, f32),
            pltpu.VMEM((4, width, width), f32),
            pltpu.SemaphoreType.DMA((7,)),
        ],
        compiler_params=pltpu.CompilerParams(vmem_limit_bytes=VMEM_LIMIT),
        cost_estimate=pl.CostEstimate(
            flops=flops, bytes_accessed=8 * 1024 * 1024, transcendentals=0
        ),
        name="freq_backward",
    )(
        place, *map(far, (features, others, q, k, v, o, probs)), near(grad_hidden),
        near(weights), gains, time_dg,
    )


def time_kernel(
    bins, own_start, total_frames, place_ref, first_ref, h_ref, up_ref, w_ref, gain_ref,
    gh_hbm, kept_ref, sent_ref, dg_ref,
    gh_ref, total, q_s, k_s, v_s, go_s, o_s, gq_s, gk_s, gv_s, sems
):
    span_rows, width = h_ref.shape
    span = span_rows // bins
    own_rows = gh_ref.shape[0]
    own = own_rows // bins
    scale = (width // HEADS) ** (-0.5)
    gain = gain_ref[1:2, :]
    chunk = own_rows
    while chunk > 256 and chunk % 32 == 0:
        chunk //= 2
    chunks = span_rows // chunk

    for i in range(chunks):
        rows = pl.ds(i * chunk, chunk)
        _, unit = norm_parts(h_ref[rows, :].astype(f32))
        n = (unit * gain).astype(bf16)
        put(q_s, rows, dot(n, w_ref[0]))
        put(k_s, rows, dot(n, w_ref[1]))
        put(v_s, rows, dot(n, w_ref[2]))
    for i in range(chunks):
        rows = pl.ds(i * chunk, chunk)
        put(go_s, rows, dot_nt(up_ref[rows, :], w_ref[3]))

    query = lax.broadcasted_iota(jnp.int32, (span, span), 0)
    key = lax.broadcasted_iota(jnp.int32, (span, span), 1)
    distance = key - query
    allowed = (distance >= -(WINDOW // 2)) & (distance < WINDOW // 2)
    if own != span:
        frame = first_ref[0] + key
        allowed = allowed & (frame >= 0) & (frame < total_frames)

    together = max(n for n in (1, 2, 4) if bins % n == 0 and (n == 1 or n * span <= 512))

    def some_bins(start):
        places = [pl.ds(start + b, span, stride=bins) for b in range(together)]
        first = []
        for rows in places:
            q, k, v, grad_out = (get(ref, rows).astype(bf16) for ref in (q_s, k_s, v_s, go_s))
            out_spread = spread(grad_out, 1.0)
            first.append((q, k, v, out_spread, dot_nt(spread(q, scale), k), dot_nt(out_spread, v)))
        second = []
        for q, k, v, out_spread, scores, grad_probs in first:
            probs = head_probs(scores, allowed)
            second.append((stacked_low(probs), head_grads(probs, grad_probs, scale)))
        for rows, (q, k, v, out_spread, _, _), (low, grad_scores) in zip(places, first, second):
            put(o_s, rows, own_channels(dot(low, v), span))
            put(gq_s, rows, own_channels(dot(grad_scores, k), span))
            put(gk_s, rows, dot_tn(grad_scores, spread(q, 1.0)))
            put(gv_s, rows, dot_tn(low, out_spread))

    for start in range(0, bins, together):
        some_bins(start)

    dg_ref[...] = jnp.zeros_like(dg_ref)
    stores = []
    for i in range(own_rows // chunk):
        mine = pl.ds(i * chunk, chunk)
        rows = pl.ds(own_start + i * chunk, chunk)
        g_q = get(gq_s, rows).astype(bf16)
        g_k = get(gk_s, rows).astype(bf16)
        g_v = get(gv_s, rows).astype(bf16)
        g_n = dot_nt(g_q, w_ref[0]) + dot_nt(g_k, w_ref[1]) + dot_nt(g_v, w_ref[2])
        inverse, unit = norm_parts(h_ref[rows, :].astype(f32))
        n = (unit * gain).astype(bf16)
        up = up_ref[rows, :]
        grad_hidden = up.astype(f32) + norm_backward(g_n, inverse, unit, gain)
        gh_ref[mine, :] = grad_hidden.astype(bf16)
        stores.append(pltpu.make_async_copy(gh_ref.at[mine], gh_hbm.at[mine], sems.at[3 + i]))
        stores[-1].start()
        dg_ref[...] += jnp.sum(g_n * unit, axis=0, keepdims=True)
        parts = (dot_tn(n, g_q), dot_tn(n, g_k), dot_tn(n, g_v), dot_tn(get(o_s, rows).astype(bf16), up))
        for m, part in enumerate(parts):
            total[m] = part if i == 0 else total[m] + part
    put_halves(place_ref[1], total, kept_ref, sent_ref)
    for store in stores:
        store.wait()


def time_attention(place, first, hidden, upstream, weights, gains, bins, own_start, own_rows, total):
    span_rows, width = hidden.shape
    vmem = pl.BlockSpec(memory_space=pltpu.VMEM)
    hbm = pl.BlockSpec(memory_space=pltpu.HBM)
    smem = pl.BlockSpec(memory_space=pltpu.SMEM)
    span = span_rows // bins
    flops = 2 * span_rows * (11 * width * width + 6 * HEADS * span * width)
    return pl.pallas_call(
        functools.partial(time_kernel, bins, own_start, total),
        in_specs=[smem, smem, vmem, vmem, vmem, vmem],
        out_specs=[hbm] + [vmem] * 3,
        out_shape=[pltpu.HBM((own_rows, width), bf16)]
        + [pltpu.VMEM((2, width, width), bf16)] * 2
        + [jax.ShapeDtypeStruct((1, width), f32)],
        scratch_shapes=[
            pltpu.VMEM((own_rows, width), bf16),
            pltpu.VMEM((4, width, width), f32),
        ]
        + [pltpu.VMEM((width // LANES, span_rows, LANES), f32)] * 8
        + [pltpu.SemaphoreType.DMA((16,))],
        compiler_params=pltpu.CompilerParams(vmem_limit_bytes=VMEM_LIMIT),
        cost_estimate=pl.CostEstimate(
            flops=flops,
            bytes_accessed=4 * 1024 * 1024,
            transcendentals=bins * HEADS * span * span,
        ),
        name="time_attention",
    )(place, first, near(hidden), near(upstream), near(weights), gains)


def sums_kernel(kept_ref, arrived_ref, time_ref, gains_ref, out_ref):
    peers, _, width = out_ref.shape
    arrived = arrived_ref[...].astype(f32)
    rows = arrived.shape[0] - gains_ref.shape[0]
    total = kept_ref[...].astype(f32).reshape(rows, width) + arrived[:rows]
    gains = jnp.concatenate([gains_ref[0:4], arrived[rows : rows + 4]], axis=0)
    parts = [
        total.reshape(peers, -1, width),
        time_ref[...].astype(f32).reshape(peers, -1, width),
        jnp.broadcast_to(gains[None], (peers,) + gains.shape),
    ]
    out_ref[...] = jnp.concatenate(parts, axis=1).astype(bf16)


def sums_by_peer(kept, arrived, time_rows, gains, peers):
    width = kept.shape[-1]
    freq_count = kept.size // (peers * width)
    time_count = time_rows.size // (peers * width)
    if freq_count % 8 or time_count % 8:
        rows = 2 * width
        total = kept.astype(f32).reshape(rows, width) + arrived[:rows].astype(f32)
        gains = jnp.concatenate([gains[:4].astype(bf16), arrived[rows : rows + 4]], axis=0)
        parts = [
            total.astype(bf16).reshape(peers, -1, width),
            time_rows.reshape(peers, -1, width),
            jnp.broadcast_to(gains[None], (peers,) + gains.shape),
        ]
        return jnp.concatenate(parts, axis=1), freq_count, time_count
    vmem = pl.BlockSpec(memory_space=pltpu.VMEM)
    sums = pl.pallas_call(
        sums_kernel,
        in_specs=[vmem] * 4,
        out_specs=vmem,
        out_shape=pltpu.HBM((peers, freq_count + time_count + 8, width), bf16),
        compiler_params=pltpu.CompilerParams(vmem_limit_bytes=VMEM_LIMIT),
        cost_estimate=pl.CostEstimate(
            flops=kept.size, bytes_accessed=6 * kept.size, transcendentals=0
        ),
        name="sums_by_peer",
    )(kept, arrived, time_rows, gains)
    return sums, freq_count, time_count


def group_size(devices, bins_dev):
    best = 1
    for size in range(1, devices + 1):
        if devices % size == 0 and bins_dev % (8 * size) == 0:
            best = size
    return best


def per_device(features, upstream, weights, gains):
    frames_dev, bins_dev, width = features.shape
    tm, freq = lax.axis_size("tm"), lax.axis_size("freq")
    total_frames = frames_dev * tm
    frames = frames_dev // freq
    group = group_size(tm, bins_dev)
    bins_time = bins_dev // group
    group_frames = group * frames_dev
    whole = group == tm
    sides = 0 if whole else -(-WINDOW // group_frames)
    groups = (
        None
        if whole
        else [list(range(g * group, (g + 1) * group)) for g in range(tm // group)]
    )

    def over_tm(blocks):
        return lax.all_to_all(blocks, "tm", 0, 0, tiled=True, axis_index_groups=groups)

    def over_all(blocks):
        if whole:
            flat = blocks.reshape((tm * freq,) + blocks.shape[2:])
            return lax.all_to_all(flat, ("tm", "freq"), 0, 0, tiled=True).reshape(blocks.shape)
        return over_tm(lax.all_to_all(blocks, "freq", 1, 1, tiled=True))

    def with_sides(rows):
        parts = [rows]
        for away in range(1, sides + 1):
            shift = away * group
            before = lax.ppermute(rows, "tm", [(i, i + shift) for i in range(tm - shift)])
            after = lax.ppermute(rows, "tm", [(i + shift, i) for i in range(tm - shift)])
            parts = [before] + parts + [after]
        return jnp.concatenate(parts, axis=0) if sides else rows

    core = lax.axis_index("tm") % 2
    place = jnp.stack([lax.axis_index("freq"), core]).astype(jnp.int32)
    by_target = features.reshape(freq, frames, bins_dev, width)

    def along_freq(block, steps):
        return lax.ppermute(block, "freq", [(i, (i + steps) % freq) for i in range(freq)])

    picked = pick_others(by_target)
    others = jnp.stack(
        [
            along_freq(picked[j - 1], j) for j in range(1, freq)
        ]
    )
    up_blocks = jnp.swapaxes(upstream.reshape(frames_dev, group, bins_time, width), 0, 1)
    up_rows = over_tm(up_blocks).reshape(-1, width)
    freq_w = weights[:4]
    q, k, v, o, probs, hidden_blocks = freq_forward(place, by_target, others, freq_w, gains, group)
    time_w, hidden_blocks = lax.optimization_barrier((weights, hidden_blocks))
    time_w = time_w[4:]
    hidden_rows = over_all(hidden_blocks).reshape(-1, width)
    own_rows = hidden_rows.shape[0]
    position = lax.axis_index("tm") // group
    first = ((position - sides) * group_frames).astype(jnp.int32).reshape(1)
    grad_rows, time_kept, time_sent, time_dg = time_attention(
        place,
        first,
        with_sides(hidden_rows),
        with_sides(up_rows),
        time_w,
        gains,
        bins_time,
        sides * own_rows,
        own_rows,
        total_frames,
    )
    grad_hidden = over_all(grad_rows.reshape(hidden_blocks.shape))

    pairs = [(i, i ^ 1) for i in range(tm)]
    same = [
        [t * freq + f for t in range(c, tm, 2) for f in range(freq)] for c in range(2)
    ]
    peers = len(same[0])

    rows = 2 * width
    sets = 2 * freq
    halved = tm % 4 == 0 and freq & (freq - 1) == 0 and rows % (8 * sets * peers) == 0
    steps = [("tm", 1)] + [("freq", k) for k in reversed(range(freq.bit_length() - 1))]
    if not halved:
        sets, steps = 1, []

    def scattered(partial):
        partial = partial.reshape((2,) * len(steps) + (-1, width))
        for axis, k in steps:
            mine = (lax.axis_index(axis) >> k) & 1
            sent = lax.dynamic_index_in_dim(partial, 1 - mine, 0, False)
            kept = lax.dynamic_index_in_dim(partial, mine, 0, False)
            devices = range(lax.axis_size(axis))
            came = lax.ppermute(sent, axis, [(d, d ^ (1 << k)) for d in devices])
            partial = (kept.astype(f32) + came.astype(f32)).astype(bf16)
        return partial

    def over_same(blocks):
        return lax.all_to_all(
            blocks, ("tm", "freq"), 0, 0, tiled=True, axis_index_groups=same
        )

    time_arrived = lax.ppermute(time_sent, "tm", pairs)
    time_rows = scattered((time_kept.astype(f32) + time_arrived.astype(f32)).astype(bf16))
    grad_own, grad_others, freq_kept, freq_sent, own_gains = freq_backward(
        place, by_target, others, q, k, v, o, probs, grad_hidden, freq_w, gains, time_dg
    )
    freq_arrived = lax.ppermute(freq_sent, "tm", pairs)
    sums, freq_count, time_count = sums_by_peer(
        freq_kept, freq_arrived, time_rows, own_gains, peers
    )
    arrived = over_same(sums)
    returned = [grad_own] + [along_freq(grad_others[j - 1], -j) for j in range(1, freq)]
    returned, arrived = lax.optimization_barrier((returned, arrived))
    grad_input = jnp.roll(jnp.stack(returned), place[0], axis=0).reshape(features.shape)

    inv_root = (total_frames * bins_dev * freq) ** (-0.5)
    summed = jnp.sum(arrived.astype(f32), axis=0) * inv_root
    gain_sum = summed[freq_count + time_count :]
    time_arrived = arrived[:, freq_count : freq_count + time_count].astype(f32)
    time_sum = jnp.sum(time_arrived.reshape(-1, sets, time_count, width), axis=0) * inv_root
    block = jnp.concatenate([summed[:freq_count], time_sum.reshape(-1, width)], axis=0)
    block, gain_sum = lax.optimization_barrier((block.astype(bf16), gain_sum))
    gathered = over_same(jnp.broadcast_to(block[None], (peers,) + block.shape))
    gathered, gain_sum = lax.optimization_barrier((gathered, gain_sum))
    gain_grads = jnp.sum(gain_sum.reshape(4, 2, width), axis=0)
    theirs = lax.ppermute(gathered, "tm", pairs)
    first_core = core == 0
    halves = jnp.stack(
        [jnp.where(first_core, gathered, theirs), jnp.where(first_core, theirs, gathered)]
    )
    freq_grads = halves[:, :, :freq_count].reshape(4, width, width)
    time_grads = halves[:, :, freq_count:].reshape(2, peers, sets, time_count, width)
    time_grads = jnp.swapaxes(time_grads, 1, 2).reshape(4, width, width)
    weight_grads = jnp.concatenate([freq_grads, time_grads], axis=0).astype(f32)
    return (grad_input, weight_grads, gain_grads)


def solution(mesh):
    return jax.shard_map(
        per_device,
        mesh=mesh,
        in_specs=(P("tm", "freq", None), P("tm", "freq", None), P(), P()),
        out_specs=(P("tm", "freq", None), P(), P()),
        check_vma=False,
    )
```

```python
import functools

import jax
import jax.numpy as jnp
from jax import lax
from jax.experimental import pallas as pl
from jax.experimental.pallas import tpu as pltpu
from jax.sharding import PartitionSpec as P

HEADS = 4
WINDOW = 128

epsilon = 1e-06
masked_score = -1e30

f32 = jnp.float32
bf16 = jnp.bfloat16
LANES = 128
GAIN_ROWS = 16
MIB = 1024 * 1024
VMEM_LIMIT = 24 * MIB
FORWARD_WEIGHT = 40
PLACE_FLOPS = 10_000_000_000

CONTRACT_LAST = (((1,), (1,)), ((), ()))
CONTRACT_FIRST = (((0,), (0,)), ((), ()))


def dot(left, right):
    return jnp.dot(left, right, preferred_element_type=f32)


def dot_nt(left, right):
    return lax.dot_general(left, right, CONTRACT_LAST, preferred_element_type=f32)


def dot_tn(left, right):
    return lax.dot_general(left, right, CONTRACT_FIRST, preferred_element_type=f32)


def put(ref, rows, value):
    for c in range(ref.shape[0]):
        ref[c, rows, :] = value[:, c * LANES : (c + 1) * LANES]


def get(ref, rows):
    return jnp.concatenate([ref[c, rows, :] for c in range(ref.shape[0])], axis=1)


def norm_parts(widened):
    inverse = lax.rsqrt(jnp.mean(widened * widened, axis=-1, keepdims=True) + epsilon)
    return inverse, widened * inverse


def norm_backward(incoming, inverse, unit_rows, gain):
    scaled = incoming * gain
    return inverse * (scaled - unit_rows * jnp.mean(scaled * unit_rows, axis=-1, keepdims=True))


def spread(rows, factor):
    width = rows.shape[-1]
    owner = lax.broadcasted_iota(jnp.int32, (1, width), 1) // (width // HEADS)
    return jnp.concatenate(
        [rows * jnp.where(owner == h, factor, 0.0).astype(rows.dtype) for h in range(HEADS)], axis=0
    )


def own_channels(stacked, rows):
    width = stacked.shape[-1]
    owner = lax.broadcasted_iota(jnp.int32, (1, width), 1) // (width // HEADS)
    result = stacked[:rows]
    for h in range(1, HEADS):
        result = jnp.where(owner == h, stacked[h * rows : (h + 1) * rows], result)
    return result


def head_probs(scores, allowed):
    rows = scores.shape[0] // HEADS
    probs = []
    for h in range(HEADS):
        s = scores[h * rows : (h + 1) * rows]
        if allowed is not None:
            s = jnp.where(allowed, s, masked_score)
        e = jnp.exp(s - jnp.max(s, axis=-1, keepdims=True))
        probs.append(e * (1.0 / jnp.sum(e, axis=-1, keepdims=True)))
    return probs


def head_grads(probs, grad_probs, scale):
    rows = grad_probs.shape[0] // HEADS
    grad_scores = []
    for h in range(HEADS):
        gp = grad_probs[h * rows : (h + 1) * rows]
        row_dot = jnp.sum(gp * probs[h], axis=-1, keepdims=True)
        grad_scores.append((probs[h] * (gp - row_dot) * scale).astype(bf16))
    return jnp.concatenate(grad_scores, axis=0)


def stacked_low(probs):
    return jnp.concatenate([p.astype(bf16) for p in probs], axis=0)


def slot_of(position, back, freq):
    return lax.rem(position - back + freq, freq)


def pick_kernel(x_hbm, out_ref, sems):
    freq = x_hbm.shape[0]
    place = lax.axis_index("freq")
    copies = [
        pltpu.make_async_copy(x_hbm.at[lax.rem(place + j, freq)], out_ref.at[j - 1], sems.at[j - 1])
        for j in range(1, freq)
    ]
    for copy in copies:
        copy.start()
    for copy in copies:
        copy.wait()


def pick_others(features):
    freq = features.shape[0]
    return pl.pallas_call(
        pick_kernel,
        in_specs=[pl.BlockSpec(memory_space=pltpu.HBM)],
        out_specs=pl.BlockSpec(memory_space=pltpu.VMEM),
        out_shape=pltpu.VMEM((freq - 1,) + features.shape[1:], bf16),
        scratch_shapes=[pltpu.SemaphoreType.DMA((freq - 1,))],
        name="pick_others",
    )(far(features))


def freq_forward_kernel(
    place_ref, x_hbm, others_ref, w_ref, gain_ref,
    q_hbm, k_hbm, v_hbm, o_hbm, p_hbm, h_hbm,
    own_ref, q_ref, k_ref, v_ref, o_ref, p_ref, hold, h_low, load_sem, sems
):
    frames, bins_dev, width = own_ref.shape
    freq = others_ref.shape[0] + 1
    bins_time = hold.shape[2] // frames
    scale = (width // HEADS) ** (-0.5)
    stores = []

    def store(source, target):
        stores.append(pltpu.make_async_copy(source, target, sems.at[len(stores)]))
        stores[-1].start()

    load = pltpu.make_async_copy(x_hbm.at[place_ref[0]], own_ref, load_sem)
    load.start()
    load.wait()
    first = []
    for f in range(frames):
        _, unit = norm_parts(joined(own_ref.at[f], others_ref.at[:, f]))
        n = (unit * gain_ref[0:1, :]).astype(bf16)
        q = dot(n, w_ref[0]).astype(bf16)
        k = dot(n, w_ref[1]).astype(bf16)
        v = dot(n, w_ref[2]).astype(bf16)
        q_ref[f] = q
        k_ref[f] = k
        v_ref[f] = v
        first.append((v, dot_nt(spread(q, scale), k)))
    store(q_ref, q_hbm)
    store(k_ref, k_hbm)
    store(v_ref, v_hbm)
    second = []
    for f, (v, scores) in enumerate(first):
        low = stacked_low(head_probs(scores, None))
        p_ref[f] = low.reshape(p_ref.shape[1:])
        store(p_ref.at[f], p_hbm.at[f])
        second.append(own_channels(dot(low, v), v.shape[0]).astype(bf16))
    for f, o in enumerate(second):
        o_ref[f] = o
        hidden = joined(own_ref.at[f], others_ref.at[:, f]) + dot(o, w_ref[3])
        rows = pl.ds(f * bins_time, bins_time)
        for j in range(freq):
            part = hidden[j * bins_dev : (j + 1) * bins_dev].reshape(-1, bins_time, width)
            hold[:, slot_of(place_ref[0], j, freq), rows, :] = part
    store(o_ref, o_hbm)
    h_low[...] = hold[...].astype(bf16)
    store(h_low, h_hbm)
    for copy in stores:
        copy.wait()


def joined(own_ref, others_ref):
    width = own_ref.shape[-1]
    return jnp.concatenate(
        [own_ref[...].reshape(-1, width), others_ref[...].reshape(-1, width)], axis=0
    ).astype(f32)


def near(array):
    return pltpu.with_memory_space_constraint(array, pltpu.VMEM)


def far(array):
    return pltpu.with_memory_space_constraint(array, pltpu.HBM)


def freq_forward(place, features, others, weights, gains, group):
    freq, frames, bins_dev, width = features.shape
    bins = freq * bins_dev
    whole = (group, freq, frames * (bins_dev // group), width)
    probs = (frames, HEADS, bins, bins)
    rows = (frames, bins, width)
    flops = frames * 2 * bins * (4 * width * width + 2 * HEADS * bins * width)
    vmem = pl.BlockSpec(memory_space=pltpu.VMEM)
    hbm = pl.BlockSpec(memory_space=pltpu.HBM)
    return pl.pallas_call(
        freq_forward_kernel,
        in_specs=[pl.BlockSpec(memory_space=pltpu.SMEM), hbm, vmem, vmem, vmem],
        out_specs=[hbm] * 6,
        out_shape=[pltpu.HBM(rows, bf16)] * 4 + [pltpu.HBM(probs, bf16), pltpu.HBM(whole, bf16)],
        scratch_shapes=[pltpu.VMEM((frames, bins_dev, width), bf16)]
        + [pltpu.VMEM(rows, bf16)] * 4
        + [
            pltpu.VMEM(probs, bf16),
            pltpu.VMEM(whole, f32),
            pltpu.VMEM(whole, bf16),
            pltpu.SemaphoreType.DMA,
            pltpu.SemaphoreType.DMA((frames + 5,)),
        ],
        compiler_params=pltpu.CompilerParams(vmem_limit_bytes=VMEM_LIMIT),
        cost_estimate=pl.CostEstimate(
            flops=flops * FORWARD_WEIGHT,
            bytes_accessed=2 * 1024 * 1024,
            transcendentals=frames * HEADS * bins * bins,
        ),
        name="freq_forward",
    )(place, far(features), near(others), near(weights), gains)


def freq_backward_kernel(
    place_ref, x_hbm, others_hbm, q_hbm, k_hbm, v_hbm, o_hbm, p_hbm, gh_ref, w_ref, gain_ref,
    time_dg_ref, gown_ref, gothers_ref, kept_ref, sent_ref, gains_ref,
    own_ref, others_ref, q_ref, k_ref, v_ref, o_ref, p_ref, hold, total, sems
):
    frames, bins_dev, width = own_ref.shape
    freq = others_ref.shape[0] + 1
    bins_time = bins_dev // hold.shape[0]
    scale = (width // HEADS) ** (-0.5)
    gain = gain_ref[0:1, :]
    loads = {}
    for name, source, target in (
        ("v", v_hbm, v_ref),
        ("p", p_hbm, p_ref),
        ("k", k_hbm, k_ref),
        ("q", q_hbm, q_ref),
        ("own", x_hbm.at[place_ref[0]], own_ref),
        ("others", others_hbm, others_ref),
        ("o", o_hbm, o_ref),
    ):
        loads[name] = pltpu.make_async_copy(source, target, sems.at[len(loads)])
        loads[name].start()
    hold[...] = gh_ref[...].astype(f32)
    first = []
    for f in range(frames):
        grad_hidden = grad_hidden_rows(place_ref, hold, f, freq, bins_time)
        low = grad_hidden.astype(bf16)
        out_spread = spread(dot_nt(low, w_ref[3]).astype(bf16), 1.0)
        first.append((grad_hidden, low, out_spread))
    loads["v"].wait()
    first = [parts + (dot_nt(parts[2], v_ref[f]),) for f, parts in enumerate(first)]
    loads["p"].wait()
    second = []
    for f, (_, _, out_spread, grad_probs) in enumerate(first):
        probs = [p_ref[f, h].astype(f32) for h in range(HEADS)]
        g_v = dot_tn(p_ref[f].reshape(-1, p_ref.shape[3]), out_spread).astype(bf16)
        second.append((g_v, head_grads(probs, grad_probs, scale)))
    for name in ("k", "q", "own", "others", "o"):
        loads[name].wait()
    third = []
    for f, (g_v, grad_scores) in enumerate(second):
        g_q = own_channels(dot(grad_scores, k_ref[f]), freq * bins_dev).astype(bf16)
        g_k = dot_tn(grad_scores, spread(q_ref[f], 1.0)).astype(bf16)
        third.append((g_q, g_k, g_v))
    gains_ref[...] = jnp.zeros_like(gains_ref)
    for f, ((grad_hidden, low, _, _), (g_q, g_k, g_v)) in enumerate(zip(first, third)):
        inverse, unit = norm_parts(joined(own_ref.at[f], others_ref.at[:, f]))
        n = (unit * gain).astype(bf16)
        parts = (dot_tn(n, g_q), dot_tn(n, g_k), dot_tn(n, g_v), dot_tn(o_ref[f], low))
        for m, part in enumerate(parts):
            total[m] = part if f == 0 else total[m] + part
        g_n = dot_nt(g_q, w_ref[0]) + dot_nt(g_k, w_ref[1]) + dot_nt(g_v, w_ref[2])
        grad_x = (grad_hidden + norm_backward(g_n, inverse, unit, gain)).astype(bf16)
        gown_ref[f] = grad_x[:bins_dev]
        gothers_ref[:, f] = grad_x[bins_dev:].reshape(freq - 1, bins_dev, width)
        gains_ref[0:1] += jnp.sum(g_n * unit, axis=0, keepdims=True)
    gains_ref[1:2] = time_dg_ref[...]
    gains = gains_ref[0:2]
    high = gains.astype(bf16).astype(f32)
    gains_ref[0:2] = high
    gains_ref[2:4] = gains - high
    matrices = kept_ref.shape[0]
    kept_ref[...] = total[pl.ds(place_ref[1] * matrices, matrices)].astype(bf16)
    sent = total[pl.ds((1 - place_ref[1]) * matrices, matrices)].reshape(-1, width)
    sent_ref[...] = jnp.concatenate([sent, gains_ref[...]], axis=0).astype(bf16)


def put_halves(core, total, kept_ref, sent_ref):
    half = kept_ref.shape[0]
    kept_ref[...] = total[pl.ds(core * half, half)].astype(bf16)
    sent_ref[...] = total[pl.ds((1 - core) * half, half)].astype(bf16)


def grad_hidden_rows(place_ref, hold, frame, freq, bins_time):
    width = hold.shape[-1]
    rows = pl.ds(frame * bins_time, bins_time)
    return jnp.concatenate(
        [hold[:, slot_of(place_ref[0], f, freq), rows, :].reshape(-1, width) for f in range(freq)],
        axis=0,
    )


def freq_backward(
    place, features, others, q, k, v, o, probs, grad_hidden, weights, gains, time_dg
):
    freq, frames, bins_dev, width = features.shape
    bins = freq * bins_dev
    flops = frames * 2 * bins * (8 * width * width + 4 * HEADS * bins * width)
    half = (2, width, width)
    vmem = pl.BlockSpec(memory_space=pltpu.VMEM)
    hbm = pl.BlockSpec(memory_space=pltpu.HBM)
    rows = pltpu.VMEM((frames, bins, width), bf16)
    return pl.pallas_call(
        freq_backward_kernel,
        in_specs=[pl.BlockSpec(memory_space=pltpu.SMEM)] + [hbm] * 7 + [vmem] * 4,
        out_specs=[vmem] * 5,
        out_shape=[
            pltpu.VMEM((frames, bins_dev, width), bf16),
            pltpu.VMEM(others.shape, bf16),
            pltpu.VMEM(half, bf16),
            pltpu.VMEM((2 * width + GAIN_ROWS, width), bf16),
            pltpu.VMEM((GAIN_ROWS, width), f32),
        ],
        scratch_shapes=[
            pltpu.VMEM((frames, bins_dev, width), bf16),
            pltpu.VMEM(others.shape, bf16),
            rows,
            rows,
            rows,
            rows,
            pltpu.VMEM(probs.shape, bf16),
            pltpu.VMEM(grad_hidden.shape, f32),
            pltpu.VMEM((4, width, width), f32),
            pltpu.SemaphoreType.DMA((7,)),
        ],
        compiler_params=pltpu.CompilerParams(vmem_limit_bytes=VMEM_LIMIT),
        cost_estimate=pl.CostEstimate(
            flops=flops, bytes_accessed=8 * 1024 * 1024, transcendentals=0
        ),
        name="freq_backward",
    )(
        place, *map(far, (features, others, q, k, v, o, probs)), near(grad_hidden),
        near(weights), gains, time_dg,
    )


def time_kernel(
    bins, own_start, total_frames, place_ref, first_ref, h_ref, up_ref, w_ref, gain_ref,
    gh_hbm, kept_ref, sent_ref, dg_ref,
    gh_ref, total, q_s, k_s, v_s, go_s, o_s, gq_s, gk_s, gv_s, sems
):
    span_rows, width = h_ref.shape
    span = span_rows // bins
    own_rows = gh_ref.shape[0]
    own = own_rows // bins
    scale = (width // HEADS) ** (-0.5)
    gain = gain_ref[1:2, :]
    chunk = own_rows
    while chunk > 256 and chunk % 32 == 0:
        chunk //= 2
    chunks = span_rows // chunk

    for i in range(chunks):
        rows = pl.ds(i * chunk, chunk)
        _, unit = norm_parts(h_ref[rows, :].astype(f32))
        n = (unit * gain).astype(bf16)
        put(q_s, rows, dot(n, w_ref[0]))
        put(k_s, rows, dot(n, w_ref[1]))
        put(v_s, rows, dot(n, w_ref[2]))
    for i in range(chunks):
        rows = pl.ds(i * chunk, chunk)
        put(go_s, rows, dot_nt(up_ref[rows, :], w_ref[3]))

    query = lax.broadcasted_iota(jnp.int32, (span, span), 0)
    key = lax.broadcasted_iota(jnp.int32, (span, span), 1)
    distance = key - query
    allowed = (distance >= -(WINDOW // 2)) & (distance < WINDOW // 2)
    if own != span:
        frame = first_ref[0] + key
        allowed = allowed & (frame >= 0) & (frame < total_frames)

    together = max(n for n in (1, 2, 4) if bins % n == 0 and (n == 1 or n * span <= 512))

    def some_bins(start):
        places = [pl.ds(start + b, span, stride=bins) for b in range(together)]
        first = []
        for rows in places:
            q, k, v, grad_out = (get(ref, rows).astype(bf16) for ref in (q_s, k_s, v_s, go_s))
            out_spread = spread(grad_out, 1.0)
            first.append((q, k, v, out_spread, dot_nt(spread(q, scale), k), dot_nt(out_spread, v)))
        second = []
        for q, k, v, out_spread, scores, grad_probs in first:
            probs = head_probs(scores, allowed)
            second.append((stacked_low(probs), head_grads(probs, grad_probs, scale)))
        for rows, (q, k, v, out_spread, _, _), (low, grad_scores) in zip(places, first, second):
            put(o_s, rows, own_channels(dot(low, v), span))
            put(gq_s, rows, own_channels(dot(grad_scores, k), span))
            put(gk_s, rows, dot_tn(grad_scores, spread(q, 1.0)))
            put(gv_s, rows, dot_tn(low, out_spread))

    for start in range(0, bins, together):
        some_bins(start)

    dg_ref[...] = jnp.zeros_like(dg_ref)
    stores = []
    for i in range(own_rows // chunk):
        mine = pl.ds(i * chunk, chunk)
        rows = pl.ds(own_start + i * chunk, chunk)
        g_q = get(gq_s, rows).astype(bf16)
        g_k = get(gk_s, rows).astype(bf16)
        g_v = get(gv_s, rows).astype(bf16)
        g_n = dot_nt(g_q, w_ref[0]) + dot_nt(g_k, w_ref[1]) + dot_nt(g_v, w_ref[2])
        inverse, unit = norm_parts(h_ref[rows, :].astype(f32))
        n = (unit * gain).astype(bf16)
        up = up_ref[rows, :]
        grad_hidden = up.astype(f32) + norm_backward(g_n, inverse, unit, gain)
        gh_ref[mine, :] = grad_hidden.astype(bf16)
        stores.append(pltpu.make_async_copy(gh_ref.at[mine], gh_hbm.at[mine], sems.at[3 + i]))
        stores[-1].start()
        dg_ref[...] += jnp.sum(g_n * unit, axis=0, keepdims=True)
        parts = (dot_tn(n, g_q), dot_tn(n, g_k), dot_tn(n, g_v), dot_tn(get(o_s, rows).astype(bf16), up))
        for m, part in enumerate(parts):
            total[m] = part if i == 0 else total[m] + part
    put_halves(place_ref[1], total, kept_ref, sent_ref)
    for store in stores:
        store.wait()


def time_attention(place, first, hidden, upstream, weights, gains, bins, own_start, own_rows, total):
    span_rows, width = hidden.shape
    vmem = pl.BlockSpec(memory_space=pltpu.VMEM)
    hbm = pl.BlockSpec(memory_space=pltpu.HBM)
    smem = pl.BlockSpec(memory_space=pltpu.SMEM)
    span = span_rows // bins
    flops = 2 * span_rows * (11 * width * width + 6 * HEADS * span * width)
    return pl.pallas_call(
        functools.partial(time_kernel, bins, own_start, total),
        in_specs=[smem, smem, vmem, vmem, vmem, vmem],
        out_specs=[hbm] + [vmem] * 3,
        out_shape=[pltpu.HBM((own_rows, width), bf16)]
        + [pltpu.VMEM((2, width, width), bf16)] * 2
        + [jax.ShapeDtypeStruct((1, width), f32)],
        scratch_shapes=[
            pltpu.VMEM((own_rows, width), bf16),
            pltpu.VMEM((4, width, width), f32),
        ]
        + [pltpu.VMEM((width // LANES, span_rows, LANES), f32)] * 8
        + [pltpu.SemaphoreType.DMA((16,))],
        compiler_params=pltpu.CompilerParams(vmem_limit_bytes=VMEM_LIMIT),
        cost_estimate=pl.CostEstimate(
            flops=flops,
            bytes_accessed=4 * 1024 * 1024,
            transcendentals=bins * HEADS * span * span,
        ),
        name="time_attention",
    )(place, first, near(hidden), near(upstream), near(weights), gains)


def place_kernel(place_ref, *refs):
    *parts, out_hbm, sems = refs
    freq = len(parts)
    copies = [
        pltpu.make_async_copy(part, out_hbm.at[lax.rem(place_ref[0] + j, freq)], sems.at[j])
        for j, part in enumerate(parts)
    ]
    for copy in copies:
        copy.start()
    for copy in copies:
        copy.wait()


def place_frames(place, parts):
    vmem = pl.BlockSpec(memory_space=pltpu.VMEM)
    return pl.pallas_call(
        place_kernel,
        in_specs=[pl.BlockSpec(memory_space=pltpu.SMEM)] + [vmem] * len(parts),
        out_specs=pl.BlockSpec(memory_space=pltpu.HBM),
        out_shape=pltpu.HBM((len(parts),) + parts[0].shape, bf16),
        scratch_shapes=[pltpu.SemaphoreType.DMA((len(parts),))],
        compiler_params=pltpu.CompilerParams(vmem_limit_bytes=VMEM_LIMIT),
        cost_estimate=pl.CostEstimate(
            flops=PLACE_FLOPS, bytes_accessed=4 * parts[0].size, transcendentals=0
        ),
        name="place_frames",
    )(place, *map(near, parts))


def sums_kernel(kept_ref, arrived_ref, time_ref, gains_ref, out_ref):
    peers, _, width = out_ref.shape
    arrived = arrived_ref[...].astype(f32)
    rows = arrived.shape[0] - gains_ref.shape[0]
    total = kept_ref[...].astype(f32).reshape(rows, width) + arrived[:rows]
    gains = jnp.concatenate([gains_ref[0:4], arrived[rows : rows + 4]], axis=0)
    parts = [
        total.reshape(peers, -1, width),
        time_ref[...].astype(f32).reshape(peers, -1, width),
        jnp.broadcast_to(gains[None], (peers,) + gains.shape),
    ]
    out_ref[...] = jnp.concatenate(parts, axis=1).astype(bf16)


def sums_by_peer(kept, arrived, time_rows, gains, peers):
    width = kept.shape[-1]
    freq_count = kept.size // (peers * width)
    time_count = time_rows.size // (peers * width)
    if freq_count % 8 or time_count % 8:
        rows = 2 * width
        total = kept.astype(f32).reshape(rows, width) + arrived[:rows].astype(f32)
        gains = jnp.concatenate([gains[:4].astype(bf16), arrived[rows : rows + 4]], axis=0)
        parts = [
            total.astype(bf16).reshape(peers, -1, width),
            time_rows.reshape(peers, -1, width),
            jnp.broadcast_to(gains[None], (peers,) + gains.shape),
        ]
        return jnp.concatenate(parts, axis=1), freq_count, time_count
    vmem = pl.BlockSpec(memory_space=pltpu.VMEM)
    sums = pl.pallas_call(
        sums_kernel,
        in_specs=[vmem] * 4,
        out_specs=vmem,
        out_shape=pltpu.HBM((peers, freq_count + time_count + 8, width), bf16),
        compiler_params=pltpu.CompilerParams(vmem_limit_bytes=VMEM_LIMIT),
        cost_estimate=pl.CostEstimate(
            flops=kept.size, bytes_accessed=6 * kept.size, transcendentals=0
        ),
        name="sums_by_peer",
    )(kept, arrived, time_rows, gains)
    return sums, freq_count, time_count


def group_size(devices, bins_dev):
    best = 1
    for size in range(1, devices + 1):
        if devices % size == 0 and bins_dev % (8 * size) == 0:
            best = size
    return best


def per_device(features, upstream, weights, gains):
    frames_dev, bins_dev, width = features.shape
    tm, freq = lax.axis_size("tm"), lax.axis_size("freq")
    total_frames = frames_dev * tm
    frames = frames_dev // freq
    group = group_size(tm, bins_dev)
    bins_time = bins_dev // group
    group_frames = group * frames_dev
    whole = group == tm
    sides = 0 if whole else -(-WINDOW // group_frames)
    groups = (
        None
        if whole
        else [list(range(g * group, (g + 1) * group)) for g in range(tm // group)]
    )

    def over_tm(blocks):
        return lax.all_to_all(blocks, "tm", 0, 0, tiled=True, axis_index_groups=groups)

    def over_all(blocks):
        if whole:
            flat = blocks.reshape((tm * freq,) + blocks.shape[2:])
            return lax.all_to_all(flat, ("tm", "freq"), 0, 0, tiled=True).reshape(blocks.shape)
        return over_tm(lax.all_to_all(blocks, "freq", 1, 1, tiled=True))

    def with_sides(rows):
        parts = [rows]
        for away in range(1, sides + 1):
            shift = away * group
            before = lax.ppermute(rows, "tm", [(i, i + shift) for i in range(tm - shift)])
            after = lax.ppermute(rows, "tm", [(i + shift, i) for i in range(tm - shift)])
            parts = [before] + parts + [after]
        return jnp.concatenate(parts, axis=0) if sides else rows

    core = lax.axis_index("tm") % 2
    place = jnp.stack([lax.axis_index("freq"), core]).astype(jnp.int32)
    by_target = features.reshape(freq, frames, bins_dev, width)

    def along_freq(block, steps):
        return lax.ppermute(block, "freq", [(i, (i + steps) % freq) for i in range(freq)])

    picked = pick_others(by_target)
    others = jnp.stack(
        [
            along_freq(picked[j - 1], j) for j in range(1, freq)
        ]
    )
    up_blocks = jnp.swapaxes(upstream.reshape(frames_dev, group, bins_time, width), 0, 1)
    up_rows = over_tm(up_blocks).reshape(-1, width)
    freq_w = weights[:4]
    q, k, v, o, probs, hidden_blocks = freq_forward(place, by_target, others, freq_w, gains, group)
    time_w, hidden_blocks = lax.optimization_barrier((weights, hidden_blocks))
    time_w = time_w[4:]
    hidden_rows = over_all(hidden_blocks).reshape(-1, width)
    own_rows = hidden_rows.shape[0]
    position = lax.axis_index("tm") // group
    first = ((position - sides) * group_frames).astype(jnp.int32).reshape(1)
    grad_rows, time_kept, time_sent, time_dg = time_attention(
        place,
        first,
        with_sides(hidden_rows),
        with_sides(up_rows),
        time_w,
        gains,
        bins_time,
        sides * own_rows,
        own_rows,
        total_frames,
    )
    grad_hidden = over_all(grad_rows.reshape(hidden_blocks.shape))

    pairs = [(i, i ^ 1) for i in range(tm)]
    same = [
        [t * freq + f for t in range(c, tm, 2) for f in range(freq)] for c in range(2)
    ]
    peers = len(same[0])

    rows = 2 * width
    sets = 2 * freq
    halved = tm % 4 == 0 and freq & (freq - 1) == 0 and rows % (8 * sets * peers) == 0
    steps = [("tm", 1)] + [("freq", k) for k in reversed(range(freq.bit_length() - 1))]
    if not halved:
        sets, steps = 1, []

    def scattered(partial):
        partial = partial.reshape((2,) * len(steps) + (-1, width))
        for axis, k in steps:
            mine = (lax.axis_index(axis) >> k) & 1
            sent = lax.dynamic_index_in_dim(partial, 1 - mine, 0, False)
            kept = lax.dynamic_index_in_dim(partial, mine, 0, False)
            devices = range(lax.axis_size(axis))
            came = lax.ppermute(sent, axis, [(d, d ^ (1 << k)) for d in devices])
            partial = (kept.astype(f32) + came.astype(f32)).astype(bf16)
        return partial

    def over_same(blocks):
        return lax.all_to_all(
            blocks, ("tm", "freq"), 0, 0, tiled=True, axis_index_groups=same
        )

    time_arrived = lax.ppermute(time_sent, "tm", pairs)
    time_rows = scattered((time_kept.astype(f32) + time_arrived.astype(f32)).astype(bf16))
    grad_own, grad_others, freq_kept, freq_sent, own_gains = freq_backward(
        place, by_target, others, q, k, v, o, probs, grad_hidden, freq_w, gains, time_dg
    )
    freq_arrived = lax.ppermute(freq_sent, "tm", pairs)
    sums, freq_count, time_count = sums_by_peer(
        freq_kept, freq_arrived, time_rows, own_gains, peers
    )
    arrived = over_same(sums)
    returned = [grad_own] + [along_freq(grad_others[j - 1], -j) for j in range(1, freq)]
    grad_input = place_frames(place, returned).reshape(features.shape)
    grad_input, arrived = lax.optimization_barrier((grad_input, arrived))

    inv_root = (total_frames * bins_dev * freq) ** (-0.5)
    summed = jnp.sum(arrived.astype(f32), axis=0) * inv_root
    gain_sum = summed[freq_count + time_count :]
    time_arrived = arrived[:, freq_count : freq_count + time_count].astype(f32)
    time_sum = jnp.sum(time_arrived.reshape(-1, sets, time_count, width), axis=0) * inv_root
    block = jnp.concatenate([summed[:freq_count], time_sum.reshape(-1, width)], axis=0)
    block, gain_sum = lax.optimization_barrier((block.astype(bf16), gain_sum))
    gathered = over_same(jnp.broadcast_to(block[None], (peers,) + block.shape))
    gathered, gain_sum = lax.optimization_barrier((gathered, gain_sum))
    gain_grads = jnp.sum(gain_sum.reshape(4, 2, width), axis=0)
    theirs = lax.ppermute(gathered, "tm", pairs)
    first_core = core == 0
    halves = jnp.stack(
        [jnp.where(first_core, gathered, theirs), jnp.where(first_core, theirs, gathered)]
    )
    freq_grads = halves[:, :, :freq_count].reshape(4, width, width)
    time_grads = halves[:, :, freq_count:].reshape(2, peers, sets, time_count, width)
    time_grads = jnp.swapaxes(time_grads, 1, 2).reshape(4, width, width)
    weight_grads = jnp.concatenate([freq_grads, time_grads], axis=0).astype(f32)
    return (grad_input, weight_grads, gain_grads)


def solution(mesh):
    return jax.shard_map(
        per_device,
        mesh=mesh,
        in_specs=(P("tm", "freq", None), P("tm", "freq", None), P(), P()),
        out_specs=(P("tm", "freq", None), P(), P()),
        check_vma=False,
    )
```

```python
import functools

import jax
import jax.numpy as jnp
from jax import lax
from jax.experimental import pallas as pl
from jax.experimental.pallas import tpu as pltpu
from jax.sharding import PartitionSpec as P

HEADS = 4
WINDOW = 128

epsilon = 1e-06
masked_score = -1e30

f32 = jnp.float32
bf16 = jnp.bfloat16
LANES = 128
GAIN_ROWS = 16
MIB = 1024 * 1024
VMEM_LIMIT = 24 * MIB
FORWARD_WEIGHT = 40
PLACE_FLOPS = 10_000_000_000

CONTRACT_LAST = (((1,), (1,)), ((), ()))
CONTRACT_FIRST = (((0,), (0,)), ((), ()))


def dot(left, right):
    return jnp.dot(left, right, preferred_element_type=f32)


def dot_nt(left, right):
    return lax.dot_general(left, right, CONTRACT_LAST, preferred_element_type=f32)


def dot_tn(left, right):
    return lax.dot_general(left, right, CONTRACT_FIRST, preferred_element_type=f32)


def put(ref, rows, value):
    for c in range(ref.shape[0]):
        ref[c, rows, :] = value[:, c * LANES : (c + 1) * LANES]


def get(ref, rows):
    return jnp.concatenate([ref[c, rows, :] for c in range(ref.shape[0])], axis=1)


def norm_parts(widened):
    inverse = lax.rsqrt(jnp.mean(widened * widened, axis=-1, keepdims=True) + epsilon)
    return inverse, widened * inverse


def norm_backward(incoming, inverse, unit_rows, gain):
    scaled = incoming * gain
    return inverse * (scaled - unit_rows * jnp.mean(scaled * unit_rows, axis=-1, keepdims=True))


def spread(rows, factor):
    width = rows.shape[-1]
    owner = lax.broadcasted_iota(jnp.int32, (1, width), 1) // (width // HEADS)
    return jnp.concatenate(
        [rows * jnp.where(owner == h, factor, 0.0).astype(rows.dtype) for h in range(HEADS)], axis=0
    )


def own_channels(stacked, rows):
    width = stacked.shape[-1]
    owner = lax.broadcasted_iota(jnp.int32, (1, width), 1) // (width // HEADS)
    result = stacked[:rows]
    for h in range(1, HEADS):
        result = jnp.where(owner == h, stacked[h * rows : (h + 1) * rows], result)
    return result


def head_probs(scores, allowed):
    rows = scores.shape[0] // HEADS
    probs = []
    for h in range(HEADS):
        s = scores[h * rows : (h + 1) * rows]
        if allowed is not None:
            s = jnp.where(allowed, s, masked_score)
        e = jnp.exp(s - jnp.max(s, axis=-1, keepdims=True))
        probs.append(e * (1.0 / jnp.sum(e, axis=-1, keepdims=True)))
    return probs


def head_grads(probs, grad_probs, scale):
    rows = grad_probs.shape[0] // HEADS
    grad_scores = []
    for h in range(HEADS):
        gp = grad_probs[h * rows : (h + 1) * rows]
        row_dot = jnp.sum(gp * probs[h], axis=-1, keepdims=True)
        grad_scores.append((probs[h] * (gp - row_dot) * scale).astype(bf16))
    return jnp.concatenate(grad_scores, axis=0)


def stacked_low(probs):
    return jnp.concatenate([p.astype(bf16) for p in probs], axis=0)


def slot_of(position, back, freq):
    return lax.rem(position - back + freq, freq)


def pick_kernel(x_hbm, out_ref, sems):
    freq = x_hbm.shape[0]
    place = lax.axis_index("freq")
    copies = [
        pltpu.make_async_copy(x_hbm.at[lax.rem(place + j, freq)], out_ref.at[j - 1], sems.at[j - 1])
        for j in range(1, freq)
    ]
    for copy in copies:
        copy.start()
    for copy in copies:
        copy.wait()


def pick_others(features):
    freq = features.shape[0]
    return pl.pallas_call(
        pick_kernel,
        in_specs=[pl.BlockSpec(memory_space=pltpu.HBM)],
        out_specs=pl.BlockSpec(memory_space=pltpu.VMEM),
        out_shape=pltpu.VMEM((freq - 1,) + features.shape[1:], bf16),
        scratch_shapes=[pltpu.SemaphoreType.DMA((freq - 1,))],
        name="pick_others",
    )(far(features))


def freq_forward_kernel(
    place_ref, x_hbm, others_ref, w_ref, gain_ref,
    q_hbm, k_hbm, v_hbm, o_hbm, p_hbm, h_hbm,
    own_ref, q_ref, k_ref, v_ref, o_ref, p_ref, hold, h_low, load_sem, sems
):
    frames, bins_dev, width = own_ref.shape
    freq = others_ref.shape[0] + 1
    bins_time = hold.shape[2] // frames
    scale = (width // HEADS) ** (-0.5)
    stores = []

    def store(source, target):
        stores.append(pltpu.make_async_copy(source, target, sems.at[len(stores)]))
        stores[-1].start()

    load = pltpu.make_async_copy(x_hbm.at[place_ref[0]], own_ref, load_sem)
    load.start()
    load.wait()
    first = []
    for f in range(frames):
        _, unit = norm_parts(joined(own_ref.at[f], others_ref.at[:, f]))
        n = (unit * gain_ref[0:1, :]).astype(bf16)
        q = dot(n, w_ref[0]).astype(bf16)
        k = dot(n, w_ref[1]).astype(bf16)
        v = dot(n, w_ref[2]).astype(bf16)
        q_ref[f] = q
        k_ref[f] = k
        v_ref[f] = v
        first.append((v, dot_nt(spread(q, scale), k)))
    store(q_ref, q_hbm)
    store(k_ref, k_hbm)
    store(v_ref, v_hbm)
    second = []
    for f, (v, scores) in enumerate(first):
        low = stacked_low(head_probs(scores, None))
        p_ref[f] = low.reshape(p_ref.shape[1:])
        store(p_ref.at[f], p_hbm.at[f])
        second.append(own_channels(dot(low, v), v.shape[0]).astype(bf16))
    for f, o in enumerate(second):
        o_ref[f] = o
        hidden = joined(own_ref.at[f], others_ref.at[:, f]) + dot(o, w_ref[3])
        rows = pl.ds(f * bins_time, bins_time)
        for j in range(freq):
            part = hidden[j * bins_dev : (j + 1) * bins_dev].reshape(-1, bins_time, width)
            hold[:, slot_of(place_ref[0], j, freq), rows, :] = part
    store(o_ref, o_hbm)
    h_low[...] = hold[...].astype(bf16)
    store(h_low, h_hbm)
    for copy in stores:
        copy.wait()


def joined(own_ref, others_ref):
    width = own_ref.shape[-1]
    return jnp.concatenate(
        [own_ref[...].reshape(-1, width), others_ref[...].reshape(-1, width)], axis=0
    ).astype(f32)


def near(array):
    return pltpu.with_memory_space_constraint(array, pltpu.VMEM)


def far(array):
    return pltpu.with_memory_space_constraint(array, pltpu.HBM)


def freq_forward(place, features, others, weights, gains, group):
    freq, frames, bins_dev, width = features.shape
    bins = freq * bins_dev
    whole = (group, freq, frames * (bins_dev // group), width)
    probs = (frames, HEADS, bins, bins)
    rows = (frames, bins, width)
    flops = frames * 2 * bins * (4 * width * width + 2 * HEADS * bins * width)
    vmem = pl.BlockSpec(memory_space=pltpu.VMEM)
    hbm = pl.BlockSpec(memory_space=pltpu.HBM)
    return pl.pallas_call(
        freq_forward_kernel,
        in_specs=[pl.BlockSpec(memory_space=pltpu.SMEM), hbm, vmem, vmem, vmem],
        out_specs=[hbm] * 6,
        out_shape=[pltpu.HBM(rows, bf16)] * 4 + [pltpu.HBM(probs, bf16), pltpu.HBM(whole, bf16)],
        scratch_shapes=[pltpu.VMEM((frames, bins_dev, width), bf16)]
        + [pltpu.VMEM(rows, bf16)] * 4
        + [
            pltpu.VMEM(probs, bf16),
            pltpu.VMEM(whole, f32),
            pltpu.VMEM(whole, bf16),
            pltpu.SemaphoreType.DMA,
            pltpu.SemaphoreType.DMA((frames + 5,)),
        ],
        compiler_params=pltpu.CompilerParams(vmem_limit_bytes=VMEM_LIMIT),
        cost_estimate=pl.CostEstimate(
            flops=flops * FORWARD_WEIGHT,
            bytes_accessed=2 * 1024 * 1024,
            transcendentals=frames * HEADS * bins * bins,
        ),
        name="freq_forward",
    )(place, far(features), near(others), near(weights), gains)


def freq_backward_kernel(
    place_ref, x_hbm, others_hbm, q_hbm, k_hbm, v_hbm, o_hbm, p_hbm, gh_ref, w_ref, gain_ref,
    time_dg_ref, gown_ref, gothers_ref, kept_ref, sent_ref, gains_ref,
    own_ref, others_ref, q_ref, k_ref, v_ref, o_ref, p_ref, hold, total, sems
):
    frames, bins_dev, width = own_ref.shape
    freq = others_ref.shape[0] + 1
    bins_time = bins_dev // hold.shape[0]
    scale = (width // HEADS) ** (-0.5)
    gain = gain_ref[0:1, :]
    loads = {}
    for name, source, target in (
        ("v", v_hbm, v_ref),
        ("p", p_hbm, p_ref),
        ("k", k_hbm, k_ref),
        ("q", q_hbm, q_ref),
        ("own", x_hbm.at[place_ref[0]], own_ref),
        ("others", others_hbm, others_ref),
        ("o", o_hbm, o_ref),
    ):
        loads[name] = pltpu.make_async_copy(source, target, sems.at[len(loads)])
        loads[name].start()
    hold[...] = gh_ref[...].astype(f32)
    first = []
    for f in range(frames):
        grad_hidden = grad_hidden_rows(place_ref, hold, f, freq, bins_time)
        low = grad_hidden.astype(bf16)
        out_spread = spread(dot_nt(low, w_ref[3]).astype(bf16), 1.0)
        first.append((grad_hidden, low, out_spread))
    loads["v"].wait()
    first = [parts + (dot_nt(parts[2], v_ref[f]),) for f, parts in enumerate(first)]
    loads["p"].wait()
    second = []
    for f, (_, _, out_spread, grad_probs) in enumerate(first):
        probs = [p_ref[f, h].astype(f32) for h in range(HEADS)]
        g_v = dot_tn(p_ref[f].reshape(-1, p_ref.shape[3]), out_spread).astype(bf16)
        second.append((g_v, head_grads(probs, grad_probs, scale)))
    for name in ("k", "q", "own", "others", "o"):
        loads[name].wait()
    third = []
    for f, (g_v, grad_scores) in enumerate(second):
        g_q = own_channels(dot(grad_scores, k_ref[f]), freq * bins_dev).astype(bf16)
        g_k = dot_tn(grad_scores, spread(q_ref[f], 1.0)).astype(bf16)
        third.append((g_q, g_k, g_v))
    gains_ref[...] = jnp.zeros_like(gains_ref)
    for f, ((grad_hidden, low, _, _), (g_q, g_k, g_v)) in enumerate(zip(first, third)):
        inverse, unit = norm_parts(joined(own_ref.at[f], others_ref.at[:, f]))
        n = (unit * gain).astype(bf16)
        parts = (dot_tn(n, g_q), dot_tn(n, g_k), dot_tn(n, g_v), dot_tn(o_ref[f], low))
        for m, part in enumerate(parts):
            total[m] = part if f == 0 else total[m] + part
        g_n = dot_nt(g_q, w_ref[0]) + dot_nt(g_k, w_ref[1]) + dot_nt(g_v, w_ref[2])
        grad_x = (grad_hidden + norm_backward(g_n, inverse, unit, gain)).astype(bf16)
        gown_ref[f] = grad_x[:bins_dev]
        gothers_ref[:, f] = grad_x[bins_dev:].reshape(freq - 1, bins_dev, width)
        gains_ref[0:1] += jnp.sum(g_n * unit, axis=0, keepdims=True)
    gains_ref[1:2] = time_dg_ref[...]
    gains = gains_ref[0:2]
    high = gains.astype(bf16).astype(f32)
    gains_ref[0:2] = high
    gains_ref[2:4] = gains - high
    matrices = kept_ref.shape[0]
    kept_ref[...] = total[pl.ds(place_ref[1] * matrices, matrices)].astype(bf16)
    sent = total[pl.ds((1 - place_ref[1]) * matrices, matrices)].reshape(-1, width)
    sent_ref[...] = jnp.concatenate([sent, gains_ref[...]], axis=0).astype(bf16)


def put_halves(core, total, kept_ref, sent_ref):
    half = kept_ref.shape[0]
    kept_ref[...] = total[pl.ds(core * half, half)].astype(bf16)
    sent_ref[...] = total[pl.ds((1 - core) * half, half)].astype(bf16)


def grad_hidden_rows(place_ref, hold, frame, freq, bins_time):
    width = hold.shape[-1]
    rows = pl.ds(frame * bins_time, bins_time)
    return jnp.concatenate(
        [hold[:, slot_of(place_ref[0], f, freq), rows, :].reshape(-1, width) for f in range(freq)],
        axis=0,
    )


def freq_backward(
    place, features, others, q, k, v, o, probs, grad_hidden, weights, gains, time_dg
):
    freq, frames, bins_dev, width = features.shape
    bins = freq * bins_dev
    flops = frames * 2 * bins * (8 * width * width + 4 * HEADS * bins * width)
    half = (2, width, width)
    vmem = pl.BlockSpec(memory_space=pltpu.VMEM)
    hbm = pl.BlockSpec(memory_space=pltpu.HBM)
    rows = pltpu.VMEM((frames, bins, width), bf16)
    return pl.pallas_call(
        freq_backward_kernel,
        in_specs=[pl.BlockSpec(memory_space=pltpu.SMEM)] + [hbm] * 7 + [vmem] * 4,
        out_specs=[vmem] * 5,
        out_shape=[
            pltpu.VMEM((frames, bins_dev, width), bf16),
            pltpu.VMEM(others.shape, bf16),
            pltpu.VMEM(half, bf16),
            pltpu.VMEM((2 * width + GAIN_ROWS, width), bf16),
            pltpu.VMEM((GAIN_ROWS, width), f32),
        ],
        scratch_shapes=[
            pltpu.VMEM((frames, bins_dev, width), bf16),
            pltpu.VMEM(others.shape, bf16),
            rows,
            rows,
            rows,
            rows,
            pltpu.VMEM(probs.shape, bf16),
            pltpu.VMEM(grad_hidden.shape, f32),
            pltpu.VMEM((4, width, width), f32),
            pltpu.SemaphoreType.DMA((7,)),
        ],
        compiler_params=pltpu.CompilerParams(vmem_limit_bytes=VMEM_LIMIT),
        cost_estimate=pl.CostEstimate(
            flops=flops, bytes_accessed=8 * 1024 * 1024, transcendentals=0
        ),
        name="freq_backward",
    )(
        place, *map(far, (features, others, q, k, v, o, probs)), near(grad_hidden),
        near(weights), gains, time_dg,
    )


def time_kernel(
    bins, own_start, total_frames, place_ref, first_ref, h_ref, up_ref, w_ref, gain_ref,
    gh_hbm, kept_ref, sent_ref, dg_ref,
    gh_ref, total, q_s, k_s, v_s, go_s, o_s, gq_s, gk_s, gv_s, sems
):
    span_rows, width = h_ref.shape
    span = span_rows // bins
    own_rows = gh_ref.shape[0]
    own = own_rows // bins
    scale = (width // HEADS) ** (-0.5)
    gain = gain_ref[1:2, :]
    chunk = own_rows
    while chunk > 256 and chunk % 32 == 0:
        chunk //= 2
    chunks = span_rows // chunk

    for i in range(chunks):
        rows = pl.ds(i * chunk, chunk)
        _, unit = norm_parts(h_ref[rows, :].astype(f32))
        n = (unit * gain).astype(bf16)
        put(q_s, rows, dot(n, w_ref[0]))
        put(k_s, rows, dot(n, w_ref[1]))
        put(v_s, rows, dot(n, w_ref[2]))
    for i in range(chunks):
        rows = pl.ds(i * chunk, chunk)
        put(go_s, rows, dot_nt(up_ref[rows, :], w_ref[3]))

    query = lax.broadcasted_iota(jnp.int32, (span, span), 0)
    key = lax.broadcasted_iota(jnp.int32, (span, span), 1)
    distance = key - query
    allowed = (distance >= -(WINDOW // 2)) & (distance < WINDOW // 2)
    if own != span:
        frame = first_ref[0] + key
        allowed = allowed & (frame >= 0) & (frame < total_frames)

    together = max(n for n in (1, 2) if bins % n == 0 and (n == 1 or n * span <= 512))

    def products(start):
        result = []
        for b in range(together):
            rows = pl.ds(start + b, span, stride=bins)
            q, k, v, grad_out = (get(ref, rows).astype(bf16) for ref in (q_s, k_s, v_s, go_s))
            out_spread = spread(grad_out, 1.0)
            scores, grad_probs = dot_nt(spread(q, scale), k), dot_nt(out_spread, v)
            result.append((rows, q, k, v, out_spread, scores, grad_probs))
        return result

    def cotangents(result):
        second = []
        for *_, scores, grad_probs in result:
            probs = head_probs(scores, allowed)
            second.append((stacked_low(probs), head_grads(probs, grad_probs, scale)))
        return second

    def mix(result, second):
        for (rows, q, k, v, out_spread, *_), (low, grad_scores) in zip(result, second):
            put(o_s, rows, own_channels(dot(low, v), span))
            put(gq_s, rows, own_channels(dot(grad_scores, k), span))
            put(gk_s, rows, dot_tn(grad_scores, spread(q, 1.0)))
            put(gv_s, rows, dot_tn(low, out_spread))

    starts = list(range(0, bins, together))
    ahead = products(starts[0])
    for i in range(len(starts)):
        first, ahead = ahead, None
        second = cotangents(first)
        more = i + 1 < len(starts)
        if more and together > 1:
            ahead = products(starts[i + 1])
        mix(first, second)
        if more and together == 1:
            ahead = products(starts[i + 1])

    dg_ref[...] = jnp.zeros_like(dg_ref)
    stores = []
    for i in range(own_rows // chunk):
        mine = pl.ds(i * chunk, chunk)
        rows = pl.ds(own_start + i * chunk, chunk)
        g_q = get(gq_s, rows).astype(bf16)
        g_k = get(gk_s, rows).astype(bf16)
        g_v = get(gv_s, rows).astype(bf16)
        g_n = dot_nt(g_q, w_ref[0]) + dot_nt(g_k, w_ref[1]) + dot_nt(g_v, w_ref[2])
        inverse, unit = norm_parts(h_ref[rows, :].astype(f32))
        n = (unit * gain).astype(bf16)
        up = up_ref[rows, :]
        grad_hidden = up.astype(f32) + norm_backward(g_n, inverse, unit, gain)
        gh_ref[mine, :] = grad_hidden.astype(bf16)
        stores.append(pltpu.make_async_copy(gh_ref.at[mine], gh_hbm.at[mine], sems.at[3 + i]))
        stores[-1].start()
        dg_ref[...] += jnp.sum(g_n * unit, axis=0, keepdims=True)
        parts = (dot_tn(n, g_q), dot_tn(n, g_k), dot_tn(n, g_v), dot_tn(get(o_s, rows).astype(bf16), up))
        for m, part in enumerate(parts):
            total[m] = part if i == 0 else total[m] + part
    put_halves(place_ref[1], total, kept_ref, sent_ref)
    for store in stores:
        store.wait()


def time_attention(place, first, hidden, upstream, weights, gains, bins, own_start, own_rows, total):
    span_rows, width = hidden.shape
    vmem = pl.BlockSpec(memory_space=pltpu.VMEM)
    hbm = pl.BlockSpec(memory_space=pltpu.HBM)
    smem = pl.BlockSpec(memory_space=pltpu.SMEM)
    span = span_rows // bins
    flops = 2 * span_rows * (11 * width * width + 6 * HEADS * span * width)
    return pl.pallas_call(
        functools.partial(time_kernel, bins, own_start, total),
        in_specs=[smem, smem, vmem, vmem, vmem, vmem],
        out_specs=[hbm] + [vmem] * 3,
        out_shape=[pltpu.HBM((own_rows, width), bf16)]
        + [pltpu.VMEM((2, width, width), bf16)] * 2
        + [jax.ShapeDtypeStruct((1, width), f32)],
        scratch_shapes=[
            pltpu.VMEM((own_rows, width), bf16),
            pltpu.VMEM((4, width, width), f32),
        ]
        + [pltpu.VMEM((width // LANES, span_rows, LANES), f32)] * 8
        + [pltpu.SemaphoreType.DMA((16,))],
        compiler_params=pltpu.CompilerParams(vmem_limit_bytes=VMEM_LIMIT),
        cost_estimate=pl.CostEstimate(
            flops=flops,
            bytes_accessed=4 * 1024 * 1024,
            transcendentals=bins * HEADS * span * span,
        ),
        name="time_attention",
    )(place, first, near(hidden), near(upstream), near(weights), gains)


def place_kernel(place_ref, *refs):
    *parts, out_hbm, sems = refs
    freq = len(parts)
    copies = [
        pltpu.make_async_copy(part, out_hbm.at[lax.rem(place_ref[0] + j, freq)], sems.at[j])
        for j, part in enumerate(parts)
    ]
    for copy in copies:
        copy.start()
    for copy in copies:
        copy.wait()


def place_frames(place, parts):
    vmem = pl.BlockSpec(memory_space=pltpu.VMEM)
    return pl.pallas_call(
        place_kernel,
        in_specs=[pl.BlockSpec(memory_space=pltpu.SMEM)] + [vmem] * len(parts),
        out_specs=pl.BlockSpec(memory_space=pltpu.HBM),
        out_shape=pltpu.HBM((len(parts),) + parts[0].shape, bf16),
        scratch_shapes=[pltpu.SemaphoreType.DMA((len(parts),))],
        compiler_params=pltpu.CompilerParams(vmem_limit_bytes=VMEM_LIMIT),
        cost_estimate=pl.CostEstimate(
            flops=PLACE_FLOPS, bytes_accessed=4 * parts[0].size, transcendentals=0
        ),
        name="place_frames",
    )(place, *map(near, parts))


def sums_kernel(kept_ref, arrived_ref, time_ref, gains_ref, out_ref):
    peers, _, width = out_ref.shape
    arrived = arrived_ref[...].astype(f32)
    rows = arrived.shape[0] - gains_ref.shape[0]
    total = kept_ref[...].astype(f32).reshape(rows, width) + arrived[:rows]
    gains = jnp.concatenate([gains_ref[0:4], arrived[rows : rows + 4]], axis=0)
    parts = [
        total.reshape(peers, -1, width),
        time_ref[...].astype(f32).reshape(peers, -1, width),
        jnp.broadcast_to(gains[None], (peers,) + gains.shape),
    ]
    out_ref[...] = jnp.concatenate(parts, axis=1).astype(bf16)


def sums_by_peer(kept, arrived, time_rows, gains, peers):
    width = kept.shape[-1]
    freq_count = kept.size // (peers * width)
    time_count = time_rows.size // (peers * width)
    if freq_count % 8 or time_count % 8:
        rows = 2 * width
        total = kept.astype(f32).reshape(rows, width) + arrived[:rows].astype(f32)
        gains = jnp.concatenate([gains[:4].astype(bf16), arrived[rows : rows + 4]], axis=0)
        parts = [
            total.astype(bf16).reshape(peers, -1, width),
            time_rows.reshape(peers, -1, width),
            jnp.broadcast_to(gains[None], (peers,) + gains.shape),
        ]
        return jnp.concatenate(parts, axis=1), freq_count, time_count
    vmem = pl.BlockSpec(memory_space=pltpu.VMEM)
    sums = pl.pallas_call(
        sums_kernel,
        in_specs=[vmem] * 4,
        out_specs=vmem,
        out_shape=pltpu.HBM((peers, freq_count + time_count + 8, width), bf16),
        compiler_params=pltpu.CompilerParams(vmem_limit_bytes=VMEM_LIMIT),
        cost_estimate=pl.CostEstimate(
            flops=kept.size, bytes_accessed=6 * kept.size, transcendentals=0
        ),
        name="sums_by_peer",
    )(kept, arrived, time_rows, gains)
    return sums, freq_count, time_count


def group_size(devices, bins_dev):
    best = 1
    for size in range(1, devices + 1):
        if devices % size == 0 and bins_dev % (8 * size) == 0:
            best = size
    return best


def per_device(features, upstream, weights, gains):
    frames_dev, bins_dev, width = features.shape
    tm, freq = lax.axis_size("tm"), lax.axis_size("freq")
    total_frames = frames_dev * tm
    frames = frames_dev // freq
    group = group_size(tm, bins_dev)
    bins_time = bins_dev // group
    group_frames = group * frames_dev
    whole = group == tm
    sides = 0 if whole else -(-WINDOW // group_frames)
    groups = (
        None
        if whole
        else [list(range(g * group, (g + 1) * group)) for g in range(tm // group)]
    )

    def over_tm(blocks):
        return lax.all_to_all(blocks, "tm", 0, 0, tiled=True, axis_index_groups=groups)

    def over_all(blocks):
        if whole:
            flat = blocks.reshape((tm * freq,) + blocks.shape[2:])
            return lax.all_to_all(flat, ("tm", "freq"), 0, 0, tiled=True).reshape(blocks.shape)
        return over_tm(lax.all_to_all(blocks, "freq", 1, 1, tiled=True))

    def with_sides(rows):
        parts = [rows]
        for away in range(1, sides + 1):
            shift = away * group
            before = lax.ppermute(rows, "tm", [(i, i + shift) for i in range(tm - shift)])
            after = lax.ppermute(rows, "tm", [(i + shift, i) for i in range(tm - shift)])
            parts = [before] + parts + [after]
        return jnp.concatenate(parts, axis=0) if sides else rows

    core = lax.axis_index("tm") % 2
    place = jnp.stack([lax.axis_index("freq"), core]).astype(jnp.int32)
    by_target = features.reshape(freq, frames, bins_dev, width)

    def along_freq(block, steps):
        return lax.ppermute(block, "freq", [(i, (i + steps) % freq) for i in range(freq)])

    picked = pick_others(by_target)
    others = jnp.stack(
        [
            along_freq(picked[j - 1], j) for j in range(1, freq)
        ]
    )
    up_blocks = jnp.swapaxes(upstream.reshape(frames_dev, group, bins_time, width), 0, 1)
    up_rows = over_tm(up_blocks).reshape(-1, width)
    freq_w = weights[:4]
    q, k, v, o, probs, hidden_blocks = freq_forward(place, by_target, others, freq_w, gains, group)
    time_w, hidden_blocks = lax.optimization_barrier((weights, hidden_blocks))
    time_w = time_w[4:]
    hidden_rows = over_all(hidden_blocks).reshape(-1, width)
    own_rows = hidden_rows.shape[0]
    position = lax.axis_index("tm") // group
    first = ((position - sides) * group_frames).astype(jnp.int32).reshape(1)
    grad_rows, time_kept, time_sent, time_dg = time_attention(
        place,
        first,
        with_sides(hidden_rows),
        with_sides(up_rows),
        time_w,
        gains,
        bins_time,
        sides * own_rows,
        own_rows,
        total_frames,
    )
    grad_hidden = over_all(grad_rows.reshape(hidden_blocks.shape))

    pairs = [(i, i ^ 1) for i in range(tm)]
    same = [
        [t * freq + f for t in range(c, tm, 2) for f in range(freq)] for c in range(2)
    ]
    peers = len(same[0])

    rows = 2 * width
    sets = 2 * freq
    halved = tm % 4 == 0 and freq & (freq - 1) == 0 and rows % (8 * sets * peers) == 0
    steps = [("tm", 1)] + [("freq", k) for k in reversed(range(freq.bit_length() - 1))]
    if not halved:
        sets, steps = 1, []

    def scattered(partial):
        partial = partial.reshape((2,) * len(steps) + (-1, width))
        for axis, k in steps:
            mine = (lax.axis_index(axis) >> k) & 1
            sent = lax.dynamic_index_in_dim(partial, 1 - mine, 0, False)
            kept = lax.dynamic_index_in_dim(partial, mine, 0, False)
            devices = range(lax.axis_size(axis))
            came = lax.ppermute(sent, axis, [(d, d ^ (1 << k)) for d in devices])
            partial = (kept.astype(f32) + came.astype(f32)).astype(bf16)
        return partial

    def over_same(blocks):
        return lax.all_to_all(
            blocks, ("tm", "freq"), 0, 0, tiled=True, axis_index_groups=same
        )

    time_arrived = lax.ppermute(time_sent, "tm", pairs)
    time_rows = scattered((time_kept.astype(f32) + time_arrived.astype(f32)).astype(bf16))
    grad_own, grad_others, freq_kept, freq_sent, own_gains = freq_backward(
        place, by_target, others, q, k, v, o, probs, grad_hidden, freq_w, gains, time_dg
    )
    freq_arrived = lax.ppermute(freq_sent, "tm", pairs)
    sums, freq_count, time_count = sums_by_peer(
        freq_kept, freq_arrived, time_rows, own_gains, peers
    )
    arrived = over_same(sums)
    returned = [grad_own] + [along_freq(grad_others[j - 1], -j) for j in range(1, freq)]
    grad_input = place_frames(place, returned).reshape(features.shape)
    grad_input, arrived = lax.optimization_barrier((grad_input, arrived))

    inv_root = (total_frames * bins_dev * freq) ** (-0.5)
    summed = jnp.sum(arrived.astype(f32), axis=0) * inv_root
    gain_sum = summed[freq_count + time_count :]
    time_arrived = arrived[:, freq_count : freq_count + time_count].astype(f32)
    time_sum = jnp.sum(time_arrived.reshape(-1, sets, time_count, width), axis=0) * inv_root
    block = jnp.concatenate([summed[:freq_count], time_sum.reshape(-1, width)], axis=0)
    block, gain_sum = lax.optimization_barrier((block.astype(bf16), gain_sum))
    gathered = over_same(jnp.broadcast_to(block[None], (peers,) + block.shape))
    gathered, gain_sum = lax.optimization_barrier((gathered, gain_sum))
    gain_grads = jnp.sum(gain_sum.reshape(4, 2, width), axis=0)
    theirs = lax.ppermute(gathered, "tm", pairs)
    first_core = core == 0
    halves = jnp.stack(
        [jnp.where(first_core, gathered, theirs), jnp.where(first_core, theirs, gathered)]
    )
    freq_grads = halves[:, :, :freq_count].reshape(4, width, width)
    time_grads = halves[:, :, freq_count:].reshape(2, peers, sets, time_count, width)
    time_grads = jnp.swapaxes(time_grads, 1, 2).reshape(4, width, width)
    weight_grads = jnp.concatenate([freq_grads, time_grads], axis=0).astype(f32)
    return (grad_input, weight_grads, gain_grads)


def solution(mesh):
    return jax.shard_map(
        per_device,
        mesh=mesh,
        in_specs=(P("tm", "freq", None), P("tm", "freq", None), P(), P()),
        out_specs=(P("tm", "freq", None), P(), P()),
        check_vma=False,
    )
```
